32 devices in a mesh: seq: 16 (over z, y, x), ffn: 2 (over core).
Axes of the slice: x: 2, y: 2, z: 4, core: 2. Of those that a mesh axis runs over, the one named last changes fastest.
Arguments:
- inputs: float32 [2, 36864, 512], P(None, ('seq', 'ffn')), may hold values from -6 to 6
- lengths: int32 [2, 32, 3], P(None, ('seq', 'ffn')), may hold values from 1 to 1024, 1088 in all within a row
- first_gain: float32 [512], replicated, may hold values from 0.25 to 1.75
- first_shift: float32 [512], replicated, may hold values from -3 to 3
- query_weight: float32 [512, 512], replicated, may hold values from -0.25 to 0.25
- key_weight: float32 [512, 512], replicated, may hold values from -0.25 to 0.25
- value_weight: float32 [512, 512], replicated, may hold values from -0.25 to 0.25
- output_weight: float32 [512, 512], replicated, may hold values from -1 to 1
- output_bias: float32 [512], replicated, may hold values from -3 to 3
- projection: float32 [8, 64, 256], replicated, may hold values from -6 to 6
- second_gain: float32 [512], replicated, may hold values from 0.25 to 1.75
- second_shift: float32 [512], replicated, may hold values from -3 to 3
- up_weight: float32 [512, 2048], P('seq', 'ffn'), may hold values from -0.25 to 0.25
- up_bias: float32 [2048], replicated, may hold values from -3 to 3
- down_weight: float32 [2048, 512], P('ffn', 'seq'), may hold values from -0.25 to 0.25
- down_bias: float32 [512], replicated, may hold values from -3 to 3
- cotangent: float32 [2, 36864, 512], P(None, ('seq', 'ffn')), may hold values from -6 to 6
Outputs:
- output: float32 [2, 36864, 512], P(None, ('seq', 'ffn'))
- input_grad: float32 [2, 36864, 512], P(None, ('seq', 'ffn'))
- first_gain_grad: float32 [512], replicated
- first_shift_grad: float32 [512], replicated
- query_grad: float32 [512, 512], replicated
- key_grad: float32 [512, 512], replicated
- value_grad: float32 [512, 512], replicated
- output_weight_grad: float32 [512, 512], replicated
- output_bias_grad: float32 [512], replicated
- second_gain_grad: float32 [512], replicated
- second_shift_grad: float32 [512], replicated
- up_weight_grad: float32 [512, 2048], P('seq', 'ffn')
- up_bias_grad: float32 [2048], replicated
- down_weight_grad: float32 [2048, 512], P('ffn', 'seq')
- down_bias_grad: float32 [512], replicated
The draws below stay inside these ranges and needn't reach their ends.
Inputs may be any that keep to these rules, and one draw needn't show every extreme that they name: Each row of 3 lengths sums to 1088, and its largest is exactly 1024.
All inputs are finite; a program needn't handle non-finite values.
Results may differ from the reference program's by a relative error of at most 0.035.
Values may be sent and summed in bfloat16 or wider, within the bound.
A program may use at most 448 MiB of HBM per device.

```python
import math
import jax
import jax.numpy as jnp
import numpy as np
from jax import lax

D = 512
HEADS = 8
HEAD_DIM = 64
FEATURES = 256
FF = 2048
LONG_DEV = 64
SHORT_DEV = 1088
SHORT_MOST = 1024
NSHORT = 3
MICRO = 2
SPAN = 32
LONG_LEN = 2048
ROWS_DEV = 1152
ROWS = 36864
N_SEQ = 16
N_FFN = 2


def raised(array, key, source, target, blocks, factor):
    def block_of(axis_at):
        return (jnp.arange(array.shape[axis_at]) // (array.shape[axis_at] // blocks)).reshape((-1,) + (1,) * (array.ndim - 1 - axis_at))

    near = jax.random.permutation(key, blocks)[block_of(target)]
    second = (block_of(target) + blocks // 2) % blocks
    return jnp.where((block_of(source) == near) | (block_of(source) == second), factor * array, array)


def levels(key, extent, cuts, least, largest):
    factor_of = 1.0
    for dim, blocks in cuts:
        draws = jax.random.uniform(jax.random.fold_in(jax.random.fold_in(key, 6), dim), (blocks,), jnp.float32, least / len(cuts), largest / len(cuts))
        factor_of = factor_of * jnp.repeat(jnp.exp(draws), extent[dim] // blocks).reshape((-1,) + (1,) * (len(extent) - 1 - dim))
    return factor_of


def length_profile(number_of, total, limit, slope):
    weights = [(1 << 20) // math.isqrt(rank ** slope) + 1 for rank in range(2, number_of + 1)]
    rest, holding = total - limit - (number_of - 1), [1] * (number_of - 1)
    while rest > 0:
        candidates = [i for i in range(number_of - 1) if holding[i] < limit]
        mass, left = sum([weights[i] for i in candidates]), rest
        for i in candidates:
            addition = min(limit - holding[i], max(1, left * weights[i] // mass), rest)
            holding[i] = holding[i] + addition
            rest = rest - addition
    return np.array([limit] + holding)


def uneven(own_key, count, total, most, slope):
    if count == 2:
        one = jax.random.randint(own_key, (), max(1, total - most), min(most, total - 1) + 1)
        return jnp.stack([one, total - one])
    tallies = jnp.asarray(length_profile(count, total, most, slope), jnp.int32)
    pairs = (count - 1) // 2
    source_of, taker = tallies[1:1 + 2 * pairs:2], tallies[2:2 + 2 * pairs:2]
    room = jnp.minimum(source_of - 1, most - taker)
    shifted = jax.random.randint(jax.random.fold_in(own_key, 1), (pairs,), 0, 1 << 20) % (room + 1)
    tallies = tallies.at[1:1 + 2 * pairs:2].set(source_of - shifted).at[2:2 + 2 * pairs:2].set(taker + shifted)
    return tallies[jax.random.permutation(jax.random.fold_in(own_key, 2), count)]


def bell_draw(rng, dims, scale, reach, split=(), kind=jnp.bfloat16):
    factor_of = levels(rng, dims, split, -0.22, 0.18) if split else 1.0
    array = jax.random.normal(rng, dims, jnp.float32) * scale * factor_of
    return jnp.minimum(jnp.maximum(array, -reach), reach).astype(kind)


def bell_draw_with(key, shape, scale, limit, pieces, heavy, kind=jnp.bfloat16):
    array = scale * jax.random.normal(key, shape, jnp.float32)
    if pieces:
        array = array * levels(key, shape, pieces, -0.22, 0.18)
    return jnp.clip(raised(array, jax.random.fold_in(key, 3), *heavy), -limit, limit).astype(kind)


def setup_inputs(seed: int = 0) -> dict:
    splits = jax.random.split(jax.random.key(seed), 18)
    inputs = bell_draw(splits[0], (MICRO, ROWS, D), 1.0, 6.0, ((1, 32),), jnp.float32)
    lengths = jax.vmap(lambda own: uneven(own, NSHORT, SHORT_DEV, SHORT_MOST, 1))(jax.random.split(splits[1], MICRO * (N_SEQ * N_FFN))).reshape((MICRO, N_SEQ * N_FFN, NSHORT)).astype(jnp.int32)
    first_gain = jnp.clip(1.0 + 0.15 * jax.random.normal(splits[2], (D,), jnp.float32), 0.25, 1.75)
    first_shift = bell_draw(splits[3], (D,), 0.5, 3.0, (), jnp.float32)
    query_weight = bell_draw(splits[4], (D, D), D ** -0.5, 0.25, (), jnp.float32)
    key_weight = bell_draw(splits[5], (D, D), D ** -0.5, 0.25, (), jnp.float32)
    value_weight = bell_draw(splits[6], (D, D), D ** -0.5, 0.25, (), jnp.float32)
    output_weight = bell_draw(splits[7], (D, D), (D // 16) ** -0.5, 1.0, (), jnp.float32)
    output_bias = bell_draw(splits[8], (D,), 0.5, 3.0, (), jnp.float32)
    projection = bell_draw(splits[9], (HEADS, HEAD_DIM, FEATURES), 1.0, 6.0, (), jnp.float32)
    second_gain = jnp.clip(1.0 + 0.15 * jax.random.normal(splits[10], (D,), jnp.float32), 0.25, 1.75)
    second_shift = bell_draw(splits[11], (D,), 0.5, 3.0, (), jnp.float32)
    up_weight = bell_draw(splits[12], (D, FF), D ** -0.5, 0.25, ((0, 16), (1, 2)), jnp.float32)
    up_bias = bell_draw(splits[13], (FF,), 0.5, 3.0, (), jnp.float32)
    down_weight = bell_draw(splits[14], (FF, D), (FF // 4) ** -0.5, 0.25, ((0, 2), (1, 16)), jnp.float32)
    down_bias = bell_draw(splits[15], (D,), 0.5, 3.0, (), jnp.float32)
    cotangent = bell_draw_with(splits[16], (MICRO, ROWS, D), 1.0, 6.0, ((1, 32),), (1, 2, 32, 2.75), jnp.float32)
    return dict(inputs=inputs, lengths=lengths, first_gain=first_gain, first_shift=first_shift, query_weight=query_weight, key_weight=key_weight, value_weight=value_weight, output_weight=output_weight, output_bias=output_bias, projection=projection, second_gain=second_gain, second_shift=second_shift, up_weight=up_weight, up_bias=up_bias, down_weight=down_weight, down_bias=down_bias, cotangent=cotangent)


PRECISE = lax.Precision.HIGHEST
EPSILON = 1e-05

@jax.custom_vjp
def low(v):
    return lax.optimization_barrier(v.astype(jnp.bfloat16)).astype(jnp.float32)

@jax.custom_vjp
def low_back(v):
    return v

def low_keep(v):
    return (low(v), None)

def low_pass(kept, grad):
    return (grad,)

def back_keep(v):
    return (v, None)

def back_low(kept, grad):
    return (low(grad),)
low.defvjp(low_keep, low_pass)
low_back.defvjp(back_keep, back_low)

def layer_norm(rows, gain, shift):
    mean = lax.optimization_barrier(jnp.mean(rows, axis=-1, keepdims=True))
    centred = rows - mean
    spread = lax.optimization_barrier(jnp.mean(centred * centred, axis=-1, keepdims=True))
    return centred * lax.rsqrt(spread + EPSILON) * gain + shift

def segment_table(lens):
    rows = jnp.arange(ROWS_DEV, dtype=jnp.int32)
    ends = jnp.cumsum(lens).astype(jnp.int32)
    inside = lax.optimization_barrier(jnp.sum((rows[:, None] - LONG_DEV >= ends[None, :]).astype(jnp.int32), axis=1))
    segment = jnp.where(rows < LONG_DEV, 0, 1 + inside)
    labels = jnp.arange(NSHORT + 1, dtype=jnp.int32)
    return (segment[None, :] == labels[:, None]).astype(jnp.float32)

def feature_map(heads, projection_low):
    scaled = heads * HEAD_DIM ** (-0.25)
    product = low_back(jnp.einsum('rhd,hdm->rhm', low(scaled), projection_low, precision=PRECISE))
    square = 0.5 * lax.optimization_barrier(jnp.sum(scaled * scaled, axis=-1, keepdims=True))
    return low(low_back(jnp.exp(product - square) / jnp.sqrt(jnp.float32(FEATURES))))

def project(normed, weight):
    return low_back(jnp.dot(normed, weight, precision=PRECISE)).reshape(normed.shape[0], HEADS, HEAD_DIM)

def block_forward(weights, long_sum, long_norm, rows, lens):
    first_gain, first_shift, query_weight, key_weight, value_weight, output_weight, output_bias, second_gain, second_shift, up_weight, up_bias, down_weight, down_bias, projection_low = weights
    table = segment_table(lens)
    normed = low(layer_norm(rows, first_gain, first_shift))
    queries = feature_map(project(normed, query_weight), projection_low)
    keys = feature_map(project(normed, key_weight), projection_low)
    values = low(project(normed, value_weight))
    short_keys = table[1:, :, None, None] * keys[None]
    short_sum = jnp.einsum('srhm,rhd->shdm', short_keys, values, precision=PRECISE)
    short_norm = lax.optimization_barrier(jnp.sum(short_keys, axis=1))
    sums = jnp.concatenate([long_sum[None], low(low_back(short_sum))], axis=0)
    norms = jnp.concatenate([long_norm[None], short_norm], axis=0)
    spread_queries = table[:, :, None, None] * queries[None]
    numer = low_back(jnp.einsum('srhm,shdm->rhd', spread_queries, sums, precision=PRECISE))
    row_norm = jnp.einsum('sr,shm->rhm', table, norms, precision=PRECISE)
    denom = lax.optimization_barrier(jnp.sum(queries * row_norm, axis=-1))
    mixed = low(low_back((numer / denom[..., None]).reshape(ROWS_DEV, D)))
    attended = rows + low_back(jnp.dot(mixed, output_weight, precision=PRECISE)) + output_bias
    second = low(layer_norm(attended, second_gain, second_shift))
    hidden = low_back(jnp.dot(second, up_weight, precision=PRECISE) + up_bias)
    active = low(jax.nn.gelu(hidden, approximate=False))
    return attended + low_back(jnp.dot(active, down_weight, precision=PRECISE)) + down_bias

def long_summary(weights, long_rows):
    normed = low(layer_norm(long_rows, weights[0], weights[1]))
    keys = feature_map(project(normed, weights[3]), weights[13])
    values = low(project(normed, weights[4]))
    return (jnp.einsum('rhm,rhd->hdm', keys, values, precision=PRECISE), lax.optimization_barrier(jnp.sum(keys, axis=0)))

def micro_forward(weights, batch_rows, lens):
    blocks = batch_rows.reshape(-1, ROWS_DEV, D)
    long_rows = blocks[:, :LONG_DEV].reshape(1, LONG_LEN, D)

    def group_summary(member_rows):
        return long_summary(weights, member_rows)
    long_sum, long_norm = lax.map(jax.checkpoint(group_summary), long_rows)
    long_low = jnp.repeat(low(low_back(long_sum)), SPAN, axis=0)
    long_norm = jnp.repeat(long_norm, SPAN, axis=0)

    def one_block(items):
        return block_forward(weights, items[2], items[3], items[0], items[1])
    return lax.map(jax.checkpoint(one_block), (blocks, lens, long_low, long_norm)).reshape(-1, D)

def reference(inputs, lengths, first_gain, first_shift, query_weight, key_weight, value_weight, output_weight, output_bias, projection, second_gain, second_shift, up_weight, up_bias, down_weight, down_bias, cotangent):
    projection_low = low(projection)
    params = (first_gain, first_shift, query_weight, key_weight, value_weight, output_weight, output_bias, second_gain, second_shift, up_weight, up_bias, down_weight, down_bias)
    outputs = []
    input_grads = []
    totals = tuple((jnp.zeros_like(item) for item in params))
    for batch in range(MICRO):
        lens = lengths[batch]

        def forward(batch_rows, *weights):
            rounded = tuple((low(weights[place]) if place in (2, 3, 4, 5, 9, 11) else weights[place] for place in range(13)))
            return micro_forward(rounded + (projection_low,), batch_rows, lens)
        result, pullback = jax.vjp(forward, inputs[batch], *params)
        grads = pullback(cotangent[batch])
        outputs.append(result)
        input_grads.append(grads[0])
        totals = tuple((first + second for first, second in zip(totals, grads[1:])))
    return (jnp.stack(outputs), jnp.stack(input_grads), totals[0], totals[1], totals[2], totals[3], totals[4], totals[5], totals[6], totals[7], totals[8], totals[9], totals[10], totals[11], totals[12])
```

```python
import functools
import math

import jax
import jax.numpy as jnp
from jax import lax
from jax.experimental import pallas as pl
from jax.experimental.pallas import tpu as pltpu
from jax.sharding import PartitionSpec as P

BF, F32 = jnp.bfloat16, jnp.float32
EPS = 1e-5
LONG = 64
TILE = 256
PAIR = 128
CHUNK = 1024
FEAT = 256
VMEM_LIMIT = 60 << 20
LOG16 = math.log(16.0)


def dot(a, b):
    return jnp.dot(a, b, preferred_element_type=F32)


def dot_nt(a, b):
    return lax.dot_general(a, b, (((1,), (1,)), ((), ())), preferred_element_type=F32)


def dot_tn(a, b):
    return lax.dot_general(a, b, (((0,), (0,)), ((), ())), preferred_element_type=F32)


def iota(shape, dim):
    return lax.broadcasted_iota(jnp.int32, shape, dim)


def normalize(rows):
    mean = jnp.mean(rows, axis=-1, keepdims=True)
    centred = rows - mean
    spread = jnp.mean(centred * centred, axis=-1, keepdims=True)
    scale = lax.rsqrt(spread + EPS)
    return centred * scale, scale


def norm_back(grad, xhat, scale):
    return scale * (
        grad
        - jnp.mean(grad, axis=-1, keepdims=True)
        - xhat * jnp.mean(grad * xhat, axis=-1, keepdims=True)
    )


def head_sums(pair):
    first = iota(pair.shape, 1) < PAIR // 2
    zero = jnp.zeros_like(pair)
    return (
        jnp.sum(jnp.where(first, pair, zero), axis=-1, keepdims=True),
        jnp.sum(jnp.where(first, zero, pair), axis=-1, keepdims=True),
    )


def features(scaled, scaled_low, proj, pair):
    cols = slice(pair * PAIR, (pair + 1) * PAIR)
    part = scaled[:, cols]
    first, second = head_sums(part * part)
    product = dot(scaled_low[:, cols], proj[pair])
    return jnp.concatenate(
        [
            jnp.exp(product[:, :FEAT] - (0.5 * first + LOG16)).astype(BF),
            jnp.exp(product[:, FEAT:] - (0.5 * second + LOG16)).astype(BF),
        ],
        axis=1,
    )


def lane_half(shape):
    return iota(shape, 1) < FEAT


def block_sums(both, norm):
    keep = (iota((PAIR, 2 * FEAT), 0) < PAIR // 2) == lane_half((PAIR, 2 * FEAT))
    zero = jnp.zeros((PAIR, 2 * FEAT), F32)
    return jnp.concatenate(
        [
            jnp.where(keep, both, zero).astype(BF),
            jnp.where(keep, jnp.broadcast_to(norm, (PAIR, 2 * FEAT)), zero).astype(BF),
        ],
        axis=0,
    )


def block_grads(both, norm):
    keep = (iota((PAIR, 2 * FEAT), 0) < PAIR // 2) == lane_half((PAIR, 2 * FEAT))
    zero = jnp.zeros((PAIR, 2 * FEAT), F32)
    row = iota((PAIR, 2 * FEAT), 0)
    high = norm.astype(BF).astype(F32)
    wide = jnp.broadcast_to(high, (PAIR, 2 * FEAT))
    rest = jnp.broadcast_to(norm - high, (PAIR, 2 * FEAT))
    return jnp.concatenate(
        [
            jnp.where(keep, both, zero).astype(BF),
            jnp.where(row == 0, wide, jnp.where(row == 1, rest, zero)).astype(BF),
        ],
        axis=0,
    )


def pack_pair(both):
    return jnp.where(lane_half((PAIR // 2, 2 * FEAT)), both[: PAIR // 2], both[PAIR // 2 :])


def unpack_pair(packed):
    return jnp.concatenate([packed, packed], axis=0)


def value_block(values, cols):
    part = values[:, cols]
    first = iota(part.shape, 1) < PAIR // 2
    zero = jnp.zeros_like(part)
    one = jnp.ones_like(part)
    top = jnp.concatenate([jnp.where(first, part, zero), jnp.where(first, one, zero)], axis=1)
    low = jnp.concatenate([jnp.where(first, zero, part), jnp.where(first, zero, one)], axis=1)
    return jnp.concatenate([top, low], axis=0)


def same_small(bounds):
    shape = (2 * LONG, 2 * LONG)

    def label(dim):
        at = iota(shape, dim)
        cut = jnp.where(at < LONG, bounds[0], LONG + bounds[1])
        return jnp.where(at < cut, 1, 0) + jnp.where(at < LONG, 0, 2)

    return label(0) == label(1)


def swap_rows(buffer, cuts):
    most = buffer.shape[1]
    width = buffer.shape[2]
    for batch in range(2):
        head = buffer[batch, LONG : 2 * LONG]
        tail = buffer[batch, most - LONG :]
        small_first = iota((LONG, width), 0) < cuts[batch]
        buffer[batch, LONG : 2 * LONG] = jnp.where(small_first, tail, head)
        buffer[batch, most - LONG :] = jnp.where(small_first, head, tail)


def edge_rows(buffer):
    most = buffer.shape[1]
    return jnp.concatenate(
        [
            buffer[0, :LONG],
            buffer[1, :LONG],
            buffer[0, most - LONG :],
            buffer[1, most - LONG :],
        ],
        axis=0,
    )


def store_edge(buffer, value):
    most = buffer.shape[1]
    buffer[0, :LONG] = value[:LONG]
    buffer[1, :LONG] = value[LONG : 2 * LONG]
    buffer[0, most - LONG :] = value[2 * LONG : 3 * LONG]
    buffer[1, most - LONG :] = value[3 * LONG :]


def digits_of(size):
    out = []
    while size > 1:
        step = 4 if size % 4 == 0 else size
        out.append(step)
        size //= step
    return tuple(out)


class Net:
    def __init__(self, digits, send, recv):
        self.digits = digits
        self.send, self.recv = send, recv
        self.me = lax.axis_index("seq")
        self.core = lax.axis_index("ffn")
        self.slots = {}
        strides = [math.prod(digits[k + 1 :]) for k in range(len(digits))]
        self.own = [lax.rem(lax.div(self.me, s), n) for s, n in zip(strides, digits)]
        self.strides = strides

    def partner(self):
        return (self.me, 1 - self.core)

    def other(self, k, step):
        return lax.rem(self.own[k] + step, self.digits[k])

    def peer(self, k, step):
        return (self.me + (self.other(k, step) - self.own[k]) * self.strides[k], self.core)

    def barrier(self):
        semaphore = pltpu.get_barrier_semaphore()
        peers = [self.partner()] + [
            self.peer(k, step) for k, n in enumerate(self.digits) for step in range(1, n)
        ]
        for peer in peers:
            pl.semaphore_signal(
                semaphore, inc=1, device_id=peer, device_id_type=pl.DeviceIdType.MESH
            )
        pl.semaphore_wait(semaphore, len(peers))

    def copy(self, key, source, target, device):
        slot = self.slots.setdefault(key, len(self.slots))
        return pltpu.make_async_remote_copy(
            src_ref=source,
            dst_ref=target,
            send_sem=self.send.at[slot],
            recv_sem=self.recv.at[slot],
            device_id=device,
            device_id_type=pl.DeviceIdType.MESH,
        )


class Gather:
    def __init__(self, net, name, out):
        self.net, self.name, self.out = net, name, out

    def copies(self, k):
        net = self.net
        depth = len(net.digits)
        if k == depth:
            block = self.out.at[net.core]
            return [net.copy((self.name, "core"), block, block, net.partner())]
        at = (net.core,) + (slice(None),) * k + tuple(net.own[k:])
        block = self.out.at[at]
        return [
            net.copy((self.name, k, step), block, block, net.peer(k, step))
            for step in range(1, net.digits[k])
        ]

    def steps(self):
        depth = len(self.net.digits)

        def start(k):
            for copy in self.copies(k):
                copy.start()

        def follow(k):
            for copy in self.copies(k - 1):
                copy.wait_recv()
            if k <= depth:
                start(k)

        return [functools.partial(start, 0)] + [
            functools.partial(follow, k) for k in range(1, depth + 2)
        ]

    def drain(self):
        for k in range(len(self.net.digits) + 1):
            for copy in self.copies(k):
                copy.wait_send()


class Scatter:
    def __init__(self, net, name, blocks, first, slots, parts, finish, apart=None):
        self.net, self.name = net, name
        self.away = (blocks if apart is None else apart).at[1 - net.core]
        self.held = blocks.at[net.core] if apart is None else blocks
        self.first, self.slots, self.parts, self.finish = first, slots, parts, finish

    @staticmethod
    def scratch(digits, rows, cols):
        shapes = [pltpu.VMEM(digits + (rows, cols), BF)]
        for k in reversed(range(len(digits))):
            shapes.append(pltpu.VMEM((digits[k] - 1,) + digits[:k] + (rows, cols), BF))
        for k in reversed(range(1, len(digits))):
            shapes.append(pltpu.VMEM(digits[:k] + (rows, cols), BF))
        return shapes

    @classmethod
    def of(cls, net, name, blocks, refs, finish, apart=None):
        depth = len(net.digits)
        slots, parts = refs[1 : 1 + depth], refs[1 + depth :]
        return cls(net, name, blocks, refs[0], slots, parts, finish, apart)

    def copies(self, k):
        net = self.net
        depth = len(net.digits)
        if k == 0:
            return [net.copy((self.name, "core"), self.away, self.first, net.partner())]
        digit = depth - k
        held = self.held if k == 1 else self.parts[k - 2]
        copies = []
        for step in range(1, net.digits[digit]):
            at = (slice(None),) * digit + (net.other(digit, step),)
            copies.append(
                net.copy(
                    (self.name, k, step),
                    held.at[at],
                    self.slots[k - 1].at[step - 1],
                    net.peer(digit, step),
                )
            )
        return copies

    def add(self, k):
        net = self.net
        depth = len(net.digits)
        if k == 0:
            lead = net.digits
            for at in _indices(lead):
                mine = self.held[at].astype(F32)
                self.held[at] = (mine + self.first[at].astype(F32)).astype(BF)
            return
        digit = depth - k
        held = self.held if k == 1 else self.parts[k - 2]
        for at in _indices(net.digits[:digit]):
            total = held[at + (net.own[digit],)].astype(F32)
            for step in range(net.digits[digit] - 1):
                total = total + self.slots[k - 1][(step,) + at].astype(F32)
            if digit:
                self.parts[k - 1][at] = total.astype(BF)
            else:
                self.finish(total)

    def steps(self):
        depth = len(self.net.digits)

        def start(k):
            for copy in self.copies(k):
                copy.start()

        def follow(k):
            for copy in self.copies(k - 1):
                copy.wait_recv()
            self.add(k - 1)
            if k <= depth:
                start(k)

        return [functools.partial(start, 0)] + [
            functools.partial(follow, k) for k in range(1, depth + 2)
        ]

    def drain(self):
        for k in range(len(self.net.digits) + 1):
            for copy in self.copies(k):
                copy.wait_send()


def _indices(lead):
    if not lead:
        return [()]
    return [(i,) + rest for i in range(lead[0]) for rest in _indices(lead[1:])]


class Whole:
    def __init__(self, net, name, held, slots):
        self.net, self.name, self.held, self.slots = net, name, held, slots

    @staticmethod
    def scratch(digits, rows, cols):
        return [
            pltpu.VMEM((len(digits) + 2, rows, cols), F32),
            pltpu.VMEM((1 + sum(n - 1 for n in digits), rows, cols), F32),
        ]

    def base(self, k):
        return 0 if k == 0 else 1 + sum(n - 1 for n in self.net.digits[: k - 1])

    def copies(self, k):
        net = self.net
        source = self.held.at[k]
        if k == 0:
            return [net.copy((self.name, 0), source, self.slots.at[0], net.partner())]
        return [
            net.copy(
                (self.name, k, step),
                source,
                self.slots.at[self.base(k) + step - 1],
                net.peer(k - 1, step),
            )
            for step in range(1, net.digits[k - 1])
        ]

    def steps(self):
        depth = len(self.net.digits)

        def start(k):
            for copy in self.copies(k):
                copy.start()

        def follow(k):
            total = self.held[k - 1]
            for i, copy in enumerate(self.copies(k - 1)):
                copy.wait_recv()
                total = total + self.slots[self.base(k - 1) + i]
            self.held[k] = total
            if k <= depth:
                start(k)

        return [functools.partial(start, 0)] + [
            functools.partial(follow, k) for k in range(1, depth + 2)
        ]

    def drain(self):
        for k in range(len(self.net.digits) + 1):
            for copy in self.copies(k):
                copy.wait_send()


def together(*parts):
    most = max(len(part) for part in parts)

    def run(i):
        for part in parts:
            if i < len(part):
                part[i]()

    return [functools.partial(run, i) for i in range(most)]


def block_shape(ways, rows, cols):
    lanes = cols * (rows // 16) // ways
    return 16, lanes


def block_at(digits, index):
    at = []
    for n in reversed(digits):
        at.append(index % n)
        index //= n
    return tuple(reversed(at))


def store_blocks(blocks, row, value):
    lanes = blocks.shape[-1]
    per_row = value.shape[1] // lanes
    ways = (2,) + blocks.shape[1:-2]
    for i in range(value.shape[0] // 16):
        for j in range(per_row):
            at = block_at(ways, (row // 16 + i) * per_row + j)
            blocks[at] = value[16 * i : 16 * i + 16, j * lanes : (j + 1) * lanes]


def load_blocks(blocks, row, rows, cols):
    lanes = blocks.shape[-1]
    per_row = cols // lanes
    ways = (2,) + blocks.shape[1:-2]
    out = []
    for i in range(rows // 16):
        line = [
            blocks[block_at(ways, (row // 16 + i) * per_row + j)] for j in range(per_row)
        ]
        out.append(line[0] if per_row == 1 else jnp.concatenate(line, axis=1))
    return jnp.concatenate(out, axis=0)


class Loads:
    def __init__(self, semaphores):
        self.semaphores = semaphores
        self.count = 0

    def start(self, source, target):
        copy = pltpu.make_async_copy(source, target, self.semaphores.at[self.count])
        self.count += 1
        copy.start()
        return copy


PIECES = ((0, 128), (1088, 64), (128, 192), (320, 256), (576, 256), (832, 256))


def raw_pieces(rows):
    quarter = (rows - 2 * LONG) // 4
    pieces = [(0, 2 * LONG), (rows - LONG, LONG), (2 * LONG, quarter - LONG)]
    return pieces + [(LONG + quarter * i, quarter) for i in range(1, 4)]


def big_start(batch, rows_big, step, tile):
    return TILE + batch * rows_big + step * tile


def attention_forward(
    digits, cuts, x_hbm, vec, wqkv, wo, proj, block,
    k_out, q_out, v_out, ks_out, qs_out, n_out, mix_out, inv_out, att_out, sd_out, small_out, w_out,
    x, kf, qf, v, ks, qs, n, mix, inv, att, sd, small, acc, nacc, parts, total,
    load_sem, store_sem, own_sem, send, recv, whole_held, whole_slots, *slots,
):
    rows = x.shape[1]
    big = rows - 2 * LONG
    pairs = proj.shape[0]
    width = wo.shape[0]
    scale = (PAIR // 2) ** -0.25
    net = Net(digits, send, recv)
    loads = Loads(load_sem)
    pending = {}
    for piece in raw_pieces(rows):
        for batch in range(2):
            span = pl.ds(*piece)
            pending[batch, piece] = loads.start(x_hbm.at[batch, span], x.at[batch, span])
    first, *later = raw_pieces(rows)
    edges = [first, later[0]]
    place = pltpu.make_async_copy(block, w_out.at[(net.core,) + tuple(net.own)], own_sem)
    place.start()
    net.barrier()
    place.wait()
    gather = Gather(net, "w", w_out)
    gather_steps = gather.steps()
    gather_steps[0]()

    def finish(value):
        total[(net.core,) + tuple(net.own)] = value.astype(BF)

    scatter = Scatter.of(net, "s", parts, slots, finish)
    spread = Gather(net, "t", total)
    whole = Whole(net, "n", whole_held, whole_slots)
    scatter_steps = scatter.steps()
    spread_steps = spread.steps()
    depth = len(digits)

    def turn():
        scatter_steps[-1]()
        spread_steps[0]()

    sum_steps = together(scatter_steps[:-1] + [turn] + spread_steps[1:], whole.steps())

    def front(rows_x):
        xhat, _ = normalize(rows_x)
        low = (xhat * vec[0:1] + vec[1:2]).astype(BF)
        raw = dot(low, wqkv[...])
        q = raw[:, :width] * scale
        k = raw[:, width : 2 * width] * scale
        return low, q, k, raw[:, 2 * width :].astype(BF)

    def attend(numer_denom, at, pair):
        cols = slice(pair * PAIR, (pair + 1) * PAIR)
        inverse = 1.0 / numer_denom[:, PAIR:]
        inv[at, cols] = inverse
        mix[at, cols] = (numer_denom[:, :PAIR] * inverse).astype(BF)

    for batch in range(2):
        for piece in edges:
            pending[batch, piece].wait()
    swap_rows(x, [cuts[0, 0], cuts[1, 0]])
    edge = slice(0, TILE)
    x_edge = edge_rows(x)
    low, q, k, values = front(x_edge)
    n[edge] = low
    v[edge] = values
    k_low = k.astype(BF)
    ks[edge] = k_low
    for pair in range(pairs):
        cols = slice(pair * PAIR, (pair + 1) * PAIR)
        feats = slice(pair * 2 * FEAT, (pair + 1) * 2 * FEAT)
        mapped = features(k, k_low, proj, pair)
        kf[edge, feats] = mapped
        for batch in range(2):
            own = slice(batch * LONG, (batch + 1) * LONG)
            both = dot_tn(values[own, cols], mapped[own])
            row = batch * pairs + pair
            store_blocks(parts, row * LONG, pack_pair(both).astype(BF))
            whole_held[0, row : row + 1] = jnp.sum(mapped[own].astype(F32), axis=0, keepdims=True)
    sum_steps[0]()
    q_low = q.astype(BF)
    qs[edge] = q_low
    same = same_small([cuts[0, 1], cuts[1, 1]])
    shorts = slice(2 * LONG, TILE)
    for pair in range(pairs):
        cols = slice(pair * PAIR, (pair + 1) * PAIR)
        feats = slice(pair * 2 * FEAT, (pair + 1) * 2 * FEAT)
        mapped = features(q, q_low, proj, pair)
        qf[edge, feats] = mapped
        weights = []
        for head in range(2):
            lanes = slice((2 * pair + head) * FEAT, (2 * pair + head + 1) * FEAT)
            score = dot_nt(
                mapped[shorts, head * FEAT : (head + 1) * FEAT], kf[shorts, lanes]
            )
            score = jnp.where(same, score, 0.0).astype(BF)
            small[2 * pair + head] = score
            weights.append(score)
        attend(
            dot(jnp.concatenate(weights, axis=1), value_block(values[shorts], cols)), shorts, pair
        )

    stores = []

    def store(source, target, at, slot):
        copy = pltpu.make_async_copy(source.at[at], target.at[at], store_sem.at[slot])
        copy.start()

    store(kf, k_out, pl.ds(0, TILE), 0)
    store(qf, q_out, pl.ds(0, TILE), 1)
    store(v, v_out, pl.ds(0, TILE), 2)
    store(ks, ks_out, pl.ds(0, TILE), 3)
    store(qs, qs_out, pl.ds(0, TILE), 4)
    store(n, n_out, pl.ds(0, TILE), 5)
    small_copy = pltpu.make_async_copy(small, small_out, store_sem.at[9])
    small_copy.start()

    for piece in later[1:]:
        for batch in range(2):
            pending[batch, piece].wait()
    acc[...] = jnp.zeros_like(acc)
    nacc[...] = jnp.zeros_like(nacc)
    per = big // TILE
    comm = [None] * (2 * 2 * per)
    for i, step in enumerate(sum_steps[1:]):
        comm[i] = step
    for i, step in enumerate(gather_steps[1:]):
        spot = 1 + 3 * i
        comm[spot] = step if comm[spot] is None else functools.partial(_both, comm[spot], step)

    def pass_one(t, _):
        batch, step = lax.div(t, per), lax.rem(t, per)
        for i in range(2 * per):
            if comm[i] is not None:
                pl.when(t == i)(comm[i])
        raw_at = pl.ds(pl.multiple_of(LONG + step * TILE, LONG), TILE)
        at = pl.ds(pl.multiple_of(TILE + t * TILE, TILE), TILE)
        low, q, k, values = front(x[batch, raw_at])
        n[at] = low
        v[at] = values
        k_low = k.astype(BF)
        q_low = q.astype(BF)
        ks[at] = k_low
        qs[at] = q_low
        for pair in range(pairs):
            cols = slice(pair * PAIR, (pair + 1) * PAIR)
            feats = slice(pair * 2 * FEAT, (pair + 1) * 2 * FEAT)
            mapped = features(k, k_low, proj, pair)
            kf[at, feats] = mapped
            acc[batch, pair] += dot_tn(values[:, cols], mapped)
            nacc[batch, pair] += jnp.sum(mapped.astype(F32), axis=0, keepdims=True)
            qf[at, feats] = features(q, q_low, proj, pair)
        store(kf, k_out, at, 0)
        store(qf, q_out, at, 1)
        store(v, v_out, at, 2)
        store(ks, ks_out, at, 3)
        store(qs, qs_out, at, 4)
        store(n, n_out, at, 5)
        return 0

    lax.fori_loop(0, 2 * per, pass_one, 0)
    for batch in range(2):
        for pair in range(pairs):
            sd[batch, pair] = block_sums(acc[batch, pair], nacc[batch, pair])

    def pass_two(t, _):
        batch, step = lax.div(t, per), lax.rem(t, per)
        for i in range(2 * per):
            if comm[2 * per + i] is not None:
                pl.when(t == i)(comm[2 * per + i])
        raw_at = pl.ds(pl.multiple_of(LONG + step * TILE, LONG), TILE)
        at = pl.ds(pl.multiple_of(TILE + t * TILE, TILE), TILE)
        for pair in range(pairs):
            feats = slice(pair * 2 * FEAT, (pair + 1) * 2 * FEAT)
            attend(dot_nt(qf[at, feats], sd[batch, pair]), at, pair)
        att[at] = x[batch, raw_at] + dot(mix[at], wo[...]) + vec[2:3]
        store(mix, mix_out, at, 6)
        store(inv, inv_out, at, 7)
        store(att, att_out, at, 8)
        return 0

    lax.fori_loop(0, 2 * per, pass_two, 0)
    for batch in range(2):
        own = slice(batch * LONG, (batch + 1) * LONG)
        for pair in range(pairs):
            feats = slice(pair * 2 * FEAT, (pair + 1) * 2 * FEAT)
            row = batch * pairs + pair
            packed = load_blocks(total, row * LONG, LONG, 2 * FEAT).astype(F32)
            sd[2 + batch, pair] = block_sums(
                unpack_pair(packed), whole_held[depth + 1, row : row + 1]
            )
            attend(dot_nt(qf[own, feats], sd[2 + batch, pair]), own, pair)
    att[edge] = edge_rows(x) + dot(mix[edge], wo[...]) + vec[2:3]
    store(mix, mix_out, pl.ds(0, TILE), 6)
    store(inv, inv_out, pl.ds(0, TILE), 7)
    store(att, att_out, pl.ds(0, TILE), 8)
    sd_copy = pltpu.make_async_copy(sd, sd_out, store_sem.at[10])
    sd_copy.start()
    pairs_out = (
        (kf, k_out), (qf, q_out), (v, v_out), (ks, ks_out), (qs, qs_out), (n, n_out),
        (mix, mix_out), (inv, inv_out), (att, att_out),
    )
    for slot, (source, target) in enumerate(pairs_out):
        pltpu.make_async_copy(source, target, store_sem.at[slot]).wait()
    small_copy.wait()
    sd_copy.wait()
    gather.drain()
    scatter.drain()
    spread.drain()
    whole.drain()


def _both(first, second):
    first()
    second()


def feed_forward(
    cuts, cot_hbm, att_hbm, mix_hbm, inv_hbm, w_hbm, wo, vec, up_bias,
    out_hbm, ga_out, g_out, x_out, wo_grad, vec_grad, bias_grad,
    cot, att, mix, inv, w, up, down, dup, ddown, gr, load_sem, store_sem,
):
    rows = cot.shape[1]
    big = rows - 2 * LONG
    width = wo.shape[0]
    pairs = width // PAIR
    tile = big // 2
    loads = Loads(load_sem)
    lead = w.shape[:-2]
    deep = w.shape[-2] // 2
    half = w.shape[-1]
    wait_w = loads.start(w_hbm, w)
    pending = {}
    pieces = raw_pieces(rows)
    inner = [(0, TILE)] + [(TILE + tile * i, tile) for i in range(2 * big // tile)]
    for piece in pieces[:2]:
        for batch in range(2):
            span = pl.ds(*piece)
            pending[batch, piece] = loads.start(cot_hbm.at[batch, span], cot.at[batch, span])
    waits = []
    for i, piece in enumerate(inner):
        span = pl.ds(*piece)
        waits.append(
            [
                loads.start(a.at[span], b.at[span])
                for a, b in ((att_hbm, att), (mix_hbm, mix), (inv_hbm, inv))
            ]
        )
        if i == 0:
            for piece in pieces[2:]:
                for batch in range(2):
                    span = pl.ds(*piece)
                    pending[batch, piece] = loads.start(
                        cot_hbm.at[batch, span], cot.at[batch, span]
                    )
    wait_w.wait()
    group = max(1, 16 // deep)
    members = _indices(lead[1:])
    for core in range(2):
        cols = slice(core * half, (core + 1) * half)
        for first in range(0, len(members), group):
            parts = [w[(core,) + members[first + i]] for i in range(group)]
            at = slice(first * deep, (first + group) * deep)
            if group == 1:
                up[at, cols] = parts[0][:deep]
                down[at, cols] = parts[0][deep:]
            else:
                up[at, cols] = jnp.concatenate([part[:deep] for part in parts], axis=0)
                down[at, cols] = jnp.concatenate([part[deep:] for part in parts], axis=0)
    for batch in range(2):
        for piece in pieces[:2]:
            pending[batch, piece].wait()
    swap_rows(cot, [cuts[0, 0], cuts[1, 0]])
    dup[...] = jnp.zeros_like(dup)
    ddown[...] = jnp.zeros_like(ddown)
    wo_grad[...] = jnp.zeros_like(wo_grad)
    vec_grad[...] = jnp.zeros_like(vec_grad)
    bias_grad[...] = jnp.zeros_like(bias_grad)

    def add_row(at, value):
        vec_grad[at : at + 1] += jnp.sum(value, axis=0, keepdims=True)

    def block(att_rows, grad_out, at):
        xhat, scale = normalize(att_rows)
        second = (xhat * vec[0:1] + vec[1:2]).astype(BF)
        grad_low = grad_out.astype(BF)
        second_turned, grad_turned = second.T, grad_low.T
        branch = grad_second = None
        for first in range(0, up.shape[1], CHUNK):
            cols = slice(first, first + CHUNK)
            hidden = dot(second, up[:, cols]) + up_bias[:, cols]
            gauss = jnp.exp(-0.5 * hidden * hidden) * (1.0 / math.sqrt(2.0 * math.pi))
            cdf = 0.5 + 0.5 * lax.erf(hidden * math.sqrt(0.5))
            active = (hidden * cdf).astype(BF)
            slope = cdf + hidden * gauss
            grad_hidden = (dot(grad_low, down[:, cols]) * slope).astype(BF)
            term = dot_nt(active, down[:, cols])
            grad_term = dot_nt(grad_hidden, up[:, cols])
            branch = term if branch is None else branch + term
            grad_second = grad_term if grad_second is None else grad_second + grad_term
            dup[:, cols] += dot(second_turned, grad_hidden)
            ddown[:, cols] += dot(grad_turned, active)
            bias_grad[:, cols] += jnp.sum(grad_hidden.astype(F32), axis=0, keepdims=True)
        output = att_rows + branch + vec[2:3]
        grad_att = grad_out + norm_back(grad_second * vec[0:1], xhat, scale)
        add_row(2, grad_att)
        add_row(3, grad_second * xhat)
        add_row(4, grad_second)
        add_row(5, grad_out)
        grad_att_low = grad_att.astype(BF)
        mixed = mix[at]
        wo_grad[...] += dot_tn(mixed, grad_att_low)
        grad_mixed = dot_nt(grad_att_low, wo[...]).astype(BF).astype(F32)
        for pair in range(pairs):
            cols = slice(pair * PAIR, (pair + 1) * PAIR)
            part = grad_mixed[:, cols]
            inverse = inv[at, cols]
            first, last = head_sums(part * mixed[:, cols].astype(F32))
            lane = iota(part.shape, 1)
            grad_denom = -jnp.where(lane < PAIR // 2, first, last) * inverse
            high = grad_denom.astype(BF).astype(F32)
            both = jnp.where(lane % (PAIR // 2) < PAIR // 4, high, grad_denom - high)
            gr[at, 2 * pair * PAIR : (2 * pair + 1) * PAIR] = (part * inverse).astype(BF)
            gr[at, (2 * pair + 1) * PAIR : (2 * pair + 2) * PAIR] = (
                both * (4.0 / PAIR)
            ).astype(BF)
        att[at] = grad_att
        return output

    def store(at):
        pltpu.make_async_copy(att.at[at], ga_out.at[at], store_sem.at[0]).start()
        pltpu.make_async_copy(gr.at[at], g_out.at[at], store_sem.at[1]).start()

    edge = pl.ds(0, TILE)
    for copy in waits[0]:
        copy.wait()
    cot_edge = edge_rows(cot)
    store_edge(cot, block(att[edge], cot_edge, edge))
    store(edge)
    for batch in range(2):
        for piece in pieces[2:]:
            pending[batch, piece].wait()
    for more in waits[1:]:
        for copy in more:
            copy.wait()
    per = big // tile

    def one(t, _):
        batch, step = lax.div(t, per), lax.rem(t, per)
        raw_at = pl.ds(pl.multiple_of(LONG + step * tile, LONG), tile)
        at = pl.ds(pl.multiple_of(TILE + t * tile, TILE), tile)
        cot[batch, raw_at] = block(att[at], cot[batch, raw_at], at)
        store(at)
        return 0

    lax.fori_loop(0, 2 * per, one, 0)
    swap_rows(cot, [cuts[0, 0], cuts[1, 0]])
    out_copy = pltpu.make_async_copy(cot, out_hbm, store_sem.at[2])
    out_copy.start()
    for core in range(2):
        cols = slice(core * half, (core + 1) * half)
        for i, member in enumerate(members):
            at = slice(i * deep, (i + 1) * deep)
            w[(core,) + member] = jnp.concatenate(
                [dup[at, cols], ddown[at, cols]], axis=0
            ).astype(BF)
    x_copy = pltpu.make_async_copy(w, x_out, store_sem.at[3])
    x_copy.start()
    pltpu.make_async_copy(att, ga_out, store_sem.at[0]).wait()
    pltpu.make_async_copy(gr, g_out, store_sem.at[1]).wait()
    out_copy.wait()
    x_copy.wait()


def attention_backward(
    digits, cuts, x_hbm, ga_hbm, g_hbm, k_hbm, q_hbm, v_hbm, ks_hbm, qs_hbm, n_hbm,
    sd_hbm, small, ffn_hbm, wo_grad, vec_in, bias_in, vec, wqkv, back,
    in_grad, ffn_out, shared_out, vec_out,
    kf, v, ks, qs, n, sd, sg, ffn, total, parts, long_total,
    load_sem, store_sem, send, recv, *refs,
):
    rows = x_hbm.shape[1]
    big = rows - 2 * LONG
    pairs = back.shape[0]
    width = wqkv.shape[0]
    inner_rows = kf.shape[0]
    scale = (PAIR // 2) ** -0.25
    depth = len(digits)
    net = Net(digits, send, recv)
    each = 2 * depth
    ffn_refs, refs = refs[:each], refs[each:]
    shared_refs, refs = refs[:each], refs[each:]
    long_refs, refs = refs[:each], refs[each:]
    norm_held, norm_slots, vec_held, vec_slots = refs
    loads = Loads(load_sem)
    per = big // TILE
    steps = 2 * per
    shorts = slice(2 * LONG, TILE)
    edge = slice(0, TILE)
    same = same_small([cuts[0, 1], cuts[1, 1]])

    def finish_ffn(value):
        ffn_out[...] = value

    ffn_sum = Scatter.of(net, "f", ffn, ffn_refs, finish_ffn, apart=ffn_hbm)

    def finish_long(value):
        long_total[(net.core,) + tuple(net.own)] = value.astype(BF)

    long_sum = Scatter.of(net, "s", parts, long_refs, finish_long)
    long_spread = Gather(net, "t", long_total)
    norm_sum = Whole(net, "n", norm_held, norm_slots)
    vec_sum = Whole(net, "v", vec_held, vec_slots)

    def all_reduce(scatter, spread):
        first, second = scatter.steps(), spread.steps()
        return first[:-1] + [functools.partial(_both, first[-1], second[0])] + second[1:]

    long_steps = together(all_reduce(long_sum, long_spread), norm_sum.steps())
    ffn_steps = ffn_sum.steps()
    vec_steps = vec_sum.steps()
    comm = [[] for _ in range(2 * steps)]
    for i, step in enumerate(long_steps[1:]):
        comm[i].append(step)
    for i, step in enumerate(ffn_steps[1:]):
        comm[min(1 + 4 * i, 2 * steps - 1)].append(step)

    def talk(t, base):
        for i in range(steps):
            if comm[base + i]:
                pl.when(t == i)(functools.partial(_all, comm[base + i]))

    def feat_lanes(pair):
        return slice(pair * 2 * FEAT, (pair + 1) * 2 * FEAT)

    def pair_cols(pair):
        return slice(pair * PAIR, (pair + 1) * PAIR)

    def grad_lanes(pair):
        return slice(2 * pair * PAIR, (2 * pair + 2) * PAIR)

    def feature_back(grad, mapped, scaled, pair):
        term = (grad * mapped.astype(F32)).astype(BF)
        both = dot(term, back[pair])
        return (
            (both[:, :PAIR] - scaled[:, pair_cols(pair)].astype(F32) * both[:, PAIR:]) * scale
        ).astype(BF)

    def norm_rows(both):
        return jnp.where(
            lane_half((1, 2 * FEAT)),
            jnp.sum(both[PAIR : PAIR + PAIR // 2], axis=0, keepdims=True),
            jnp.sum(both[PAIR + PAIR // 2 :], axis=0, keepdims=True),
        )

    def ones_beside(values):
        return jnp.concatenate([values, jnp.ones_like(values)], axis=1)

    inner = [(0, TILE)] + [(TILE + big * i, big) for i in range(2)]

    def load(pairs_of):
        waits = []
        for piece in inner:
            span = pl.ds(*piece)
            waits.append([loads.start(a.at[span], b.at[span]) for a, b in pairs_of])
        return waits

    def query_phase(qf, gr, acc):
        early = load([(g_hbm, gr), (q_hbm, qf), (qs_hbm, qs), (k_hbm, kf), (v_hbm, v), (ks_hbm, ks)])
        wait_sd = loads.start(sd_hbm, sd)
        wait_ffn = loads.start(ffn_hbm.at[net.core], ffn)
        late = load([(n_hbm, n)])
        net.barrier()
        for copy in early[0]:
            copy.wait()
        for batch in range(2):
            own = slice(batch * LONG, (batch + 1) * LONG)
            for pair in range(pairs):
                both = dot_tn(gr[own, grad_lanes(pair)], qf[own, feat_lanes(pair)])
                row = batch * pairs + pair
                store_blocks(parts, row * LONG, pack_pair(both[:PAIR]).astype(BF))
                norm_held[0, row : row + 1] = norm_rows(both)
        long_steps[0]()
        ffn_steps[0]()
        wait_sd.wait()
        for pair in range(pairs):
            lanes, cols = feat_lanes(pair), pair_cols(pair)
            mapped_q, mapped_k = qf[edge, lanes], kf[shorts, lanes]
            grads, values = gr[edge, grad_lanes(pair)], v[shorts, cols]
            grad_q = [
                dot(grads[batch * LONG : (batch + 1) * LONG], sd[2 + batch, pair])
                for batch in range(2)
            ]
            weight = dot_nt(grads[shorts], value_block(values, slice(0, PAIR)))
            more_q, more_k, more_v = [], [], []
            for head in range(2):
                own = slice(head * FEAT, (head + 1) * FEAT)
                part = jnp.where(same, weight[:, head * PAIR : (head + 1) * PAIR], 0.0).astype(BF)
                more_q.append(dot(part, mapped_k[:, own]))
                more_k.append(dot_tn(part, mapped_q[shorts, own]))
                more_v.append(dot_tn(small[2 * pair + head], grads[shorts, :PAIR]))
            grad_q.append(jnp.concatenate(more_q, axis=1))
            grad_k = jnp.concatenate(more_k, axis=1)
            grad_v = jnp.where(iota((2 * LONG, PAIR), 1) < PAIR // 2, more_v[0], more_v[1])
            qs[edge, cols] = feature_back(
                jnp.concatenate(grad_q, axis=0), mapped_q, qs[edge], pair
            )
            ks[shorts, cols] = feature_back(grad_k, mapped_k, ks[shorts], pair)
            v[shorts, cols] = grad_v.astype(BF)
        for more in early[1:] + late:
            for copy in more:
                copy.wait()
        wait_ffn.wait()
        acc[...] = jnp.zeros_like(acc)

        def queries(t, _):
            batch = lax.div(t, per)
            talk(t, 0)
            at = pl.ds(pl.multiple_of(TILE + t * TILE, TILE), TILE)
            for pair in range(pairs):
                mapped = qf[at, feat_lanes(pair)]
                grads = gr[at, grad_lanes(pair)]
                acc[batch, pair] += dot_tn(grads, mapped)
                grad = dot(grads, sd[batch, pair])
                qs[at, pair_cols(pair)] = feature_back(grad, mapped, qs[at], pair)
            return 0

        lax.fori_loop(0, steps, queries, 0)
        for batch in range(2):
            for pair in range(pairs):
                both = acc[batch, pair]
                sg[batch, pair] = block_grads(both[:PAIR], norm_rows(both))

    def key_phase(x, ga, wgrad, shared):
        wait_x = [loads.start(x_hbm, x), loads.start(ga_hbm, ga)]
        wgrad[...] = jnp.zeros_like(wgrad)

        def finish_shared(value):
            total[(net.core,) + tuple(net.own)] = value.astype(BF)

        shared_sum = Scatter.of(net, "g", shared, shared_refs, finish_shared)
        shared_spread = Gather(net, "h", total)
        shared_steps = all_reduce(shared_sum, shared_spread)

        def add_weights(at):
            turned = n[at].T
            wgrad[:, :width] += dot(turned, qs[at])
            wgrad[:, width : 2 * width] += dot(turned, ks[at])
            wgrad[:, 2 * width :] += dot(turned, v[at])

        def keys(t, _):
            batch = lax.div(t, per)
            talk(t, steps)
            at = pl.ds(pl.multiple_of(TILE + t * TILE, TILE), TILE)
            for pair in range(pairs):
                mapped = kf[at, feat_lanes(pair)]
                grad = dot(ones_beside(v[at, pair_cols(pair)]), sg[batch, pair])
                v[at, pair_cols(pair)] = dot_nt(mapped, sg[batch, pair, :PAIR]).astype(BF)
                ks[at, pair_cols(pair)] = feature_back(grad, mapped, ks[at], pair)
            add_weights(at)
            return 0

        lax.fori_loop(0, steps, keys, 0)
        for batch in range(2):
            own = slice(batch * LONG, (batch + 1) * LONG)
            for pair in range(pairs):
                lanes, cols = feat_lanes(pair), pair_cols(pair)
                row = batch * pairs + pair
                packed = load_blocks(long_total, row * LONG, LONG, 2 * FEAT).astype(F32)
                grads = block_grads(unpack_pair(packed), norm_held[depth + 1, row : row + 1])
                mapped = kf[own, lanes]
                grad = dot(ones_beside(v[own, cols]), grads)
                v[own, cols] = dot_nt(mapped, grads[:PAIR]).astype(BF)
                ks[own, cols] = feature_back(grad, mapped, ks[own], pair)
        add_weights(edge)
        for i in range(width // 16):
            at = slice(16 * i, 16 * i + 16)
            line = jnp.concatenate([wgrad[at], wo_grad[at]], axis=1).astype(BF)
            store_blocks(shared, 16 * i, line)
        shared_steps[0]()
        for copy in wait_x:
            copy.wait()
        swap_rows(x, [cuts[0, 0], cuts[1, 0]])
        vec_held[0] = jnp.zeros(vec_held.shape[1:], F32)
        vec_held[0, 2:6] = vec_in[2:6]
        for i in range(bias_in.shape[1] // width):
            vec_held[0, 6 + i : 7 + i] = bias_in[:, i * width : (i + 1) * width]

        def last(rows_x, rows_ga, at):
            xhat, spread = normalize(rows_x)
            grad = (
                dot_nt(qs[at], wqkv[:, :width])
                + dot_nt(ks[at], wqkv[:, width : 2 * width])
                + dot_nt(v[at], wqkv[:, 2 * width :])
            )
            vec_held[0, 0:1] += jnp.sum(grad * xhat, axis=0, keepdims=True)
            vec_held[0, 1:2] += jnp.sum(grad, axis=0, keepdims=True)
            return rows_ga + norm_back(grad * vec[0:1], xhat, spread)

        store_edge(x, last(edge_rows(x), ga[edge], edge))
        final = [[] for _ in range(steps)]
        for i, step in enumerate(shared_steps[1:]):
            final[min(i, steps - 1)].append(step)

        def inputs(t, _):
            batch, step = lax.div(t, per), lax.rem(t, per)
            for i in range(steps):
                if final[i]:
                    pl.when(t == i)(functools.partial(_all, final[i]))
            raw_at = pl.ds(pl.multiple_of(LONG + step * TILE, LONG), TILE)
            at = pl.ds(pl.multiple_of(TILE + t * TILE, TILE), TILE)
            x[batch, raw_at] = last(x[batch, raw_at], ga[at], at)
            return 0

        lax.fori_loop(0, steps, inputs, 0)
        vec_steps[0]()
        swap_rows(x, [cuts[0, 0], cuts[1, 0]])
        copy = pltpu.make_async_copy(x, in_grad, store_sem.at[0])
        copy.start()
        spread_copy = pltpu.make_async_copy(total, shared_out, store_sem.at[1])
        spread_copy.start()
        for step in vec_steps[1:]:
            step()
        vec_out[...] = vec_held[depth + 1]
        copy.wait()
        spread_copy.wait()
        shared_sum.drain()
        shared_spread.drain()

    wide = kf.shape[1]
    pl.run_scoped(
        query_phase,
        pltpu.VMEM((inner_rows, wide), BF),
        pltpu.VMEM((inner_rows, 2 * width), BF),
        pltpu.VMEM((2, pairs, 2 * PAIR, 2 * FEAT), F32),
    )
    pl.run_scoped(
        key_phase,
        pltpu.VMEM(x_hbm.shape, F32),
        pltpu.VMEM((inner_rows, width), F32),
        pltpu.VMEM((width, 3 * width), F32),
        pltpu.VMEM(total.shape, BF),
    )
    for item in (ffn_sum, long_sum, long_spread, norm_sum, vec_sum):
        item.drain()


def _all(steps):
    for step in steps:
        step()


def body(
    inputs,
    lengths,
    first_gain,
    first_shift,
    query_weight,
    key_weight,
    value_weight,
    output_weight,
    output_bias,
    projection,
    second_gain,
    second_shift,
    up_weight,
    up_bias,
    down_weight,
    down_bias,
    cotangent,
):
    heads, head_size, feats = projection.shape
    batches, rows, width = inputs.shape
    digits = digits_of(lax.axis_size("seq"))
    ways = 2 * math.prod(digits)
    depth = len(digits)
    pairs = heads // 2
    big = rows - 2 * LONG
    inner = TILE + batches * big
    deep, half = up_weight.shape
    hidden = up_bias.shape[0]

    lens = lengths[:, 0, :]
    cut = jnp.where(
        lens[:, 0] == big, 0, jnp.where(lens[:, 1] == big, lens[:, 0], lens[:, 0] + lens[:, 1])
    )
    bound = jnp.where(lens[:, 0] == big, lens[:, 1], lens[:, 0])
    cuts = jnp.stack([cut, bound], axis=1)
    wqkv = jnp.concatenate([query_weight, key_weight, value_weight], axis=1).astype(BF)
    wo = output_weight.astype(BF)
    proj_low = projection.astype(BF).reshape(pairs, 2, head_size, feats)
    zero = jnp.zeros((pairs, head_size, feats), BF)
    proj = jnp.concatenate(
        [
            jnp.concatenate([proj_low[:, 0], zero], axis=2),
            jnp.concatenate([zero, proj_low[:, 1]], axis=2),
        ],
        axis=1,
    )
    turned = jnp.swapaxes(proj_low, 2, 3)
    gap = jnp.zeros((pairs, feats, head_size), BF)
    one = jnp.ones((pairs, feats, head_size), BF)
    back = jnp.concatenate(
        [
            jnp.concatenate([turned[:, 0], gap, one, gap], axis=2),
            jnp.concatenate([gap, turned[:, 1], gap, one], axis=2),
        ],
        axis=1,
    )
    block = jnp.concatenate([up_weight, down_weight.T], axis=0).astype(BF)

    hbm = pl.BlockSpec(memory_space=pl.ANY)
    vmem = pl.BlockSpec(memory_space=pltpu.VMEM)
    smem = pl.BlockSpec(memory_space=pltpu.SMEM)

    def shape(*dims, dtype=BF):
        return jax.ShapeDtypeStruct(dims, dtype)

    wide = 2 * FEAT * pairs
    long_block = block_shape(ways, batches * pairs * LONG, 2 * FEAT)
    inner_shapes = [
        ((inner, wide), BF), ((inner, wide), BF), ((inner, width), BF), ((inner, width), BF),
        ((inner, width), BF), ((inner, width), BF), ((inner, width), BF), ((inner, width), F32),
        ((inner, width), F32), ((4, pairs, 2 * PAIR, 2 * FEAT), BF),
        ((heads, 2 * LONG, 2 * LONG), BF),
    ]
    kf, qf, v, ks, qs, n, mix, inv, att, sd, small, w = pl.pallas_call(
        functools.partial(attention_forward, digits),
        out_shape=[shape(*dims, dtype=kind) for dims, kind in inner_shapes]
        + [shape(2, *digits, 2 * deep, half)],
        in_specs=[smem, hbm, vmem, vmem, vmem, vmem, vmem],
        out_specs=[hbm] * 12,
        scratch_shapes=[pltpu.VMEM(inputs.shape, F32)]
        + [pltpu.VMEM(dims, kind) for dims, kind in inner_shapes]
        + [
            pltpu.VMEM((batches, pairs, PAIR, 2 * FEAT), F32),
            pltpu.VMEM((batches, pairs, 1, 2 * FEAT), F32),
            pltpu.VMEM((2,) + digits + long_block, BF),
            pltpu.VMEM((2,) + digits + long_block, BF),
            pltpu.SemaphoreType.DMA((16,)),
            pltpu.SemaphoreType.DMA((16,)),
            pltpu.SemaphoreType.DMA,
            pltpu.SemaphoreType.DMA((64,)),
            pltpu.SemaphoreType.DMA((64,)),
        ]
        + Whole.scratch(digits, batches * pairs, 2 * FEAT)
        + Scatter.scratch(digits, *long_block),
        compiler_params=pltpu.CompilerParams(
            collective_id=0, has_side_effects=True, vmem_limit_bytes=VMEM_LIMIT
        ),
        name="attention_forward",
    )(
        cuts,
        inputs,
        jnp.stack([first_gain, first_shift, output_bias]),
        wqkv,
        wo,
        proj,
        block,
    )

    output, ga, gr, ffn, wo_grad, vec_in, bias_in = pl.pallas_call(
        feed_forward,
        out_shape=[
            shape(*inputs.shape, dtype=F32),
            shape(inner, width, dtype=F32),
            shape(inner, 2 * width),
            shape(2, *digits, 2 * deep, half),
            shape(width, width, dtype=F32),
            shape(8, width, dtype=F32),
            shape(1, hidden, dtype=F32),
        ],
        in_specs=[smem, hbm, hbm, hbm, hbm, hbm, vmem, vmem, vmem],
        out_specs=[hbm] * 4 + [vmem] * 3,
        scratch_shapes=[
            pltpu.VMEM(inputs.shape, F32),
            pltpu.VMEM((inner, width), F32),
            pltpu.VMEM((inner, width), BF),
            pltpu.VMEM((inner, width), F32),
            pltpu.VMEM((2,) + digits + (2 * deep, half), BF),
            pltpu.VMEM((width, hidden), BF),
            pltpu.VMEM((width, hidden), BF),
            pltpu.VMEM((width, hidden), F32),
            pltpu.VMEM((width, hidden), F32),
            pltpu.VMEM((inner, 2 * width), BF),
            pltpu.SemaphoreType.DMA((32,)),
            pltpu.SemaphoreType.DMA((4,)),
        ],
        compiler_params=pltpu.CompilerParams(vmem_limit_bytes=VMEM_LIMIT),
        name="feed_forward",
    )(
        cuts,
        cotangent,
        att,
        mix,
        inv,
        w,
        wo,
        jnp.stack([second_gain, second_shift, down_bias]),
        up_bias[None],
    )

    shared_block = block_shape(ways, width, 4 * width)
    in_grad, ffn_grad, shared, vectors = pl.pallas_call(
        functools.partial(attention_backward, digits),
        out_shape=[
            shape(*inputs.shape, dtype=F32),
            shape(2 * deep, half, dtype=F32),
            shape(2, *digits, *shared_block),
            shape(16, width, dtype=F32),
        ],
        in_specs=[smem] + [hbm] * 10 + [vmem, hbm] + [vmem] * 6,
        out_specs=[hbm, vmem, hbm, vmem],
        scratch_shapes=[
            pltpu.VMEM((inner, wide), BF),
            pltpu.VMEM((inner, width), BF),
            pltpu.VMEM((inner, width), BF),
            pltpu.VMEM((inner, width), BF),
            pltpu.VMEM((inner, width), BF),
            pltpu.VMEM((4, pairs, 2 * PAIR, 2 * FEAT), BF),
            pltpu.VMEM((batches, pairs, 2 * PAIR, 2 * FEAT), BF),
            pltpu.VMEM(digits + (2 * deep, half), BF),
            pltpu.VMEM((2,) + digits + shared_block, BF),
            pltpu.VMEM((2,) + digits + long_block, BF),
            pltpu.VMEM((2,) + digits + long_block, BF),
            pltpu.SemaphoreType.DMA((32,)),
            pltpu.SemaphoreType.DMA((2,)),
            pltpu.SemaphoreType.DMA((96,)),
            pltpu.SemaphoreType.DMA((96,)),
        ]
        + Scatter.scratch(digits, 2 * deep, half)
        + Scatter.scratch(digits, *shared_block)
        + Scatter.scratch(digits, *long_block)
        + Whole.scratch(digits, batches * pairs, 2 * FEAT)
        + Whole.scratch(digits, 16, width),
        compiler_params=pltpu.CompilerParams(
            collective_id=1, has_side_effects=True, vmem_limit_bytes=VMEM_LIMIT
        ),
        name="attention_backward",
    )(
        cuts, inputs, ga, gr, kf, qf, v, ks, qs, n, sd, small, ffn, wo_grad, vec_in, bias_in,
        jnp.stack([first_gain, first_shift]), wqkv, back,
    )

    per_row = 4 * width // shared_block[1]
    shared = shared.reshape(width // 16, per_row, 16, shared_block[1])
    shared = jnp.swapaxes(shared, 1, 2).reshape(width, 4, width).astype(F32)
    return (
        output,
        in_grad,
        vectors[0],
        vectors[1],
        shared[:, 0],
        shared[:, 1],
        shared[:, 2],
        shared[:, 3],
        vectors[2],
        vectors[3],
        vectors[4],
        ffn_grad[:deep],
        vectors[6 : 6 + hidden // width].reshape(hidden),
        ffn_grad[deep:].T,
        vectors[5],
    )


def solution(mesh):
    rows = P(None, ("seq", "ffn"), None)
    up, down = P("seq", "ffn"), P("ffn", "seq")
    in_specs = (rows, rows) + (P(),) * 10 + (up, P(), down, P(), rows)
    out_specs = (rows, rows) + (P(),) * 9 + (up, P(), down, P())
    return jax.shard_map(body, mesh=mesh, in_specs=in_specs, out_specs=out_specs, check_vma=False)
```

```python
import functools
import math

import jax
import jax.numpy as jnp
from jax import lax
from jax.experimental import pallas as pl
from jax.experimental.pallas import tpu as pltpu
from jax.sharding import PartitionSpec as P

BF, F32 = jnp.bfloat16, jnp.float32
EPS = 1e-5
LONG = 64
TILE = 256
PAIR = 128
AHEAD = 3
CHUNKS = 2
FEAT = 256
VMEM_LIMIT = 63 << 20
LOG16 = math.log(16.0)


def dot(a, b):
    return jnp.dot(a, b, preferred_element_type=F32)


def dot_nt(a, b):
    return lax.dot_general(a, b, (((1,), (1,)), ((), ())), preferred_element_type=F32)


def dot_tn(a, b):
    return lax.dot_general(a, b, (((0,), (0,)), ((), ())), preferred_element_type=F32)


def iota(shape, dim):
    return lax.broadcasted_iota(jnp.int32, shape, dim)


def normalize(rows):
    mean = jnp.mean(rows, axis=-1, keepdims=True)
    centred = rows - mean
    spread = jnp.mean(centred * centred, axis=-1, keepdims=True)
    scale = lax.rsqrt(spread + EPS)
    return centred * scale, scale


def norm_back(grad, xhat, scale):
    return scale * (
        grad
        - jnp.mean(grad, axis=-1, keepdims=True)
        - xhat * jnp.mean(grad * xhat, axis=-1, keepdims=True)
    )


def head_sums(pair):
    first = iota(pair.shape, 1) < PAIR // 2
    zero = jnp.zeros_like(pair)
    return (
        jnp.sum(jnp.where(first, pair, zero), axis=-1, keepdims=True),
        jnp.sum(jnp.where(first, zero, pair), axis=-1, keepdims=True),
    )


def features(scaled, scaled_low, proj, pair):
    cols = slice(pair * PAIR, (pair + 1) * PAIR)
    part = scaled[:, cols]
    first, second = head_sums(part * part)
    product = dot(scaled_low[:, cols], proj[pair])
    return jnp.concatenate(
        [
            jnp.exp(product[:, :FEAT] - (0.5 * first + LOG16)).astype(BF),
            jnp.exp(product[:, FEAT:] - (0.5 * second + LOG16)).astype(BF),
        ],
        axis=1,
    )


def lane_half(shape):
    return iota(shape, 1) < FEAT


def block_sums(both, norm):
    keep = (iota((PAIR, 2 * FEAT), 0) < PAIR // 2) == lane_half((PAIR, 2 * FEAT))
    zero = jnp.zeros((PAIR, 2 * FEAT), F32)
    return jnp.concatenate(
        [
            jnp.where(keep, both, zero).astype(BF),
            jnp.where(keep, jnp.broadcast_to(norm, (PAIR, 2 * FEAT)), zero).astype(BF),
        ],
        axis=0,
    )


def block_grads(both, norm):
    keep = (iota((PAIR, 2 * FEAT), 0) < PAIR // 2) == lane_half((PAIR, 2 * FEAT))
    zero = jnp.zeros((PAIR, 2 * FEAT), F32)
    row = iota((PAIR, 2 * FEAT), 0)
    high = norm.astype(BF).astype(F32)
    wide = jnp.broadcast_to(high, (PAIR, 2 * FEAT))
    rest = jnp.broadcast_to(norm - high, (PAIR, 2 * FEAT))
    return jnp.concatenate(
        [
            jnp.where(keep, both, zero).astype(BF),
            jnp.where(row == 0, wide, jnp.where(row == 1, rest, zero)).astype(BF),
        ],
        axis=0,
    )


def pack_pair(both):
    return jnp.where(lane_half((PAIR // 2, 2 * FEAT)), both[: PAIR // 2], both[PAIR // 2 :])


def norm_rows(both):
    return jnp.where(
        lane_half((1, 2 * FEAT)),
        jnp.sum(both[PAIR : PAIR + PAIR // 2], axis=0, keepdims=True),
        jnp.sum(both[PAIR + PAIR // 2 :], axis=0, keepdims=True),
    )


def unpack_pair(packed):
    return jnp.concatenate([packed, packed], axis=0)


def value_block(values, cols):
    part = values[:, cols]
    first = iota(part.shape, 1) < PAIR // 2
    zero = jnp.zeros_like(part)
    one = jnp.ones_like(part)
    top = jnp.concatenate([jnp.where(first, part, zero), jnp.where(first, one, zero)], axis=1)
    low = jnp.concatenate([jnp.where(first, zero, part), jnp.where(first, zero, one)], axis=1)
    return jnp.concatenate([top, low], axis=0)


def same_small(bounds):
    shape = (2 * LONG, 2 * LONG)

    def label(dim):
        at = iota(shape, dim)
        cut = jnp.where(at < LONG, bounds[0], LONG + bounds[1])
        return jnp.where(at < cut, 1, 0) + jnp.where(at < LONG, 0, 2)

    return label(0) == label(1)


def cuts_of(lens, big):
    cuts, bounds = [], []
    for batch in range(2):
        first, second = lens[batch, 0], lens[batch, 1]
        behind = jnp.where(second == big, first, first + second)
        cuts.append(jnp.where(first == big, 0, behind))
        bounds.append(jnp.where(first == big, second, first))
    return cuts, bounds


def swap_rows(buffer, cuts):
    most = buffer.shape[1]
    width = buffer.shape[2]
    for batch in range(2):
        head = buffer[batch, LONG : 2 * LONG]
        tail = buffer[batch, most - LONG :]
        small_first = iota((LONG, width), 0) < cuts[batch]
        buffer[batch, LONG : 2 * LONG] = jnp.where(small_first, tail, head)
        buffer[batch, most - LONG :] = jnp.where(small_first, head, tail)


def edge_rows(buffer):
    most = buffer.shape[1]
    return jnp.concatenate(
        [
            buffer[0, :LONG],
            buffer[1, :LONG],
            buffer[0, most - LONG :],
            buffer[1, most - LONG :],
        ],
        axis=0,
    )


def store_edge(buffer, value):
    most = buffer.shape[1]
    buffer[0, :LONG] = value[:LONG]
    buffer[1, :LONG] = value[LONG : 2 * LONG]
    buffer[0, most - LONG :] = value[2 * LONG : 3 * LONG]
    buffer[1, most - LONG :] = value[3 * LONG :]


def digits_of(size):
    out = []
    while size > 1:
        step = 4 if size % 4 == 0 else size
        out.append(step)
        size //= step
    return tuple(out)


class Net:
    def __init__(self, digits, send, recv):
        self.digits = digits
        self.send, self.recv = send, recv
        self.me = lax.axis_index("seq")
        self.core = lax.axis_index("ffn")
        self.slots = {}
        strides = [math.prod(digits[k + 1 :]) for k in range(len(digits))]
        self.own = [lax.rem(lax.div(self.me, s), n) for s, n in zip(strides, digits)]
        self.strides = strides

    def partner(self):
        return (self.me, 1 - self.core)

    def other(self, k, step):
        return lax.rem(self.own[k] + step, self.digits[k])

    def peer(self, k, step):
        return (self.me + (self.other(k, step) - self.own[k]) * self.strides[k], self.core)

    def greet(self):
        semaphore = pltpu.get_barrier_semaphore()
        peers = [self.partner()] + [
            self.peer(k, step) for k, n in enumerate(self.digits) for step in range(1, n)
        ]
        for peer in peers:
            pl.semaphore_signal(
                semaphore, inc=1, device_id=peer, device_id_type=pl.DeviceIdType.MESH
            )

    def meet(self):
        pl.semaphore_wait(
            pltpu.get_barrier_semaphore(), 1 + sum(n - 1 for n in self.digits)
        )

    def copy(self, key, source, target, device):
        slot = self.slots.setdefault(key, len(self.slots))
        return pltpu.make_async_remote_copy(
            src_ref=source,
            dst_ref=target,
            send_sem=self.send.at[slot],
            recv_sem=self.recv.at[slot],
            device_id=device,
            device_id_type=pl.DeviceIdType.MESH,
        )

    def group(self, key, size):
        return self.copy(key, size, size, self.partner())


def groups(depth, gathers, others):
    return gathers * (depth + 1) * (depth + 2) // 2 + others * (depth + 1)


class Gather:
    def __init__(self, net, name, out):
        self.net, self.name, self.out = net, name, out

    def fresh(self, j):
        net = self.net
        if j == 0:
            return [(net.core,) + tuple(net.own)]
        lead = (net.core,) + (slice(None),) * (j - 1)
        return [
            lead + (net.other(j - 1, step),) + tuple(net.own[j:])
            for step in range(1, net.digits[j - 1])
        ]

    def copies(self, j, k):
        net = self.net
        depth = len(net.digits)
        copies = []
        for at in self.fresh(j):
            block = self.out.at[at]
            if k == depth:
                copies.append(net.copy((self.name, j, k), block, block, net.partner()))
                continue
            for step in range(1, net.digits[k]):
                copies.append(net.copy((self.name, j, k), block, block, net.peer(k, step)))
        return copies

    def group(self, j, k):
        digits = self.net.digits
        at = [0] * (1 + len(digits))
        if j:
            at[1:j] = [slice(None)] * (j - 1)
            at[j] = pl.ds(0, digits[j - 1] - 1)
        if k < len(digits):
            at[1 + k] = pl.ds(0, digits[k] - 1)
        return self.net.group((self.name, j, k), self.out.at[tuple(at)])

    def steps(self):
        depth = len(self.net.digits)

        def run(j):
            for i in range(j):
                self.group(i, j - 1).wait_recv()
            for k in range(j, depth + 1):
                for copy in self.copies(j, k):
                    copy.start()

        def last():
            for j in range(depth + 1):
                self.group(j, depth).wait_recv()

        return [functools.partial(run, j) for j in range(depth + 1)] + [last]

    def drain(self):
        depth = len(self.net.digits)
        for j in range(depth + 1):
            for k in range(j, depth + 1):
                self.group(j, k).wait_send()


class Scatter:
    def __init__(self, net, name, blocks, first, slots, parts, finish, apart=None):
        self.net, self.name = net, name
        self.away = (blocks if apart is None else apart).at[1 - net.core]
        self.held = blocks.at[net.core] if apart is None else blocks
        self.first, self.slots, self.parts, self.finish = first, slots, parts, finish

    @staticmethod
    def scratch(digits, rows, cols):
        shapes = [pltpu.VMEM(digits + (rows, cols), BF)]
        for k in reversed(range(len(digits))):
            shapes.append(pltpu.VMEM((digits[k] - 1,) + digits[:k] + (rows, cols), BF))
        for k in reversed(range(1, len(digits))):
            shapes.append(pltpu.VMEM(digits[:k] + (rows, cols), BF))
        return shapes

    @classmethod
    def of(cls, net, name, blocks, refs, finish, apart=None):
        depth = len(net.digits)
        slots, parts = refs[1 : 1 + depth], refs[1 + depth :]
        return cls(net, name, blocks, refs[0], slots, parts, finish, apart)

    def copies(self, k):
        net = self.net
        depth = len(net.digits)
        if k == 0:
            return [net.copy((self.name, 0), self.away, self.first, net.partner())]
        digit = depth - k
        held = self.held if k == 1 else self.parts[k - 2]
        copies = []
        for step in range(1, net.digits[digit]):
            at = (slice(None),) * digit + (net.other(digit, step),)
            copies.append(
                net.copy(
                    (self.name, k),
                    held.at[at],
                    self.slots[k - 1].at[step - 1],
                    net.peer(digit, step),
                )
            )
        return copies

    def group(self, k):
        return self.net.group((self.name, k), self.slots[k - 1] if k else self.first)

    def add(self, k):
        net = self.net
        depth = len(net.digits)
        if k == 0:
            lead = net.digits
            for at in _indices(lead):
                mine = self.held[at].astype(F32)
                self.held[at] = (mine + self.first[at].astype(F32)).astype(BF)
            return
        digit = depth - k
        held = self.held if k == 1 else self.parts[k - 2]
        for at in _indices(net.digits[:digit]):
            total = held[at + (net.own[digit],)].astype(F32)
            for step in range(net.digits[digit] - 1):
                total = total + self.slots[k - 1][(step,) + at].astype(F32)
            if digit:
                self.parts[k - 1][at] = total.astype(BF)
            else:
                self.finish(total)

    def steps(self):
        depth = len(self.net.digits)

        def start(k):
            for copy in self.copies(k):
                copy.start()

        def follow(k):
            self.group(k - 1).wait_recv()
            self.add(k - 1)
            if k <= depth:
                start(k)

        return [functools.partial(start, 0)] + [
            functools.partial(follow, k) for k in range(1, depth + 2)
        ]

    def drain(self):
        for k in range(len(self.net.digits) + 1):
            self.group(k).wait_send()


def _indices(lead):
    if not lead:
        return [()]
    return [(i,) + rest for i in range(lead[0]) for rest in _indices(lead[1:])]


class Whole:
    def __init__(self, net, name, held, slots):
        self.net, self.name, self.held, self.slots = net, name, held, slots

    @staticmethod
    def scratch(digits, rows, cols):
        return [
            pltpu.VMEM((len(digits) + 2, rows, cols), F32),
            pltpu.VMEM((1 + sum(n - 1 for n in digits), rows, cols), F32),
        ]

    def span(self, k):
        digits = self.net.digits
        return (0, 1) if k == 0 else (1 + sum(n - 1 for n in digits[: k - 1]), digits[k - 1] - 1)

    def copies(self, k):
        net = self.net
        source = self.held.at[k]
        first, number = self.span(k)
        peers = [net.partner()] if k == 0 else [net.peer(k - 1, 1 + i) for i in range(number)]
        return [
            net.copy((self.name, k), source, self.slots.at[first + i], peer)
            for i, peer in enumerate(peers)
        ]

    def group(self, k):
        return self.net.group((self.name, k), self.slots.at[pl.ds(*self.span(k))])

    def steps(self):
        depth = len(self.net.digits)

        def start(k):
            for copy in self.copies(k):
                copy.start()

        def follow(k):
            self.group(k - 1).wait_recv()
            total = self.held[k - 1]
            first, number = self.span(k - 1)
            for i in range(number):
                total = total + self.slots[first + i]
            self.held[k] = total
            if k <= depth:
                start(k)

        return [functools.partial(start, 0)] + [
            functools.partial(follow, k) for k in range(1, depth + 2)
        ]

    def drain(self):
        for k in range(len(self.net.digits) + 1):
            self.group(k).wait_send()


def together(*parts):
    most = max(len(part) for part in parts)

    def run(i):
        for part in parts:
            if i < len(part):
                part[i]()

    return [functools.partial(run, i) for i in range(most)]


def block_shape(ways, rows, cols):
    lanes = cols * (rows // 16) // ways
    return 16, lanes


def block_at(digits, index):
    at = []
    for n in reversed(digits):
        at.append(index % n)
        index //= n
    return tuple(reversed(at))


def store_blocks(blocks, row, value):
    lanes = blocks.shape[-1]
    per_row = value.shape[1] // lanes
    ways = (2,) + blocks.shape[1:-2]
    for i in range(value.shape[0] // 16):
        for j in range(per_row):
            at = block_at(ways, (row // 16 + i) * per_row + j)
            blocks[at] = value[16 * i : 16 * i + 16, j * lanes : (j + 1) * lanes]


def load_blocks(blocks, row, rows, cols):
    lanes = blocks.shape[-1]
    per_row = cols // lanes
    ways = (2,) + blocks.shape[1:-2]
    out = []
    for i in range(rows // 16):
        line = [
            blocks[block_at(ways, (row // 16 + i) * per_row + j)] for j in range(per_row)
        ]
        out.append(line[0] if per_row == 1 else jnp.concatenate(line, axis=1))
    return jnp.concatenate(out, axis=0)


class Loads:
    def __init__(self, semaphores):
        self.semaphores = semaphores
        self.count = 0

    def start(self, source, target):
        copy = pltpu.make_async_copy(source, target, self.semaphores.at[self.count])
        self.count += 1
        copy.start()
        return copy


PIECES = ((0, 128), (1088, 64), (128, 192), (320, 256), (576, 256), (832, 256))


def raw_pieces(rows):
    quarter = (rows - 2 * LONG) // 4
    pieces = [(0, 2 * LONG), (rows - LONG, LONG), (2 * LONG, quarter - LONG)]
    return pieces + [(LONG + quarter * i, quarter) for i in range(1, 4)]


def big_start(batch, rows_big, step, tile):
    return TILE + batch * rows_big + step * tile


def pair_projection(projection, pair):
    first, second = projection[2 * pair], projection[2 * pair + 1]
    gap = jnp.zeros_like(first)
    return jnp.concatenate(
        [jnp.concatenate([first, gap], axis=1), jnp.concatenate([gap, second], axis=1)], axis=0
    )


def place(steps, spots, count):
    lists = [[] for _ in range(count)]
    for step, spot in zip(steps, spots, strict=True):
        lists[spot].append(step)
    return lists


def spots(known, number):
    if number == len(known):
        return list(known)
    last = len(known) - 1
    return [known[min(last, -(-i * last // max(1, number - 1)))] for i in range(number)]


def side_by_side(chains):
    most = max(len(chain) for chain in chains)
    return [
        chain[i - most] for i in range(most) for chain in chains if i >= most - len(chain)
    ]


def talk(lists, t):
    for i, steps in enumerate(lists):
        if steps:
            pl.when(t == i)(functools.partial(_all, steps))


def _all(steps):
    for step in steps:
        step()


def all_reduce(scatter, spread):
    first, second = scatter.steps(), spread.steps()
    return first[:-1] + [functools.partial(_both, first[-1], second[0])] + second[1:]


def weight_block(up, down, chunk):
    half = up.shape[1] // CHUNKS
    at = slice(chunk * half, (chunk + 1) * half)
    return jnp.concatenate([up[:, at], down[:, at]], axis=0).astype(BF)


def attention_forward(
    digits, lens, x_hbm, gain, shift, bias, wq_hbm, wk_hbm, wv_hbm, wo_hbm, projection, up, down,
    k_out, q_out, v_out, ks_out, qs_out, n_out, mix_out, inv_out, att_out, sd_out, small_out,
    wqkv_out, wo_out, w_out,
    x, kf, qf, v, ks, qs, n, mix, inv, att, sd, small, wqkv, wo, proj, block, acc, nacc, parts,
    total, load_sem, store_sem, own_sem, send, recv, whole_held, whole_slots, *slots,
):
    rows = x.shape[1]
    big = rows - 2 * LONG
    pairs = proj.shape[0]
    width = wo.shape[0]
    scale = (PAIR // 2) ** -0.25
    depth = len(digits)
    net = Net(digits, send, recv)
    loads = Loads(load_sem)
    pieces = raw_pieces(rows)
    pending = {}

    def load_rows(some):
        for piece in some:
            for batch in range(2):
                span = pl.ds(*piece)
                pending[batch, piece] = loads.start(x_hbm.at[batch, span], x.at[batch, span])

    load_rows(pieces[:2])
    weights = [
        loads.start(source, att.at[pl.ds(i * width, width)])
        for i, source in enumerate((wq_hbm, wk_hbm, wv_hbm, wo_hbm))
    ]
    net.greet()
    block[...] = weight_block(up, down, 0)
    own_block = pltpu.make_async_copy(block, w_out.at[(net.core,) + tuple(net.own)], own_sem)
    own_block.start()
    for pair in range(pairs):
        proj[pair] = pair_projection(projection, pair).astype(BF)
    own_block.wait()
    net.meet()
    gather = Gather(net, "w", w_out)
    gather_steps = gather.steps()
    gather_steps[0]()

    def finish(value):
        total[(net.core,) + tuple(net.own)] = value.astype(BF)

    scatter = Scatter.of(net, "s", parts, slots, finish)
    spread = Gather(net, "t", total)
    whole = Whole(net, "n", whole_held, whole_slots)
    sum_steps = together(all_reduce(scatter, spread), whole.steps())
    cuts, bounds = cuts_of(lens, big)
    for i, copy in enumerate(weights):
        copy.wait()
        rounded = att[i * width : (i + 1) * width].astype(BF)
        if i < 3:
            wqkv[:, i * width : (i + 1) * width] = rounded
        else:
            wo[...] = rounded

    def front(rows_x, tile):
        xhat, _ = normalize(rows_x)
        low = (xhat * gain[...] + shift[...]).astype(BF)
        n[tile] = low.T
        raw = dot(low, wqkv[...])
        q = raw[:, :width] * scale
        k = raw[:, width : 2 * width] * scale
        return q, k, raw[:, 2 * width :].astype(BF)

    def attend(numer_denom, at, pair):
        cols = slice(pair * PAIR, (pair + 1) * PAIR)
        inverse = 1.0 / numer_denom[:, PAIR:]
        inv[at, cols] = inverse
        mix[at, cols] = (numer_denom[:, :PAIR] * inverse).astype(BF)

    load_rows(pieces[2:])
    for piece in pieces[:2]:
        for batch in range(2):
            pending[batch, piece].wait()
    swap_rows(x, cuts)
    edge = slice(0, TILE)
    q, k, values = front(edge_rows(x), 0)
    v[edge] = values
    k_low = k.astype(BF)
    ks[edge] = k_low
    for pair in range(pairs):
        cols = slice(pair * PAIR, (pair + 1) * PAIR)
        feats = slice(pair * 2 * FEAT, (pair + 1) * 2 * FEAT)
        mapped = features(k, k_low, proj, pair)
        kf[edge, feats] = mapped
        for batch in range(2):
            own = slice(batch * LONG, (batch + 1) * LONG)
            both = dot_tn(values[own, cols], mapped[own])
            row = batch * pairs + pair
            store_blocks(parts, row * LONG, pack_pair(both).astype(BF))
            whole_held[0, row : row + 1] = jnp.sum(mapped[own].astype(F32), axis=0, keepdims=True)
    sum_steps[0]()
    q_low = q.astype(BF)
    qs[edge] = q_low
    same = same_small(bounds)
    shorts = slice(2 * LONG, TILE)
    for pair in range(pairs):
        cols = slice(pair * PAIR, (pair + 1) * PAIR)
        feats = slice(pair * 2 * FEAT, (pair + 1) * 2 * FEAT)
        mapped = features(q, q_low, proj, pair)
        qf[edge, feats] = mapped
        scores = []
        for head in range(2):
            lanes = slice((2 * pair + head) * FEAT, (2 * pair + head + 1) * FEAT)
            score = dot_nt(
                mapped[shorts, head * FEAT : (head + 1) * FEAT], kf[shorts, lanes]
            )
            score = jnp.where(same, score, 0.0).astype(BF)
            small[2 * pair + head] = score
            scores.append(score)
        attend(
            dot(jnp.concatenate(scores, axis=1), value_block(values[shorts], cols)), shorts, pair
        )

    def store(source, target, at, slot):
        pltpu.make_async_copy(source.at[at], target.at[at], store_sem.at[slot]).start()

    first_pass = ((kf, k_out), (qf, q_out), (v, v_out), (ks, ks_out), (qs, qs_out), (n, n_out))
    second_pass = ((mix, mix_out), (inv, inv_out), (att, att_out))
    once = ((small, small_out), (wqkv, wqkv_out), (wo, wo_out), (sd, sd_out))

    def store_first(at, tile):
        for slot, (source, target) in enumerate(first_pass):
            store(source, target, tile if source is n else at, slot)

    def store_second(at):
        for slot, (source, target) in enumerate(second_pass):
            store(source, target, at, len(first_pass) + slot)

    def whole_copy(i):
        slot = len(first_pass) + len(second_pass) + i
        return pltpu.make_async_copy(*once[i], store_sem.at[slot])

    store_first(pl.ds(0, TILE), 0)
    for i in range(3):
        whole_copy(i).start()
    for piece in pieces[2:]:
        for batch in range(2):
            pending[batch, piece].wait()
    acc[...] = jnp.zeros_like(acc)
    nacc[...] = jnp.zeros_like(nacc)
    per = big // TILE
    count = 2 * per
    comm = place(
        sum_steps[1:] + gather_steps[1:],
        spots((1, 3, 5, 7, count + 2, count + 6), len(sum_steps) - 1)
        + spots((3, count, count + 4), len(gather_steps) - 1),
        2 * count,
    )

    def pass_one(t, _):
        batch, step = lax.div(t, per), lax.rem(t, per)
        talk(comm[:count], t)
        raw_at = pl.ds(pl.multiple_of(LONG + step * TILE, LONG), TILE)
        at = pl.ds(pl.multiple_of(TILE + t * TILE, TILE), TILE)
        q, k, values = front(x[batch, raw_at], 1 + t)
        v[at] = values
        k_low = k.astype(BF)
        q_low = q.astype(BF)
        ks[at] = k_low
        qs[at] = q_low
        for pair in range(pairs):
            cols = slice(pair * PAIR, (pair + 1) * PAIR)
            feats = slice(pair * 2 * FEAT, (pair + 1) * 2 * FEAT)
            mapped = features(k, k_low, proj, pair)
            kf[at, feats] = mapped
            acc[batch, pair] += dot_tn(values[:, cols], mapped)
            nacc[batch, pair] += jnp.sum(mapped.astype(F32), axis=0, keepdims=True)
            qf[at, feats] = features(q, q_low, proj, pair)
        store_first(at, 1 + t)
        return 0

    lax.fori_loop(0, count, pass_one, 0)
    for batch in range(2):
        for pair in range(pairs):
            sd[batch, pair] = block_sums(acc[batch, pair], nacc[batch, pair])

    def pass_two(t, _):
        batch, step = lax.div(t, per), lax.rem(t, per)
        talk(comm[count:], t)
        raw_at = pl.ds(pl.multiple_of(LONG + step * TILE, LONG), TILE)
        at = pl.ds(pl.multiple_of(TILE + t * TILE, TILE), TILE)
        for pair in range(pairs):
            feats = slice(pair * 2 * FEAT, (pair + 1) * 2 * FEAT)
            attend(dot_nt(qf[at, feats], sd[batch, pair]), at, pair)
        att[at] = x[batch, raw_at] + dot(mix[at], wo[...]) + bias[...]
        store_second(at)
        return 0

    lax.fori_loop(0, count, pass_two, 0)
    for batch in range(2):
        own = slice(batch * LONG, (batch + 1) * LONG)
        for pair in range(pairs):
            feats = slice(pair * 2 * FEAT, (pair + 1) * 2 * FEAT)
            row = batch * pairs + pair
            packed = load_blocks(total, row * LONG, LONG, 2 * FEAT).astype(F32)
            sd[2 + batch, pair] = block_sums(
                unpack_pair(packed), whole_held[depth + 1, row : row + 1]
            )
            attend(dot_nt(qf[own, feats], sd[2 + batch, pair]), own, pair)
    att[edge] = edge_rows(x) + dot(mix[edge], wo[...]) + bias[...]
    store_second(pl.ds(0, TILE))
    whole_copy(3).start()
    for slot, (source, target) in enumerate(first_pass + second_pass):
        pltpu.make_async_copy(source, target, store_sem.at[slot]).wait()
    for i in range(len(once)):
        whole_copy(i).wait()
    gather.drain()
    scatter.drain()
    spread.drain()
    whole.drain()


def _both(first, second):
    first()
    second()


def feed_forward(
    digits, lens, cot_hbm, att_hbm, mix_hbm, inv_hbm, w_hbm, wo, gain, shift, up_bias,
    up_own, down_own, q_hbm,
    out_hbm, ga_out, g_out, x_out, ffn_out, wo_grad, vec_grad, bias_grad, long_out, norm_out,
    cot, att, mix, inv, second, branch, grad_second, w_first, w_second, up, down, dup, ddown,
    gr_edge, gr, qf, parts, long_total, load_sem, store_sem, send, recv, *refs,
):
    rows = cot.shape[1]
    big = rows - 2 * LONG
    width = wo.shape[0]
    pairs = width // PAIR
    tile = big // 2
    per = big // tile
    count = 2 * per
    depth = len(digits)
    cuts, _ = cuts_of(lens, big)
    net = Net(digits, send, recv)
    net.greet()
    loads = Loads(load_sem)
    deep = w_first.shape[-2] // 2
    half = w_first.shape[-1]
    wait_w = loads.start(w_hbm, w_first)
    pieces = raw_pieces(rows)
    inner = [(0, TILE)] + [(TILE + tile * i, tile) for i in range(count)]

    def load_cot(some):
        return [
            loads.start(cot_hbm.at[batch, pl.ds(*piece)], cot.at[batch, pl.ds(*piece)])
            for piece in some
            for batch in range(2)
        ]

    def load_inner(source, target, some):
        return [loads.start(source.at[pl.ds(*p)], target.at[pl.ds(*p)]) for p in some]

    first_waits = load_inner(att_hbm, att, inner[:1]) + load_cot(pieces[:2])
    w_second[(net.core,) + tuple(net.own)] = weight_block(up_own, down_own, 1)
    net.meet()
    gather = Gather(net, "w", w_second)
    gather_steps = gather.steps()
    gather_steps[0]()

    def finish(value):
        ffn_out[...] = value

    scatter = Scatter.of(net, "f", w_first, refs[: 2 * depth], finish)
    scatter_steps = scatter.steps()

    def finish_long(value):
        long_total[(net.core,) + tuple(net.own)] = value.astype(BF)

    long_scatter = Scatter.of(net, "s", parts, refs[2 * depth : 4 * depth], finish_long)
    long_spread = Gather(net, "t", long_total)
    norm_held, norm_slots = refs[4 * depth :]
    norm_sum = Whole(net, "n", norm_held, norm_slots)
    long_steps = together(all_reduce(long_scatter, long_spread), norm_sum.steps())
    members = _indices(digits)
    group = max(1, 16 // deep)

    def unpack(w):
        for core in range(2):
            cols = slice(core * half, (core + 1) * half)
            for first in range(0, len(members), group):
                parts = [w[(core,) + members[first + i]] for i in range(group)]
                at = slice(first * deep, (first + group) * deep)
                if group == 1:
                    up[at, cols] = parts[0][:deep]
                    down[at, cols] = parts[0][deep:]
                else:
                    up[at, cols] = jnp.concatenate([part[:deep] for part in parts], axis=0)
                    down[at, cols] = jnp.concatenate([part[deep:] for part in parts], axis=0)

    def pack(w):
        for core in range(2):
            cols = slice(core * half, (core + 1) * half)
            for i, member in enumerate(members):
                at = slice(i * deep, (i + 1) * deep)
                w[(core,) + member] = jnp.concatenate(
                    [dup[at, cols], ddown[at, cols]], axis=0
                ).astype(BF)

    def bias_lanes(chunk):
        return [
            slice((CHUNKS * core + chunk) * half, (CHUNKS * core + chunk + 1) * half)
            for core in range(2)
        ]

    def add_row(at, value):
        vec_grad[at : at + 1] += jnp.sum(value, axis=0, keepdims=True)

    def hidden_part(chunk, second_low, grad_low):
        bias = jnp.concatenate([up_bias[:, lanes] for lanes in bias_lanes(chunk)], axis=1)
        hidden = dot(second_low, up[...]) + bias
        gauss = jnp.exp(-0.5 * hidden * hidden) * (1.0 / math.sqrt(2.0 * math.pi))
        cdf = 0.5 + 0.5 * lax.erf(hidden * math.sqrt(0.5))
        active = (hidden * cdf).astype(BF)
        slope = cdf + hidden * gauss
        grad_hidden = (dot(grad_low, down[...]) * slope).astype(BF)
        dup[...] += dot(second_low.T, grad_hidden)
        ddown[...] += dot(grad_low.T, active)
        bias_sum = jnp.sum(grad_hidden.astype(F32), axis=0, keepdims=True)
        for core, lanes in enumerate(bias_lanes(chunk)):
            bias_grad[:, lanes] += bias_sum[:, core * half : (core + 1) * half]
        return dot_nt(active, down[...]), dot_nt(grad_hidden, up[...])

    def first_block(at, grad_out):
        xhat, _ = normalize(att[at])
        low = (xhat * gain[...] + shift[...]).astype(BF)
        second[at] = low
        branch[at], grad_second[at] = hidden_part(0, low, grad_out.astype(BF))

    def second_block(at, grad_out, put, between=lambda: None):
        more, grad_more = hidden_part(1, second[at], grad_out.astype(BF))
        between()
        att_rows = att[at]
        xhat, scale = normalize(att_rows)
        output = att_rows + (branch[at] + more)
        grad = grad_second[at] + grad_more
        grad_att = grad_out + norm_back(grad * gain[...], xhat, scale)
        add_row(2, grad_att)
        add_row(3, grad * xhat)
        add_row(4, grad)
        add_row(5, grad_out)
        grad_att_low = grad_att.astype(BF)
        mixed = mix[at]
        wo_grad[...] += dot_tn(mixed, grad_att_low)
        grad_mixed = dot_nt(grad_att_low, wo[...]).astype(BF).astype(F32)
        for pair in range(pairs):
            cols = slice(pair * PAIR, (pair + 1) * PAIR)
            part = grad_mixed[:, cols]
            inverse = inv[at, cols]
            first, last = head_sums(part * mixed[:, cols].astype(F32))
            lane = iota(part.shape, 1)
            grad_denom = -jnp.where(lane < PAIR // 2, first, last) * inverse
            high = grad_denom.astype(BF).astype(F32)
            both = jnp.where(lane % (PAIR // 2) < PAIR // 4, high, grad_denom - high)
            put(2 * pair, (part * inverse).astype(BF))
            put(2 * pair + 1, (both * (4.0 / PAIR)).astype(BF))
        att[at] = grad_att
        return output

    def lanes_of(i):
        return slice(i * PAIR, (i + 1) * PAIR)

    def store_g(t):
        slot = lax.rem(t, 2)
        at = pl.ds(pl.multiple_of(TILE + t * tile, TILE), tile)
        return pltpu.make_async_copy(gr.at[slot], g_out.at[at], store_sem.at[slot])

    def store_att(at):
        pltpu.make_async_copy(att.at[at], ga_out.at[at], store_sem.at[2]).start()

    def rows_at(t):
        batch, step = lax.div(t, per), lax.rem(t, per)
        raw_at = pl.ds(pl.multiple_of(LONG + step * tile, LONG), tile)
        return batch, raw_at, pl.ds(pl.multiple_of(TILE + t * tile, TILE), tile)

    for ref in (dup, ddown, wo_grad, vec_grad, bias_grad):
        ref[...] = jnp.zeros_like(ref)
    wait_w.wait()
    for copy in first_waits:
        copy.wait()
    next_waits = load_inner(att_hbm, att, inner[1:]) + load_cot(pieces[2:])
    unpack(w_first)
    edge = pl.ds(0, TILE)
    swap_rows(cot, cuts)
    first_block(edge, edge_rows(cot))
    for copy in next_waits:
        copy.wait()
    last_waits = [loads.start(q_hbm.at[pl.ds(0, 2 * LONG)], qf)]
    for some in (inner[:1], inner[1:]):
        last_waits += load_inner(mix_hbm, mix, some) + load_inner(inv_hbm, inv, some)
    gather_at = place(gather_steps[1:], spots((1, 3, count), len(gather_steps) - 1), count + 1)

    def first_pass(t, _):
        talk(gather_at[:count], t)
        batch, raw_at, at = rows_at(t)
        first_block(at, cot[batch, raw_at])
        return 0

    lax.fori_loop(0, count, first_pass, 0)
    _all(gather_at[count])
    pack(w_first)
    scatter_steps[0]()
    unpack(w_second)
    dup[...] = jnp.zeros_like(dup)
    ddown[...] = jnp.zeros_like(ddown)
    for copy in last_waits:
        copy.wait()

    def put_edge(i, value):
        gr_edge[:, lanes_of(i)] = value

    store_edge(cot, second_block(edge, edge_rows(cot), put_edge))
    store_att(edge)
    edge_copy = pltpu.make_async_copy(gr_edge, g_out.at[edge], store_sem.at[3])
    edge_copy.start()
    for batch in range(2):
        own = slice(batch * LONG, (batch + 1) * LONG)
        for pair in range(pairs):
            grads = gr_edge[own, 2 * pair * PAIR : (2 * pair + 2) * PAIR]
            both = dot_tn(grads, qf[own, 2 * pair * FEAT : (2 * pair + 2) * FEAT])
            row = batch * pairs + pair
            store_blocks(parts, row * LONG, pack_pair(both[:PAIR]).astype(BF))
            norm_held[0, row : row + 1] = norm_rows(both)
    long_steps[0]()
    scatter_at = place(
        scatter_steps[1:] + long_steps[1:],
        spots((0, 5, 2 * count), len(scatter_steps) - 1)
        + spots((0, 2, 3, 5, 6, 2 * count), len(long_steps) - 1),
        2 * count + 1,
    )

    def second_pass(t, _):
        talk(scatter_at[: 2 * count : 2], t)
        batch, raw_at, at = rows_at(t)

        @pl.when(t >= 2)
        def _():
            store_g(t - 2).wait()

        def put(i, value):
            gr[lax.rem(t, 2), :, lanes_of(i)] = value

        cot[batch, raw_at] = second_block(
            at, cot[batch, raw_at], put, functools.partial(talk, scatter_at[1 : 2 * count : 2], t)
        )
        store_att(at)
        store_g(t).start()
        return 0

    lax.fori_loop(0, count, second_pass, 0)
    swap_rows(cot, cuts)
    out_copy = pltpu.make_async_copy(cot, out_hbm, store_sem.at[4])
    out_copy.start()
    gather.drain()
    pack(w_second)
    x_copy = pltpu.make_async_copy(w_second, x_out, store_sem.at[5])
    x_copy.start()
    _all(scatter_at[2 * count])
    long_out[...] = long_total[...]
    norm_out[...] = norm_held[depth + 1]
    store_g(count - 2).wait()
    store_g(count - 1).wait()
    pltpu.make_async_copy(att, ga_out, store_sem.at[2]).wait()
    edge_copy.wait()
    out_copy.wait()
    x_copy.wait()
    for item in (scatter, long_scatter, long_spread, norm_sum):
        item.drain()


def attention_backward(
    digits, lens, x_hbm, ga_hbm, g_hbm, k_hbm, q_hbm, v_hbm, ks_hbm, qs_hbm, n_hbm,
    sd_hbm, small, ffn_hbm, wo_grad, vec_in, bias_in, long_total, long_norm, gain, wqkv,
    projection,
    in_grad, ffn_out, out_out, query_out, key_out, value_out, vec_out,
    kf, v, ks, qs, n, sd, sg, back, ffn, out_x, out_total, query_x, query_total, key_x, key_total,
    value_x, value_total, load_sem, tile_sem, key_sem, store_sem, send, recv, *refs,
):
    rows = x_hbm.shape[1]
    big = rows - 2 * LONG
    pairs = back.shape[0]
    width = wqkv.shape[0]
    inner_rows = kf.shape[0]
    scale = (PAIR // 2) ** -0.25
    depth = len(digits)
    net = Net(digits, send, recv)
    each = 2 * depth
    refs = list(refs)

    def take(number):
        taken, refs[:] = refs[:number], refs[number:]
        return taken

    loads = Loads(load_sem)
    per = big // TILE
    count = 2 * per
    shorts = slice(2 * LONG, TILE)
    edge = slice(0, TILE)
    cuts, bounds = cuts_of(lens, big)
    same = same_small(bounds)

    def finish_ffn(value):
        ffn_out[...] = value

    ffn_sum = Scatter.of(net, "f", ffn, take(each), finish_ffn, apart=ffn_hbm)

    def reduction(name, blocks, total):
        def finish(value):
            total[(net.core,) + tuple(net.own)] = value.astype(BF)

        return Scatter.of(net, name, blocks, take(each), finish), Gather(net, name + "t", total)

    out_sum = reduction("o", out_x, out_total)
    query_sum = reduction("q", query_x, query_total)
    key_sum = reduction("k", key_x, key_total)
    value_sum = reduction("l", value_x, value_total)
    vec_held, vec_slots = take(2)
    vec_sum = Whole(net, "v", vec_held, vec_slots)
    ffn_steps = ffn_sum.steps()
    out_steps = all_reduce(*out_sum)
    query_steps = all_reduce(*query_sum)
    key_steps = all_reduce(*key_sum)
    value_steps = all_reduce(*value_sum)
    vec_steps = vec_sum.steps()
    last_spot = 4 * count
    number = len(out_steps)
    chains = (
        (ffn_steps[1:], spots((0, 9, 18), len(ffn_steps) - 1)),
        (out_steps[1:], spots((0, 6, 9, 13, 18, 24), number - 1)),
        (query_steps, spots((8, 11, 16, 22, 28, 32, 32), number)),
        (key_steps, spots((16, 21, 28, 32, 32, 32, 32), number)),
        (value_steps, spots((24, 27, 32, 32, 32, 32, 32), number)),
    )
    comm = [[] for _ in range(last_spot)]
    ends = []
    for steps, at in chains:
        ends.append([step for step, spot in zip(steps, at, strict=True) if spot == last_spot])
        for step, spot in zip(steps, at, strict=True):
            if spot < last_spot:
                comm[spot].append(step)
    last_steps = side_by_side([end for end in ends if end] + [vec_steps[1:]])

    def feat_lanes(pair):
        return slice(pair * 2 * FEAT, (pair + 1) * 2 * FEAT)

    def pair_cols(pair):
        return slice(pair * PAIR, (pair + 1) * PAIR)

    def grad_lanes(pair):
        return slice(2 * pair * PAIR, (2 * pair + 2) * PAIR)

    def feature_back(grad, mapped, scaled, pair):
        term = (grad * mapped.astype(F32)).astype(BF)
        both = dot(term, back[pair])
        return (
            (both[:, :PAIR] - scaled[:, pair_cols(pair)].astype(F32) * both[:, PAIR:]) * scale
        ).astype(BF)

    def ones_beside(values):
        return jnp.concatenate([values, jnp.ones_like(values)], axis=1)

    def first_tile(tiled):
        waits = []
        for source, target, by_rows in tiled:
            at = pl.ds(0, TILE) if by_rows else pl.ds(0, 1)
            waits.append(loads.start(source.at[at], target.at[at]))
        return waits

    def tile_load(i, source, target, by_rows, t):
        if by_rows:
            at = pl.ds(pl.multiple_of(TILE + t * TILE, TILE), TILE)
        else:
            at = pl.ds(1 + t, 1)
        return pltpu.make_async_copy(source.at[at], target.at[at], tile_sem.at[i, t])

    def query_phase(qf, gr, acc, wgrad):
        query_side = [(g_hbm, gr, True), (q_hbm, qf, True), (qs_hbm, qs, True), (n_hbm, n, False)]
        key_side = [(k_hbm, kf, True), (v_hbm, v, True), (ks_hbm, ks, True)]
        net.greet()
        wait_edge = first_tile(query_side + key_side)
        wait_edge.append(loads.start(sd_hbm.at[pl.ds(2, 2)], sd.at[pl.ds(2, 2)]))
        wait_ffn = loads.start(ffn_hbm.at[net.core], ffn)
        wait_sd = loads.start(sd_hbm.at[pl.ds(0, 2)], sd.at[pl.ds(0, 2)])

        def start_tile(t):
            for i, item in enumerate(query_side):
                tile_load(i, *item, t).start()

        for i in range(width // 16):
            at = slice(16 * i, 16 * i + 16)
            store_blocks(out_x, 16 * i, wo_grad[at].astype(BF))
        net.meet()
        out_steps[0]()
        ffn_steps[0]()
        for pair in range(pairs):
            turned = pair_projection(projection, pair).T
            own = (iota(turned.shape, 0) < FEAT) == (iota(turned.shape, 1) < PAIR // 2)
            back[pair] = jnp.concatenate([turned, jnp.where(own, 1.0, 0.0)], axis=1).astype(BF)
        for copy in wait_edge:
            copy.wait()
        for t in range(AHEAD):
            start_tile(t)
        for pair in range(pairs):
            lanes, cols = feat_lanes(pair), pair_cols(pair)
            mapped_q, mapped_k = qf[edge, lanes], kf[shorts, lanes]
            grads, values = gr[edge, grad_lanes(pair)], v[shorts, cols]
            grad_q = [
                dot(grads[batch * LONG : (batch + 1) * LONG], sd[2 + batch, pair])
                for batch in range(2)
            ]
            weight = dot_nt(grads[shorts], value_block(values, slice(0, PAIR)))
            more_q, more_k, more_v = [], [], []
            for head in range(2):
                own = slice(head * FEAT, (head + 1) * FEAT)
                part = jnp.where(same, weight[:, head * PAIR : (head + 1) * PAIR], 0.0).astype(BF)
                more_q.append(dot(part, mapped_k[:, own]))
                more_k.append(dot_tn(part, mapped_q[shorts, own]))
                more_v.append(dot_tn(small[2 * pair + head], grads[shorts, :PAIR]))
            grad_q.append(jnp.concatenate(more_q, axis=1))
            grad_k = jnp.concatenate(more_k, axis=1)
            grad_v = jnp.where(iota((2 * LONG, PAIR), 1) < PAIR // 2, more_v[0], more_v[1])
            qs[edge, cols] = feature_back(
                jnp.concatenate(grad_q, axis=0), mapped_q, qs[edge], pair
            )
            ks[shorts, cols] = feature_back(grad_k, mapped_k, ks[shorts], pair)
            v[shorts, cols] = grad_v.astype(BF)
        wgrad[...] = dot(n[0], qs[edge])
        wait_ffn.wait()
        wait_sd.wait()

        def key_load(i):
            source, target, _ = key_side[i]
            at = pl.ds(TILE, 2 * big)
            return pltpu.make_async_copy(source.at[at], target.at[at], key_sem.at[i])

        def queries(t, _):
            batch, step = lax.div(t, per), lax.rem(t, per)
            talk(comm[:count], t)
            at = pl.ds(pl.multiple_of(TILE + t * TILE, TILE), TILE)
            for i, item in enumerate(query_side):
                tile_load(i, *item, t).wait()

            @pl.when(t + AHEAD < count)
            def _():
                start_tile(t + AHEAD)

            @pl.when(t + AHEAD == count)
            def _():
                for i in range(len(key_side)):
                    key_load(i).start()

            @pl.when(step == 0)
            def _():
                acc[...] = jnp.zeros_like(acc)

            for pair in range(pairs):
                mapped = qf[at, feat_lanes(pair)]
                grads = gr[at, grad_lanes(pair)]
                acc[pair] += dot_tn(grads, mapped)
                grad = dot(grads, sd[batch, pair])
                qs[at, pair_cols(pair)] = feature_back(grad, mapped, qs[at], pair)
            wgrad[...] += dot(n[1 + t], qs[at])

            @pl.when(step == per - 1)
            def _():
                for pair in range(pairs):
                    both = acc[pair]
                    sg[batch, pair] = block_grads(both[:PAIR], norm_rows(both))

            return 0

        lax.fori_loop(0, count, queries, 0)
        for i in range(width // 16):
            at = slice(16 * i, 16 * i + 16)
            store_blocks(query_x, 16 * i, wgrad[at].astype(BF))
        for i in range(len(key_side)):
            key_load(i).wait()

    def key_phase(x, ga, wgrad):
        wait_x = [loads.start(x_hbm, x), loads.start(ga_hbm, ga)]

        def tile_at(t):
            return pl.ds(pl.multiple_of(TILE + t * TILE, TILE), TILE)

        def pack(blocks):
            for i in range(width // 16):
                at = slice(16 * i, 16 * i + 16)
                store_blocks(blocks, 16 * i, wgrad[at].astype(BF))

        def keys(t, _):
            batch = lax.div(t, per)
            talk(comm[count : 2 * count], t)
            at = tile_at(t)
            for pair in range(pairs):
                grad = dot(ones_beside(v[at, pair_cols(pair)]), sg[batch, pair])
                ks[at, pair_cols(pair)] = feature_back(grad, kf[at, feat_lanes(pair)], ks[at], pair)
            wgrad[...] += dot(n[1 + t], ks[at])
            return 0

        def values(t, _):
            batch = lax.div(t, per)
            talk(comm[2 * count : 3 * count], t)
            at = tile_at(t)
            for pair in range(pairs):
                grad = dot_nt(kf[at, feat_lanes(pair)], sg[batch, pair, :PAIR])
                v[at, pair_cols(pair)] = grad.astype(BF)
            wgrad[...] += dot(n[1 + t], v[at])
            return 0

        wgrad[...] = jnp.zeros_like(wgrad)
        lax.fori_loop(0, count, keys, 0)
        for batch in range(2):
            own = slice(batch * LONG, (batch + 1) * LONG)
            for pair in range(pairs):
                lanes, cols = feat_lanes(pair), pair_cols(pair)
                row = batch * pairs + pair
                packed = load_blocks(long_total, row * LONG, LONG, 2 * FEAT).astype(F32)
                grads = block_grads(unpack_pair(packed), long_norm[row : row + 1])
                mapped = kf[own, lanes]
                grad = dot(ones_beside(v[own, cols]), grads)
                v[own, cols] = dot_nt(mapped, grads[:PAIR]).astype(BF)
                ks[own, cols] = feature_back(grad, mapped, ks[own], pair)
        wgrad[...] += dot(n[0], ks[edge])
        pack(key_x)
        wgrad[...] = dot(n[0], v[edge])
        lax.fori_loop(0, count, values, 0)
        pack(value_x)
        for copy in wait_x:
            copy.wait()
        swap_rows(x, cuts)
        vec_held[0] = jnp.zeros(vec_held.shape[1:], F32)
        vec_held[0, 2:6] = vec_in[2:6]
        for i in range(bias_in.shape[1] // width):
            vec_held[0, 6 + i : 7 + i] = bias_in[:, i * width : (i + 1) * width]

        def last(rows_x, rows_ga, at):
            xhat, spread = normalize(rows_x)
            grad = (
                dot_nt(qs[at], wqkv[:, :width])
                + dot_nt(ks[at], wqkv[:, width : 2 * width])
                + dot_nt(v[at], wqkv[:, 2 * width :])
            )
            vec_held[0, 0:1] += jnp.sum(grad * xhat, axis=0, keepdims=True)
            vec_held[0, 1:2] += jnp.sum(grad, axis=0, keepdims=True)
            return rows_ga + norm_back(grad * gain[...], xhat, spread)

        def inputs(t, _):
            batch, step = lax.div(t, per), lax.rem(t, per)
            talk(comm[3 * count : 4 * count], t)
            raw_at = pl.ds(pl.multiple_of(LONG + step * TILE, LONG), TILE)
            at = tile_at(t)
            x[batch, raw_at] = last(x[batch, raw_at], ga[at], at)
            return 0

        lax.fori_loop(0, count, inputs, 0)
        store_edge(x, last(edge_rows(x), ga[edge], edge))
        vec_steps[0]()
        swap_rows(x, cuts)
        copy = pltpu.make_async_copy(x, in_grad, store_sem.at[0])
        copy.start()
        _all(last_steps)
        totals = [
            pltpu.make_async_copy(source, target, store_sem.at[1 + i])
            for i, (source, target) in enumerate(
                (
                    (out_total, out_out), (query_total, query_out),
                    (key_total, key_out), (value_total, value_out),
                )
            )
        ]
        for total in totals:
            total.start()
        vec_out[...] = vec_held[depth + 1]
        copy.wait()
        for total in totals:
            total.wait()

    wide = kf.shape[1]
    pl.run_scoped(
        query_phase,
        pltpu.VMEM((inner_rows, wide), BF),
        pltpu.VMEM((inner_rows, 2 * width), BF),
        pltpu.VMEM((pairs, 2 * PAIR, 2 * FEAT), F32),
        pltpu.VMEM((width, width), F32),
    )
    pl.run_scoped(
        key_phase,
        pltpu.VMEM(x_hbm.shape, F32),
        pltpu.VMEM((inner_rows, width), F32),
        pltpu.VMEM((width, width), F32),
    )
    for item in (ffn_sum, *out_sum, *query_sum, *key_sum, *value_sum, vec_sum):
        item.drain()


def body(
    inputs,
    lengths,
    first_gain,
    first_shift,
    query_weight,
    key_weight,
    value_weight,
    output_weight,
    output_bias,
    projection,
    second_gain,
    second_shift,
    up_weight,
    up_bias,
    down_weight,
    down_bias,
    cotangent,
):
    heads, head_size, feats = projection.shape
    batches, rows, width = inputs.shape
    digits = digits_of(lax.axis_size("seq"))
    ways = 2 * math.prod(digits)
    depth = len(digits)
    pairs = heads // 2
    big = rows - 2 * LONG
    inner = TILE + batches * big
    deep, half = up_weight.shape
    hidden = up_bias.shape[0]
    part = half // CHUNKS
    down_turned = down_weight.T

    lens = lengths.reshape(batches, lengths.shape[2])
    tiles = inner // TILE
    hbm = pl.BlockSpec(memory_space=pl.ANY)
    vmem = pl.BlockSpec(memory_space=pltpu.VMEM)
    smem = pl.BlockSpec(memory_space=pltpu.SMEM)

    def shape(*dims, dtype=BF):
        return jax.ShapeDtypeStruct(dims, dtype)

    def line(vector):
        return vector.reshape(1, -1)

    wide = 2 * FEAT * pairs
    long_block = block_shape(ways, batches * pairs * LONG, 2 * FEAT)
    inner_shapes = [
        ((inner, wide), BF), ((inner, wide), BF), ((inner, width), BF), ((inner, width), BF),
        ((inner, width), BF), ((tiles, width, TILE), BF), ((inner, width), BF),
        ((inner, width), F32), ((inner, width), F32), ((4, pairs, 2 * PAIR, 2 * FEAT), BF),
        ((heads, 2 * LONG, 2 * LONG), BF), ((width, 3 * width), BF), ((width, width), BF),
    ]
    kf, qf, v, ks, qs, n, mix, inv, att, sd, small, wqkv, wo, w = pl.pallas_call(
        functools.partial(attention_forward, digits),
        out_shape=[shape(*dims, dtype=kind) for dims, kind in inner_shapes]
        + [shape(2, *digits, 2 * deep, part)],
        in_specs=[smem, hbm] + [vmem] * 3 + [hbm] * 4 + [vmem] * 3,
        out_specs=[hbm] * 14,
        scratch_shapes=[pltpu.VMEM(inputs.shape, F32)]
        + [pltpu.VMEM(dims, kind) for dims, kind in inner_shapes]
        + [
            pltpu.VMEM((pairs, PAIR, 2 * FEAT), BF),
            pltpu.VMEM((2 * deep, part), BF),
            pltpu.VMEM((batches, pairs, PAIR, 2 * FEAT), F32),
            pltpu.VMEM((batches, pairs, 1, 2 * FEAT), F32),
            pltpu.VMEM((2,) + digits + long_block, BF),
            pltpu.VMEM((2,) + digits + long_block, BF),
            pltpu.SemaphoreType.DMA((16,)),
            pltpu.SemaphoreType.DMA((13,)),
            pltpu.SemaphoreType.DMA,
            pltpu.SemaphoreType.DMA((groups(depth, 2, 2),)),
            pltpu.SemaphoreType.DMA((groups(depth, 2, 2),)),
        ]
        + Whole.scratch(digits, batches * pairs, 2 * FEAT)
        + Scatter.scratch(digits, *long_block),
        compiler_params=pltpu.CompilerParams(
            collective_id=0, has_side_effects=True, vmem_limit_bytes=VMEM_LIMIT
        ),
        name="attention_forward",
    )(
        lens, inputs, line(first_gain), line(first_shift), line(output_bias),
        query_weight, key_weight, value_weight, output_weight, projection, up_weight, down_turned,
    )

    blocks = (2,) + digits + (2 * deep, part)
    output, ga, gr, ffn, ffn_grad, wo_grad, vec_in, bias_in, long_grad, long_norm = pl.pallas_call(
        functools.partial(feed_forward, digits),
        out_shape=[
            shape(*inputs.shape, dtype=F32),
            shape(inner, width, dtype=F32),
            shape(inner, 2 * width),
            shape(*blocks),
            shape(2 * deep, part, dtype=F32),
            shape(width, width, dtype=F32),
            shape(8, width, dtype=F32),
            shape(1, hidden, dtype=F32),
            shape(2, *digits, *long_block),
            shape(batches * pairs, 2 * FEAT, dtype=F32),
        ],
        in_specs=[smem] + [hbm] * 5 + [vmem] * 6 + [hbm],
        out_specs=[hbm] * 4 + [vmem] * 6,
        scratch_shapes=[
            pltpu.VMEM(inputs.shape, F32),
            pltpu.VMEM((inner, width), F32),
            pltpu.VMEM((inner, width), BF),
            pltpu.VMEM((inner, width), F32),
            pltpu.VMEM((inner, width), BF),
            pltpu.VMEM((inner, width), F32),
            pltpu.VMEM((inner, width), F32),
            pltpu.VMEM(blocks, BF),
            pltpu.VMEM(blocks, BF),
            pltpu.VMEM((width, hidden // CHUNKS), BF),
            pltpu.VMEM((width, hidden // CHUNKS), BF),
            pltpu.VMEM((width, hidden // CHUNKS), F32),
            pltpu.VMEM((width, hidden // CHUNKS), F32),
            pltpu.VMEM((TILE, 2 * width), BF),
            pltpu.VMEM((2, big // 2, 2 * width), BF),
            pltpu.VMEM((2 * LONG, wide), BF),
            pltpu.VMEM((2,) + digits + long_block, BF),
            pltpu.VMEM((2,) + digits + long_block, BF),
            pltpu.SemaphoreType.DMA((30,)),
            pltpu.SemaphoreType.DMA((6,)),
            pltpu.SemaphoreType.DMA((groups(depth, 2, 3),)),
            pltpu.SemaphoreType.DMA((groups(depth, 2, 3),)),
        ]
        + Scatter.scratch(digits, 2 * deep, part)
        + Scatter.scratch(digits, *long_block)
        + Whole.scratch(digits, batches * pairs, 2 * FEAT),
        compiler_params=pltpu.CompilerParams(
            collective_id=1, has_side_effects=True, vmem_limit_bytes=VMEM_LIMIT
        ),
        name="feed_forward",
    )(
        lens, cotangent, att, mix, inv, w, wo, line(second_gain), line(second_shift),
        line(up_bias), up_weight, down_turned, qf,
    )

    late_block = block_shape(ways, width, width)
    late_shape = (2,) + digits + late_block
    in_grad, ffn_more, out_w, query, key, value, vectors = pl.pallas_call(
        functools.partial(attention_backward, digits),
        out_shape=[
            shape(*inputs.shape, dtype=F32),
            shape(2 * deep, part, dtype=F32),
            shape(*late_shape),
            shape(*late_shape),
            shape(*late_shape),
            shape(*late_shape),
            shape(16, width, dtype=F32),
        ],
        in_specs=[smem] + [hbm] * 10 + [vmem, hbm] + [vmem] * 8,
        out_specs=[hbm, vmem, hbm, hbm, hbm, hbm, vmem],
        scratch_shapes=[
            pltpu.VMEM((inner, wide), BF),
            pltpu.VMEM((inner, width), BF),
            pltpu.VMEM((inner, width), BF),
            pltpu.VMEM((inner, width), BF),
            pltpu.VMEM((tiles, width, TILE), BF),
            pltpu.VMEM((4, pairs, 2 * PAIR, 2 * FEAT), BF),
            pltpu.VMEM((batches, pairs, 2 * PAIR, 2 * FEAT), BF),
            pltpu.VMEM((pairs, 2 * FEAT, 2 * PAIR), BF),
            pltpu.VMEM(blocks[1:], BF),
        ]
        + [pltpu.VMEM(late_shape, BF)] * 8
        + [
            pltpu.SemaphoreType.DMA((12,)),
            pltpu.SemaphoreType.DMA((4, tiles - 1)),
            pltpu.SemaphoreType.DMA((3,)),
            pltpu.SemaphoreType.DMA((5,)),
            pltpu.SemaphoreType.DMA((groups(depth, 4, 6),)),
            pltpu.SemaphoreType.DMA((groups(depth, 4, 6),)),
        ]
        + Scatter.scratch(digits, 2 * deep, part)
        + Scatter.scratch(digits, *late_block) * 4
        + Whole.scratch(digits, 16, width),
        compiler_params=pltpu.CompilerParams(
            collective_id=2, has_side_effects=True, vmem_limit_bytes=VMEM_LIMIT
        ),
        name="attention_backward",
    )(
        lens, inputs, ga, gr, kf, qf, v, ks, qs, n, sd, small, ffn,
        wo_grad, vec_in, bias_in, long_grad, long_norm, line(first_gain), wqkv, projection,
    )

    def whole(blocks):
        lanes = blocks.shape[-1]
        if lanes != width:
            blocks = blocks.reshape(width // 16, width // lanes, 16, lanes)
            blocks = jnp.swapaxes(blocks, 1, 2)
        return blocks.reshape(width, width).astype(F32)

    ffn_all = jnp.concatenate([ffn_grad, ffn_more], axis=1)
    return (
        output + down_bias,
        in_grad,
        vectors[0],
        vectors[1],
        whole(query),
        whole(key),
        whole(value),
        whole(out_w),
        vectors[2],
        vectors[3],
        vectors[4],
        ffn_all[:deep],
        vectors[6 : 6 + hidden // width].reshape(hidden),
        ffn_all[deep:].T,
        vectors[5],
    )


def solution(mesh):
    rows = P(None, ("seq", "ffn"), None)
    up, down = P("seq", "ffn"), P("ffn", "seq")
    in_specs = (rows, rows) + (P(),) * 10 + (up, P(), down, P(), rows)
    out_specs = (rows, rows) + (P(),) * 9 + (up, P(), down, P())
    return jax.shard_map(body, mesh=mesh, in_specs=in_specs, out_specs=out_specs, check_vma=False)
```

```python
import functools
import math

import jax
import jax.numpy as jnp
from jax import lax
from jax.experimental import pallas as pl
from jax.experimental.pallas import tpu as pltpu
from jax.sharding import PartitionSpec as P

BF, F32 = jnp.bfloat16, jnp.float32
EPS = 1e-5
LONG = 64
TILE = 256
PAIR = 128
AHEAD = 3
CHUNKS = 2
FEAT = 256
VMEM_LIMIT = 63 << 20
LOG16 = math.log(16.0)


def dot(a, b):
    return jnp.dot(a, b, preferred_element_type=F32)


def dot_nt(a, b):
    return lax.dot_general(a, b, (((1,), (1,)), ((), ())), preferred_element_type=F32)


def dot_tn(a, b):
    return lax.dot_general(a, b, (((0,), (0,)), ((), ())), preferred_element_type=F32)


def iota(shape, dim):
    return lax.broadcasted_iota(jnp.int32, shape, dim)


def normalize(rows):
    mean = jnp.mean(rows, axis=-1, keepdims=True)
    centred = rows - mean
    spread = jnp.mean(centred * centred, axis=-1, keepdims=True)
    scale = lax.rsqrt(spread + EPS)
    return centred * scale, scale


def norm_back(grad, xhat, scale):
    return scale * (
        grad
        - jnp.mean(grad, axis=-1, keepdims=True)
        - xhat * jnp.mean(grad * xhat, axis=-1, keepdims=True)
    )


def head_sums(pair):
    first = iota(pair.shape, 1) < PAIR // 2
    zero = jnp.zeros_like(pair)
    return (
        jnp.sum(jnp.where(first, pair, zero), axis=-1, keepdims=True),
        jnp.sum(jnp.where(first, zero, pair), axis=-1, keepdims=True),
    )


def features(scaled, scaled_low, proj, pair):
    cols = slice(pair * PAIR, (pair + 1) * PAIR)
    part = scaled[:, cols]
    first, second = head_sums(part * part)
    product = dot(scaled_low[:, cols], proj[pair])
    return jnp.concatenate(
        [
            jnp.exp(product[:, :FEAT] - (0.5 * first + LOG16)).astype(BF),
            jnp.exp(product[:, FEAT:] - (0.5 * second + LOG16)).astype(BF),
        ],
        axis=1,
    )


def lane_half(shape):
    return iota(shape, 1) < FEAT


def block_sums(both, norm):
    keep = (iota((PAIR, 2 * FEAT), 0) < PAIR // 2) == lane_half((PAIR, 2 * FEAT))
    zero = jnp.zeros((PAIR, 2 * FEAT), F32)
    return jnp.concatenate(
        [
            jnp.where(keep, both, zero).astype(BF),
            jnp.where(keep, jnp.broadcast_to(norm, (PAIR, 2 * FEAT)), zero).astype(BF),
        ],
        axis=0,
    )


def block_grads(both, norm):
    keep = (iota((PAIR, 2 * FEAT), 0) < PAIR // 2) == lane_half((PAIR, 2 * FEAT))
    zero = jnp.zeros((PAIR, 2 * FEAT), F32)
    row = iota((PAIR, 2 * FEAT), 0)
    high = norm.astype(BF).astype(F32)
    wide = jnp.broadcast_to(high, (PAIR, 2 * FEAT))
    rest = jnp.broadcast_to(norm - high, (PAIR, 2 * FEAT))
    return jnp.concatenate(
        [
            jnp.where(keep, both, zero).astype(BF),
            jnp.where(row == 0, wide, jnp.where(row == 1, rest, zero)).astype(BF),
        ],
        axis=0,
    )


def pack_pair(both):
    return jnp.where(lane_half((PAIR // 2, 2 * FEAT)), both[: PAIR // 2], both[PAIR // 2 :])


def norm_rows(both):
    return jnp.where(
        lane_half((1, 2 * FEAT)),
        jnp.sum(both[PAIR : PAIR + PAIR // 2], axis=0, keepdims=True),
        jnp.sum(both[PAIR + PAIR // 2 :], axis=0, keepdims=True),
    )


def unpack_pair(packed):
    return jnp.concatenate([packed, packed], axis=0)


def value_block(values, cols):
    part = values[:, cols]
    first = iota(part.shape, 1) < PAIR // 2
    zero = jnp.zeros_like(part)
    one = jnp.ones_like(part)
    top = jnp.concatenate([jnp.where(first, part, zero), jnp.where(first, one, zero)], axis=1)
    low = jnp.concatenate([jnp.where(first, zero, part), jnp.where(first, zero, one)], axis=1)
    return jnp.concatenate([top, low], axis=0)


def same_small(bounds):
    shape = (2 * LONG, 2 * LONG)

    def label(dim):
        at = iota(shape, dim)
        cut = jnp.where(at < LONG, bounds[0], LONG + bounds[1])
        return jnp.where(at < cut, 1, 0) + jnp.where(at < LONG, 0, 2)

    return label(0) == label(1)


def cuts_of(lens, big):
    cuts, bounds = [], []
    for batch in range(2):
        first, second = lens[batch, 0], lens[batch, 1]
        behind = jnp.where(second == big, first, first + second)
        cuts.append(jnp.where(first == big, 0, behind))
        bounds.append(jnp.where(first == big, second, first))
    return cuts, bounds


def swap_rows(buffer, cuts):
    most = buffer.shape[1]
    width = buffer.shape[2]
    for batch in range(2):
        head = buffer[batch, LONG : 2 * LONG]
        tail = buffer[batch, most - LONG :]
        small_first = iota((LONG, width), 0) < cuts[batch]
        buffer[batch, LONG : 2 * LONG] = jnp.where(small_first, tail, head)
        buffer[batch, most - LONG :] = jnp.where(small_first, head, tail)


class RowStore:
    def __init__(self, buffer, out, semaphore, tile):
        self.buffer, self.out, self.semaphore, self.tile = buffer, out, semaphore, tile

    def start(self, batch, at):
        pltpu.make_async_copy(
            self.buffer.at[batch, at], self.out.at[batch, at], self.semaphore
        ).start()

    def tile_done(self, batch, step):
        first = LONG + step * self.tile
        self.start(batch, pl.ds(pl.multiple_of(first + LONG, LONG), self.tile - LONG))

        @pl.when(step > 0)
        def _():
            self.start(batch, pl.ds(pl.multiple_of(first, LONG), LONG))

    def finish(self):
        rows = self.buffer.shape[1]
        for batch in range(2):
            self.start(batch, pl.ds(0, 2 * LONG))
            self.start(batch, pl.ds(rows - LONG, LONG))

    def wait(self):
        pltpu.make_async_copy(self.buffer, self.out, self.semaphore).wait()


def edge_rows(buffer):
    most = buffer.shape[1]
    return jnp.concatenate(
        [
            buffer[0, :LONG],
            buffer[1, :LONG],
            buffer[0, most - LONG :],
            buffer[1, most - LONG :],
        ],
        axis=0,
    )


def store_edge(buffer, value):
    most = buffer.shape[1]
    buffer[0, :LONG] = value[:LONG]
    buffer[1, :LONG] = value[LONG : 2 * LONG]
    buffer[0, most - LONG :] = value[2 * LONG : 3 * LONG]
    buffer[1, most - LONG :] = value[3 * LONG :]


def digits_of(size):
    out = []
    while size > 1:
        step = 4 if size % 4 == 0 else size
        out.append(step)
        size //= step
    return tuple(out)


class Net:
    def __init__(self, digits, send, recv):
        self.digits = digits
        self.send, self.recv = send, recv
        self.me = lax.axis_index("seq")
        self.core = lax.axis_index("ffn")
        self.slots = {}
        strides = [math.prod(digits[k + 1 :]) for k in range(len(digits))]
        self.own = [lax.rem(lax.div(self.me, s), n) for s, n in zip(strides, digits)]
        self.strides = strides

    def partner(self):
        return (self.me, 1 - self.core)

    def other(self, k, step):
        return lax.rem(self.own[k] + step, self.digits[k])

    def peer(self, k, step):
        return (self.me + (self.other(k, step) - self.own[k]) * self.strides[k], self.core)

    def greet(self):
        semaphore = pltpu.get_barrier_semaphore()
        peers = [self.partner()] + [
            self.peer(k, step) for k, n in enumerate(self.digits) for step in range(1, n)
        ]
        for peer in peers:
            pl.semaphore_signal(
                semaphore, inc=1, device_id=peer, device_id_type=pl.DeviceIdType.MESH
            )

    def meet(self):
        pl.semaphore_wait(
            pltpu.get_barrier_semaphore(), 1 + sum(n - 1 for n in self.digits)
        )

    def copy(self, key, source, target, device):
        slot = self.slots.setdefault(key, len(self.slots))
        return pltpu.make_async_remote_copy(
            src_ref=source,
            dst_ref=target,
            send_sem=self.send.at[slot],
            recv_sem=self.recv.at[slot],
            device_id=device,
            device_id_type=pl.DeviceIdType.MESH,
        )

    def group(self, key, size):
        return self.copy(key, size, size, self.partner())


def groups(depth, gathers, others):
    return gathers * (depth + 1) * (depth + 2) // 2 + others * (depth + 1)


class Gather:
    def __init__(self, net, name, out):
        self.net, self.name, self.out = net, name, out

    def fresh(self, j):
        net = self.net
        if j == 0:
            return [(net.core,) + tuple(net.own)]
        lead = (net.core,) + (slice(None),) * (j - 1)
        return [
            lead + (net.other(j - 1, step),) + tuple(net.own[j:])
            for step in range(1, net.digits[j - 1])
        ]

    def copies(self, j, k):
        net = self.net
        depth = len(net.digits)
        copies = []
        for at in self.fresh(j):
            block = self.out.at[at]
            if k == depth:
                copies.append(net.copy((self.name, j, k), block, block, net.partner()))
                continue
            for step in range(1, net.digits[k]):
                copies.append(net.copy((self.name, j, k), block, block, net.peer(k, step)))
        return copies

    def group(self, j, k):
        digits = self.net.digits
        at = [0] * (1 + len(digits))
        if j:
            at[1:j] = [slice(None)] * (j - 1)
            at[j] = pl.ds(0, digits[j - 1] - 1)
        if k < len(digits):
            at[1 + k] = pl.ds(0, digits[k] - 1)
        return self.net.group((self.name, j, k), self.out.at[tuple(at)])

    def steps(self):
        depth = len(self.net.digits)

        def run(j):
            for i in range(j):
                self.group(i, j - 1).wait_recv()
            for k in range(j, depth + 1):
                for copy in self.copies(j, k):
                    copy.start()

        def last():
            for j in range(depth + 1):
                self.group(j, depth).wait_recv()

        return [functools.partial(run, j) for j in range(depth + 1)] + [last]

    def drain(self):
        depth = len(self.net.digits)
        for j in range(depth + 1):
            for k in range(j, depth + 1):
                self.group(j, k).wait_send()


class Scatter:
    def __init__(self, net, name, blocks, first, slots, parts, finish, apart=None):
        self.net, self.name = net, name
        self.away = (blocks if apart is None else apart).at[1 - net.core]
        self.held = blocks.at[net.core] if apart is None else blocks
        self.first, self.slots, self.parts, self.finish = first, slots, parts, finish

    @staticmethod
    def scratch(digits, rows, cols):
        shapes = [pltpu.VMEM(digits + (rows, cols), BF)]
        for k in reversed(range(len(digits))):
            shapes.append(pltpu.VMEM((digits[k] - 1,) + digits[:k] + (rows, cols), BF))
        for k in reversed(range(1, len(digits))):
            shapes.append(pltpu.VMEM(digits[:k] + (rows, cols), BF))
        return shapes

    @classmethod
    def of(cls, net, name, blocks, refs, finish, apart=None):
        depth = len(net.digits)
        slots, parts = refs[1 : 1 + depth], refs[1 + depth :]
        return cls(net, name, blocks, refs[0], slots, parts, finish, apart)

    def copies(self, k):
        net = self.net
        depth = len(net.digits)
        if k == 0:
            return [net.copy((self.name, 0), self.away, self.first, net.partner())]
        digit = depth - k
        held = self.held if k == 1 else self.parts[k - 2]
        copies = []
        for step in range(1, net.digits[digit]):
            at = (slice(None),) * digit + (net.other(digit, step),)
            copies.append(
                net.copy(
                    (self.name, k),
                    held.at[at],
                    self.slots[k - 1].at[step - 1],
                    net.peer(digit, step),
                )
            )
        return copies

    def group(self, k):
        return self.net.group((self.name, k), self.slots[k - 1] if k else self.first)

    def add(self, k):
        net = self.net
        depth = len(net.digits)
        if k == 0:
            lead = net.digits
            for at in _indices(lead):
                mine = self.held[at].astype(F32)
                self.held[at] = (mine + self.first[at].astype(F32)).astype(BF)
            return
        digit = depth - k
        held = self.held if k == 1 else self.parts[k - 2]
        for at in _indices(net.digits[:digit]):
            total = held[at + (net.own[digit],)].astype(F32)
            for step in range(net.digits[digit] - 1):
                total = total + self.slots[k - 1][(step,) + at].astype(F32)
            if digit:
                self.parts[k - 1][at] = total.astype(BF)
            else:
                self.finish(total)

    def steps(self):
        depth = len(self.net.digits)

        def start(k):
            for copy in self.copies(k):
                copy.start()

        def follow(k):
            self.group(k - 1).wait_recv()
            self.add(k - 1)
            if k <= depth:
                start(k)

        return [functools.partial(start, 0)] + [
            functools.partial(follow, k) for k in range(1, depth + 2)
        ]

    def drain(self):
        for k in range(len(self.net.digits) + 1):
            self.group(k).wait_send()


def _indices(lead):
    if not lead:
        return [()]
    return [(i,) + rest for i in range(lead[0]) for rest in _indices(lead[1:])]


class Whole:
    def __init__(self, net, name, held, slots):
        self.net, self.name, self.held, self.slots = net, name, held, slots

    @staticmethod
    def scratch(digits, rows, cols):
        return [
            pltpu.VMEM((len(digits) + 2, rows, cols), F32),
            pltpu.VMEM((1 + sum(n - 1 for n in digits), rows, cols), F32),
        ]

    def span(self, k):
        digits = self.net.digits
        return (0, 1) if k == 0 else (1 + sum(n - 1 for n in digits[: k - 1]), digits[k - 1] - 1)

    def copies(self, k):
        net = self.net
        source = self.held.at[k]
        first, number = self.span(k)
        peers = [net.partner()] if k == 0 else [net.peer(k - 1, 1 + i) for i in range(number)]
        return [
            net.copy((self.name, k), source, self.slots.at[first + i], peer)
            for i, peer in enumerate(peers)
        ]

    def group(self, k):
        return self.net.group((self.name, k), self.slots.at[pl.ds(*self.span(k))])

    def steps(self):
        depth = len(self.net.digits)

        def start(k):
            for copy in self.copies(k):
                copy.start()

        def follow(k):
            self.group(k - 1).wait_recv()
            total = self.held[k - 1]
            first, number = self.span(k - 1)
            for i in range(number):
                total = total + self.slots[first + i]
            self.held[k] = total
            if k <= depth:
                start(k)

        return [functools.partial(start, 0)] + [
            functools.partial(follow, k) for k in range(1, depth + 2)
        ]

    def drain(self):
        for k in range(len(self.net.digits) + 1):
            self.group(k).wait_send()


def together(*parts):
    most = max(len(part) for part in parts)

    def run(i):
        for part in parts:
            if i < len(part):
                part[i]()

    return [functools.partial(run, i) for i in range(most)]


def block_shape(ways, rows, cols):
    lanes = cols * (rows // 16) // ways
    return 16, lanes


def block_at(digits, index):
    at = []
    for n in reversed(digits):
        at.append(index % n)
        index //= n
    return tuple(reversed(at))


def store_blocks(blocks, row, value):
    lanes = blocks.shape[-1]
    per_row = value.shape[1] // lanes
    ways = (2,) + blocks.shape[1:-2]
    for i in range(value.shape[0] // 16):
        for j in range(per_row):
            at = block_at(ways, (row // 16 + i) * per_row + j)
            blocks[at] = value[16 * i : 16 * i + 16, j * lanes : (j + 1) * lanes]


def load_blocks(blocks, row, rows, cols):
    lanes = blocks.shape[-1]
    per_row = cols // lanes
    ways = (2,) + blocks.shape[1:-2]
    out = []
    for i in range(rows // 16):
        line = [
            blocks[block_at(ways, (row // 16 + i) * per_row + j)] for j in range(per_row)
        ]
        out.append(line[0] if per_row == 1 else jnp.concatenate(line, axis=1))
    return jnp.concatenate(out, axis=0)


class Loads:
    def __init__(self, semaphores):
        self.semaphores = semaphores
        self.count = 0

    def start(self, source, target):
        copy = pltpu.make_async_copy(source, target, self.semaphores.at[self.count])
        self.count += 1
        copy.start()
        return copy


PIECES = ((0, 128), (1088, 64), (128, 192), (320, 256), (576, 256), (832, 256))


def raw_pieces(rows):
    quarter = (rows - 2 * LONG) // 4
    pieces = [(0, 2 * LONG), (rows - LONG, LONG), (2 * LONG, quarter - LONG)]
    return pieces + [(LONG + quarter * i, quarter) for i in range(1, 4)]


def big_start(batch, rows_big, step, tile):
    return TILE + batch * rows_big + step * tile


def pair_projection(projection, pair):
    first, second = projection[2 * pair], projection[2 * pair + 1]
    gap = jnp.zeros_like(first)
    return jnp.concatenate(
        [jnp.concatenate([first, gap], axis=1), jnp.concatenate([gap, second], axis=1)], axis=0
    )


def place(steps, spots, count):
    lists = [[] for _ in range(count)]
    for step, spot in zip(steps, spots, strict=True):
        lists[spot].append(step)
    return lists


def spots(known, number):
    if number == len(known):
        return list(known)
    last = len(known) - 1
    return [known[min(last, -(-i * last // max(1, number - 1)))] for i in range(number)]


def side_by_side(chains):
    most = max(len(chain) for chain in chains)
    return [
        chain[i - most] for i in range(most) for chain in chains if i >= most - len(chain)
    ]


def talk(lists, t):
    for i, steps in enumerate(lists):
        if steps:
            pl.when(t == i)(functools.partial(_all, steps))


def _all(steps):
    for step in steps:
        step()


def all_reduce(scatter, spread):
    first, second = scatter.steps(), spread.steps()
    return first[:-1] + [functools.partial(_both, first[-1], second[0])] + second[1:]


def weight_block(up, down, chunk):
    half = up.shape[1] // CHUNKS
    at = slice(chunk * half, (chunk + 1) * half)
    return jnp.concatenate([up[:, at], down[:, at]], axis=0).astype(BF)


def attention_forward(
    digits, lens, x_hbm, gain, shift, bias, wq_hbm, wk_hbm, wv_hbm, wo_hbm, projection, up, down,
    k_out, q_out, v_out, ks_out, qs_out, n_out, mix_out, inv_out, att_out, sd_out, small_out,
    wqkv_out, wo_out, w_out,
    x, kf, qf, v, ks, qs, n, mix, inv, att, sd, small, wqkv, wo, proj, block, acc, nacc, parts,
    total, load_sem, store_sem, own_sem, send, recv, whole_held, whole_slots, *slots,
):
    rows = x.shape[1]
    big = rows - 2 * LONG
    pairs = proj.shape[0]
    width = wo.shape[0]
    scale = (PAIR // 2) ** -0.25
    depth = len(digits)
    net = Net(digits, send, recv)
    loads = Loads(load_sem)
    pieces = raw_pieces(rows)
    pending = {}

    def load_rows(some):
        for piece in some:
            for batch in range(2):
                span = pl.ds(*piece)
                pending[batch, piece] = loads.start(x_hbm.at[batch, span], x.at[batch, span])

    load_rows(pieces[:2])
    weights = [
        loads.start(source, att.at[pl.ds(i * width, width)])
        for i, source in enumerate((wq_hbm, wk_hbm, wv_hbm, wo_hbm))
    ]
    net.greet()
    block[...] = weight_block(up, down, 0)
    own_block = pltpu.make_async_copy(block, w_out.at[(net.core,) + tuple(net.own)], own_sem)
    own_block.start()
    for pair in range(pairs):
        proj[pair] = pair_projection(projection, pair).astype(BF)
    own_block.wait()
    net.meet()
    gather = Gather(net, "w", w_out)
    gather_steps = gather.steps()
    gather_steps[0]()

    def finish(value):
        total[(net.core,) + tuple(net.own)] = value.astype(BF)

    scatter = Scatter.of(net, "s", parts, slots, finish)
    spread = Gather(net, "t", total)
    whole = Whole(net, "n", whole_held, whole_slots)
    sum_steps = together(all_reduce(scatter, spread), whole.steps())
    cuts, bounds = cuts_of(lens, big)
    for i, copy in enumerate(weights):
        copy.wait()
        rounded = att[i * width : (i + 1) * width].astype(BF)
        if i < 3:
            wqkv[:, i * width : (i + 1) * width] = rounded
        else:
            wo[...] = rounded

    def front(rows_x, tile):
        xhat, _ = normalize(rows_x)
        low = (xhat * gain[...] + shift[...]).astype(BF)
        n[tile] = low.T
        raw = dot(low, wqkv[...])
        q = raw[:, :width] * scale
        k = raw[:, width : 2 * width] * scale
        return q, k, raw[:, 2 * width :].astype(BF)

    def attend(numer_denom, at, pair):
        cols = slice(pair * PAIR, (pair + 1) * PAIR)
        inverse = 1.0 / numer_denom[:, PAIR:]
        inv[at, cols] = inverse
        mix[at, cols] = (numer_denom[:, :PAIR] * inverse).astype(BF)

    load_rows(pieces[2:])
    for piece in pieces[:2]:
        for batch in range(2):
            pending[batch, piece].wait()
    swap_rows(x, cuts)
    edge = slice(0, TILE)
    q, k, values = front(edge_rows(x), 0)
    v[edge] = values
    k_low = k.astype(BF)
    ks[edge] = k_low
    for pair in range(pairs):
        cols = slice(pair * PAIR, (pair + 1) * PAIR)
        feats = slice(pair * 2 * FEAT, (pair + 1) * 2 * FEAT)
        mapped = features(k, k_low, proj, pair)
        kf[edge, feats] = mapped
        for batch in range(2):
            own = slice(batch * LONG, (batch + 1) * LONG)
            both = dot_tn(values[own, cols], mapped[own])
            row = batch * pairs + pair
            store_blocks(parts, row * LONG, pack_pair(both).astype(BF))
            whole_held[0, row : row + 1] = jnp.sum(mapped[own].astype(F32), axis=0, keepdims=True)
    sum_steps[0]()
    q_low = q.astype(BF)
    qs[edge] = q_low
    same = same_small(bounds)
    shorts = slice(2 * LONG, TILE)
    for pair in range(pairs):
        cols = slice(pair * PAIR, (pair + 1) * PAIR)
        feats = slice(pair * 2 * FEAT, (pair + 1) * 2 * FEAT)
        mapped = features(q, q_low, proj, pair)
        qf[edge, feats] = mapped
        scores = []
        for head in range(2):
            lanes = slice((2 * pair + head) * FEAT, (2 * pair + head + 1) * FEAT)
            score = dot_nt(
                mapped[shorts, head * FEAT : (head + 1) * FEAT], kf[shorts, lanes]
            )
            score = jnp.where(same, score, 0.0).astype(BF)
            small[2 * pair + head] = score
            scores.append(score)
        attend(
            dot(jnp.concatenate(scores, axis=1), value_block(values[shorts], cols)), shorts, pair
        )

    def store(source, target, at, slot):
        pltpu.make_async_copy(source.at[at], target.at[at], store_sem.at[slot]).start()

    first_pass = ((kf, k_out), (qf, q_out), (v, v_out), (ks, ks_out), (qs, qs_out), (n, n_out))
    second_pass = ((mix, mix_out), (inv, inv_out), (att, att_out))
    once = ((small, small_out), (wqkv, wqkv_out), (wo, wo_out))

    def store_first(at, tile):
        for slot, (source, target) in enumerate(first_pass):
            store(source, target, tile if source is n else at, slot)

    def store_second(at):
        for slot, (source, target) in enumerate(second_pass):
            store(source, target, at, len(first_pass) + slot)

    def whole_copy(i):
        slot = len(first_pass) + len(second_pass) + i
        return pltpu.make_async_copy(*once[i], store_sem.at[slot])

    store_first(pl.ds(0, TILE), 0)
    for i in range(3):
        whole_copy(i).start()
    for piece in pieces[2:]:
        for batch in range(2):
            pending[batch, piece].wait()
    acc[...] = jnp.zeros_like(acc)
    nacc[...] = jnp.zeros_like(nacc)
    per = big // TILE
    count = 2 * per
    comm = place(
        sum_steps[1:] + gather_steps[1:],
        spots((1, 3, 5, 7, count + 2, count + 6), len(sum_steps) - 1)
        + spots((3, count, count + 4), len(gather_steps) - 1),
        2 * count,
    )

    def pass_one(t, _):
        batch, step = lax.div(t, per), lax.rem(t, per)
        talk(comm[:count], t)
        raw_at = pl.ds(pl.multiple_of(LONG + step * TILE, LONG), TILE)
        at = pl.ds(pl.multiple_of(TILE + t * TILE, TILE), TILE)
        q, k, values = front(x[batch, raw_at], 1 + t)
        v[at] = values
        k_low = k.astype(BF)
        q_low = q.astype(BF)
        ks[at] = k_low
        qs[at] = q_low
        for pair in range(pairs):
            cols = slice(pair * PAIR, (pair + 1) * PAIR)
            feats = slice(pair * 2 * FEAT, (pair + 1) * 2 * FEAT)
            mapped = features(k, k_low, proj, pair)
            kf[at, feats] = mapped
            acc[batch, pair] += dot_tn(values[:, cols], mapped)
            nacc[batch, pair] += jnp.sum(mapped.astype(F32), axis=0, keepdims=True)
            qf[at, feats] = features(q, q_low, proj, pair)
        store_first(at, 1 + t)
        return 0

    lax.fori_loop(0, count, pass_one, 0)
    for batch in range(2):
        for pair in range(pairs):
            sd[batch, pair] = block_sums(acc[batch, pair], nacc[batch, pair])

    sd_copies = [
        pltpu.make_async_copy(sd.at[pl.ds(i, 2)], sd_out.at[pl.ds(i, 2)], store_sem.at[12 + i // 2])
        for i in (0, 2)
    ]
    sd_copies[0].start()

    def pass_two(t, _):
        batch, step = lax.div(t, per), lax.rem(t, per)
        talk(comm[count:], t)
        raw_at = pl.ds(pl.multiple_of(LONG + step * TILE, LONG), TILE)
        at = pl.ds(pl.multiple_of(TILE + t * TILE, TILE), TILE)
        for pair in range(pairs):
            feats = slice(pair * 2 * FEAT, (pair + 1) * 2 * FEAT)
            attend(dot_nt(qf[at, feats], sd[batch, pair]), at, pair)
        att[at] = x[batch, raw_at] + dot(mix[at], wo[...]) + bias[...]
        store_second(at)
        return 0

    lax.fori_loop(0, count, pass_two, 0)
    for batch in range(2):
        own = slice(batch * LONG, (batch + 1) * LONG)
        for pair in range(pairs):
            feats = slice(pair * 2 * FEAT, (pair + 1) * 2 * FEAT)
            row = batch * pairs + pair
            packed = load_blocks(total, row * LONG, LONG, 2 * FEAT).astype(F32)
            sd[2 + batch, pair] = block_sums(
                unpack_pair(packed), whole_held[depth + 1, row : row + 1]
            )
            attend(dot_nt(qf[own, feats], sd[2 + batch, pair]), own, pair)
    att[edge] = edge_rows(x) + dot(mix[edge], wo[...]) + bias[...]
    store_second(pl.ds(0, TILE))
    sd_copies[1].start()
    for slot, (source, target) in enumerate(first_pass + second_pass):
        pltpu.make_async_copy(source, target, store_sem.at[slot]).wait()
    for i in range(len(once)):
        whole_copy(i).wait()
    for copy in sd_copies:
        copy.wait()
    gather.drain()
    scatter.drain()
    spread.drain()
    whole.drain()


def _both(first, second):
    first()
    second()


def feed_forward(
    digits, lens, cot_hbm, att_hbm, mix_hbm, inv_hbm, w_hbm, wo, gain, shift, up_bias,
    up_own, down_own, q_hbm,
    out_hbm, ga_out, g_out, x_out, ffn_out, wo_grad, vec_grad, bias_grad, long_out, norm_out,
    cot, att, mix, inv, second, branch, grad_second, w_first, w_second, up, down, dup, ddown,
    gr_edge, gr, qf, parts, long_total, load_sem, store_sem, send, recv, *refs,
):
    rows = cot.shape[1]
    big = rows - 2 * LONG
    width = wo.shape[0]
    pairs = width // PAIR
    tile = big // 2
    per = big // tile
    count = 2 * per
    depth = len(digits)
    cuts, _ = cuts_of(lens, big)
    net = Net(digits, send, recv)
    net.greet()
    loads = Loads(load_sem)
    deep = w_first.shape[-2] // 2
    half = w_first.shape[-1]
    wait_w = loads.start(w_hbm, w_first)
    pieces = raw_pieces(rows)
    inner = [(0, TILE)] + [(TILE + tile * i, tile) for i in range(count)]

    def load_cot(some):
        return [
            loads.start(cot_hbm.at[batch, pl.ds(*piece)], cot.at[batch, pl.ds(*piece)])
            for piece in some
            for batch in range(2)
        ]

    def load_inner(source, target, some):
        return [loads.start(source.at[pl.ds(*p)], target.at[pl.ds(*p)]) for p in some]

    first_waits = load_inner(att_hbm, att, inner[:1]) + load_cot(pieces[:2])
    w_second[(net.core,) + tuple(net.own)] = weight_block(up_own, down_own, 1)
    net.meet()
    gather = Gather(net, "w", w_second)
    gather_steps = gather.steps()
    gather_steps[0]()

    def finish(value):
        ffn_out[...] = value

    scatter = Scatter.of(net, "f", w_first, refs[: 2 * depth], finish)
    scatter_steps = scatter.steps()

    def finish_long(value):
        long_total[(net.core,) + tuple(net.own)] = value.astype(BF)

    long_scatter = Scatter.of(net, "s", parts, refs[2 * depth : 4 * depth], finish_long)
    long_spread = Gather(net, "t", long_total)
    norm_held, norm_slots = refs[4 * depth :]
    norm_sum = Whole(net, "n", norm_held, norm_slots)
    long_steps = together(all_reduce(long_scatter, long_spread), norm_sum.steps())
    members = _indices(digits)
    group = max(1, 16 // deep)

    def unpack(w):
        for core in range(2):
            cols = slice(core * half, (core + 1) * half)
            for first in range(0, len(members), group):
                parts = [w[(core,) + members[first + i]] for i in range(group)]
                at = slice(first * deep, (first + group) * deep)
                if group == 1:
                    up[at, cols] = parts[0][:deep]
                    down[at, cols] = parts[0][deep:]
                else:
                    up[at, cols] = jnp.concatenate([part[:deep] for part in parts], axis=0)
                    down[at, cols] = jnp.concatenate([part[deep:] for part in parts], axis=0)

    def pack(w):
        for core in range(2):
            cols = slice(core * half, (core + 1) * half)
            for i, member in enumerate(members):
                at = slice(i * deep, (i + 1) * deep)
                w[(core,) + member] = jnp.concatenate(
                    [dup[at, cols], ddown[at, cols]], axis=0
                ).astype(BF)

    def bias_lanes(chunk):
        return [
            slice((CHUNKS * core + chunk) * half, (CHUNKS * core + chunk + 1) * half)
            for core in range(2)
        ]

    def add_row(at, value):
        vec_grad[at : at + 1] += jnp.sum(value, axis=0, keepdims=True)

    def hidden_part(chunk, second_low, grad_low):
        bias = jnp.concatenate([up_bias[:, lanes] for lanes in bias_lanes(chunk)], axis=1)
        hidden = dot(second_low, up[...]) + bias
        gauss = jnp.exp(-0.5 * hidden * hidden) * (1.0 / math.sqrt(2.0 * math.pi))
        cdf = 0.5 + 0.5 * lax.erf(hidden * math.sqrt(0.5))
        active = (hidden * cdf).astype(BF)
        slope = cdf + hidden * gauss
        grad_hidden = (dot(grad_low, down[...]) * slope).astype(BF)
        dup[...] += dot(second_low.T, grad_hidden)
        ddown[...] += dot(grad_low.T, active)
        bias_sum = jnp.sum(grad_hidden.astype(F32), axis=0, keepdims=True)
        for core, lanes in enumerate(bias_lanes(chunk)):
            bias_grad[:, lanes] += bias_sum[:, core * half : (core + 1) * half]
        return dot_nt(active, down[...]), dot_nt(grad_hidden, up[...])

    def first_block(at, grad_out):
        xhat, _ = normalize(att[at])
        low = (xhat * gain[...] + shift[...]).astype(BF)
        second[at] = low
        branch[at], grad_second[at] = hidden_part(0, low, grad_out.astype(BF))

    def second_block(at, grad_out, put, between=lambda: None):
        more, grad_more = hidden_part(1, second[at], grad_out.astype(BF))
        between()
        att_rows = att[at]
        xhat, scale = normalize(att_rows)
        output = att_rows + (branch[at] + more)
        grad = grad_second[at] + grad_more
        grad_att = grad_out + norm_back(grad * gain[...], xhat, scale)
        add_row(2, grad_att)
        add_row(3, grad * xhat)
        add_row(4, grad)
        add_row(5, grad_out)
        grad_att_low = grad_att.astype(BF)
        mixed = mix[at]
        wo_grad[...] += dot_tn(mixed, grad_att_low)
        grad_mixed = dot_nt(grad_att_low, wo[...]).astype(BF).astype(F32)
        for pair in range(pairs):
            cols = slice(pair * PAIR, (pair + 1) * PAIR)
            part = grad_mixed[:, cols]
            inverse = inv[at, cols]
            first, last = head_sums(part * mixed[:, cols].astype(F32))
            lane = iota(part.shape, 1)
            grad_denom = -jnp.where(lane < PAIR // 2, first, last) * inverse
            high = grad_denom.astype(BF).astype(F32)
            both = jnp.where(lane % (PAIR // 2) < PAIR // 4, high, grad_denom - high)
            put(2 * pair, (part * inverse).astype(BF))
            put(2 * pair + 1, (both * (4.0 / PAIR)).astype(BF))
        att[at] = grad_att
        return output

    def lanes_of(i):
        return slice(i * PAIR, (i + 1) * PAIR)

    def store_g(t):
        slot = lax.rem(t, 2)
        at = pl.ds(pl.multiple_of(TILE + t * tile, TILE), tile)
        return pltpu.make_async_copy(gr.at[slot], g_out.at[at], store_sem.at[slot])

    def store_att(at):
        pltpu.make_async_copy(att.at[at], ga_out.at[at], store_sem.at[2]).start()

    def rows_at(t):
        batch, step = lax.div(t, per), lax.rem(t, per)
        raw_at = pl.ds(pl.multiple_of(LONG + step * tile, LONG), tile)
        return batch, raw_at, pl.ds(pl.multiple_of(TILE + t * tile, TILE), tile)

    for ref in (dup, ddown, wo_grad, vec_grad, bias_grad):
        ref[...] = jnp.zeros_like(ref)
    wait_w.wait()
    for copy in first_waits:
        copy.wait()
    next_waits = load_inner(att_hbm, att, inner[1:]) + load_cot(pieces[2:])
    unpack(w_first)
    edge = pl.ds(0, TILE)
    swap_rows(cot, cuts)
    first_block(edge, edge_rows(cot))
    for copy in next_waits:
        copy.wait()
    last_waits = [loads.start(q_hbm.at[pl.ds(0, 2 * LONG)], qf)]
    for some in (inner[:1], inner[1:]):
        last_waits += load_inner(mix_hbm, mix, some) + load_inner(inv_hbm, inv, some)
    gather_at = place(gather_steps[1:], spots((1, 3, count), len(gather_steps) - 1), count + 1)

    def first_pass(t, _):
        talk(gather_at[:count], t)
        batch, raw_at, at = rows_at(t)
        first_block(at, cot[batch, raw_at])
        return 0

    lax.fori_loop(0, count, first_pass, 0)
    _all(gather_at[count])
    pack(w_first)
    scatter_steps[0]()
    unpack(w_second)
    dup[...] = jnp.zeros_like(dup)
    ddown[...] = jnp.zeros_like(ddown)
    for copy in last_waits:
        copy.wait()

    def put_edge(i, value):
        gr_edge[:, lanes_of(i)] = value

    store_edge(cot, second_block(edge, edge_rows(cot), put_edge))
    store_att(edge)
    edge_copy = pltpu.make_async_copy(gr_edge, g_out.at[edge], store_sem.at[3])
    edge_copy.start()
    for batch in range(2):
        own = slice(batch * LONG, (batch + 1) * LONG)
        for pair in range(pairs):
            grads = gr_edge[own, 2 * pair * PAIR : (2 * pair + 2) * PAIR]
            both = dot_tn(grads, qf[own, 2 * pair * FEAT : (2 * pair + 2) * FEAT])
            row = batch * pairs + pair
            store_blocks(parts, row * LONG, pack_pair(both[:PAIR]).astype(BF))
            norm_held[0, row : row + 1] = norm_rows(both)
    long_steps[0]()
    scatter_at = place(
        long_steps[1:] + scatter_steps[1:],
        spots((0, 2, 4, 6, 2 * count, 2 * count), len(long_steps) - 1)
        + spots((0, 6, 2 * count), len(scatter_steps) - 1),
        2 * count + 1,
    )

    out_store = RowStore(cot, out_hbm, store_sem.at[4], tile)
    finals = scatter_at[2 * count]
    split = sum(step in long_steps for step in finals)
    last_steps = side_by_side([finals[:split], finals[split:]])

    def second_pass(t, _):
        talk(scatter_at[: 2 * count : 2], t)
        batch, raw_at, at = rows_at(t)

        @pl.when(t >= 2)
        def _():
            store_g(t - 2).wait()

        def put(i, value):
            gr[lax.rem(t, 2), :, lanes_of(i)] = value

        cot[batch, raw_at] = second_block(
            at, cot[batch, raw_at], put, functools.partial(talk, scatter_at[1 : 2 * count : 2], t)
        )
        out_store.tile_done(batch, lax.rem(t, per))
        store_att(at)
        store_g(t).start()
        return 0

    lax.fori_loop(0, count, second_pass, 0)
    swap_rows(cot, cuts)
    out_store.finish()
    gather.drain()
    pack(w_second)
    x_copy = pltpu.make_async_copy(w_second, x_out, store_sem.at[5])
    x_copy.start()
    _all(last_steps)
    long_out[...] = long_total[...]
    norm_out[...] = norm_held[depth + 1]
    store_g(count - 2).wait()
    store_g(count - 1).wait()
    pltpu.make_async_copy(att, ga_out, store_sem.at[2]).wait()
    edge_copy.wait()
    out_store.wait()
    x_copy.wait()
    for item in (scatter, long_scatter, long_spread, norm_sum):
        item.drain()


def attention_backward(
    digits, lens, x_hbm, ga_hbm, g_hbm, k_hbm, q_hbm, v_hbm, ks_hbm, qs_hbm, n_hbm,
    sd_hbm, small, ffn_hbm, wo_grad, vec_in, bias_in, long_total, long_norm, gain, wqkv,
    projection,
    in_grad, ffn_out, out_out, query_out, key_out, value_out, vec_out,
    kf, v, ks, qs, n, sd, sg, back, ffn, out_x, out_total, query_x, query_total, key_x, key_total,
    value_x, value_total, load_sem, tile_sem, key_sem, store_sem, send, recv, *refs,
):
    rows = x_hbm.shape[1]
    big = rows - 2 * LONG
    pairs = back.shape[0]
    width = wqkv.shape[0]
    inner_rows = kf.shape[0]
    scale = (PAIR // 2) ** -0.25
    depth = len(digits)
    net = Net(digits, send, recv)
    each = 2 * depth
    refs = list(refs)

    def take(number):
        taken, refs[:] = refs[:number], refs[number:]
        return taken

    loads = Loads(load_sem)
    per = big // TILE
    count = 2 * per
    shorts = slice(2 * LONG, TILE)
    edge = slice(0, TILE)
    cuts, bounds = cuts_of(lens, big)
    same = same_small(bounds)

    def finish_ffn(value):
        ffn_out[...] = value

    ffn_sum = Scatter.of(net, "f", ffn, take(each), finish_ffn, apart=ffn_hbm)

    def reduction(name, blocks, total):
        def finish(value):
            total[(net.core,) + tuple(net.own)] = value.astype(BF)

        return Scatter.of(net, name, blocks, take(each), finish), Gather(net, name + "t", total)

    out_sum = reduction("o", out_x, out_total)
    query_sum = reduction("q", query_x, query_total)
    key_sum = reduction("k", key_x, key_total)
    value_sum = reduction("l", value_x, value_total)
    vec_held, vec_slots = take(2)
    vec_sum = Whole(net, "v", vec_held, vec_slots)
    ffn_steps = ffn_sum.steps()
    out_steps = all_reduce(*out_sum)
    query_steps = all_reduce(*query_sum)
    key_steps = all_reduce(*key_sum)
    value_steps = all_reduce(*value_sum)
    vec_steps = vec_sum.steps()
    last_spot = 4 * count
    number = len(out_steps)
    chains = (
        (out_steps[1:], spots((0, 4, 7, 11, 16, 22), number - 1)),
        (ffn_steps[1:], spots((0, 12, 24), len(ffn_steps) - 1)),
        (query_steps, spots((8, 10, 16, 25, 31, 32, 32), number)),
        (key_steps, spots((16, 20, 29, 32, 32, 32, 32), number)),
        (value_steps, spots((24, 26, 32, 32, 32, 32, 32), number)),
    )
    comm = [[] for _ in range(last_spot)]
    ends = []
    for steps, at in chains:
        ends.append([step for step, spot in zip(steps, at, strict=True) if spot == last_spot])
        for step, spot in zip(steps, at, strict=True):
            if spot < last_spot:
                comm[spot].append(step)
    last_steps = side_by_side([end for end in ends if end] + [vec_steps[1:]])

    def feat_lanes(pair):
        return slice(pair * 2 * FEAT, (pair + 1) * 2 * FEAT)

    def pair_cols(pair):
        return slice(pair * PAIR, (pair + 1) * PAIR)

    def grad_lanes(pair):
        return slice(2 * pair * PAIR, (2 * pair + 2) * PAIR)

    def feature_back(grad, mapped, scaled, pair):
        term = (grad * mapped.astype(F32)).astype(BF)
        both = dot(term, back[pair])
        return (
            (both[:, :PAIR] - scaled[:, pair_cols(pair)].astype(F32) * both[:, PAIR:]) * scale
        ).astype(BF)

    def ones_beside(values):
        return jnp.concatenate([values, jnp.ones_like(values)], axis=1)

    def first_tile(tiled):
        waits = []
        for source, target, by_rows in tiled:
            at = pl.ds(0, TILE) if by_rows else pl.ds(0, 1)
            waits.append(loads.start(source.at[at], target.at[at]))
        return waits

    def tile_load(i, source, target, by_rows, t):
        if by_rows:
            at = pl.ds(pl.multiple_of(TILE + t * TILE, TILE), TILE)
        else:
            at = pl.ds(1 + t, 1)
        return pltpu.make_async_copy(source.at[at], target.at[at], tile_sem.at[i, t])

    def query_phase(qf, gr, acc, wgrad):
        query_side = [(g_hbm, gr, True), (q_hbm, qf, True), (qs_hbm, qs, True), (n_hbm, n, False)]
        key_side = [(k_hbm, kf, True), (v_hbm, v, True), (ks_hbm, ks, True)]
        net.greet()
        wait_edge = first_tile(query_side + key_side)
        wait_edge.append(loads.start(sd_hbm.at[pl.ds(2, 2)], sd.at[pl.ds(2, 2)]))
        wait_ffn = loads.start(ffn_hbm.at[net.core], ffn)
        wait_sd = loads.start(sd_hbm.at[pl.ds(0, 2)], sd.at[pl.ds(0, 2)])

        def start_tile(t):
            for i, item in enumerate(query_side):
                tile_load(i, *item, t).start()

        for i in range(width // 16):
            at = slice(16 * i, 16 * i + 16)
            store_blocks(out_x, 16 * i, wo_grad[at].astype(BF))
        net.meet()
        out_steps[0]()
        ffn_steps[0]()
        for pair in range(pairs):
            turned = pair_projection(projection, pair).T
            own = (iota(turned.shape, 0) < FEAT) == (iota(turned.shape, 1) < PAIR // 2)
            back[pair] = jnp.concatenate([turned, jnp.where(own, 1.0, 0.0)], axis=1).astype(BF)
        for copy in wait_edge:
            copy.wait()
        for t in range(AHEAD):
            start_tile(t)
        for pair in range(pairs):
            lanes, cols = feat_lanes(pair), pair_cols(pair)
            mapped_q, mapped_k = qf[edge, lanes], kf[shorts, lanes]
            grads, values = gr[edge, grad_lanes(pair)], v[shorts, cols]
            grad_q = [
                dot(grads[batch * LONG : (batch + 1) * LONG], sd[2 + batch, pair])
                for batch in range(2)
            ]
            weight = dot_nt(grads[shorts], value_block(values, slice(0, PAIR)))
            more_q, more_k, more_v = [], [], []
            for head in range(2):
                own = slice(head * FEAT, (head + 1) * FEAT)
                part = jnp.where(same, weight[:, head * PAIR : (head + 1) * PAIR], 0.0).astype(BF)
                more_q.append(dot(part, mapped_k[:, own]))
                more_k.append(dot_tn(part, mapped_q[shorts, own]))
                more_v.append(dot_tn(small[2 * pair + head], grads[shorts, :PAIR]))
            grad_q.append(jnp.concatenate(more_q, axis=1))
            grad_k = jnp.concatenate(more_k, axis=1)
            grad_v = jnp.where(iota((2 * LONG, PAIR), 1) < PAIR // 2, more_v[0], more_v[1])
            qs[edge, cols] = feature_back(
                jnp.concatenate(grad_q, axis=0), mapped_q, qs[edge], pair
            )
            ks[shorts, cols] = feature_back(grad_k, mapped_k, ks[shorts], pair)
            v[shorts, cols] = grad_v.astype(BF)
        wgrad[...] = dot(n[0], qs[edge])
        wait_ffn.wait()
        wait_sd.wait()

        def key_load(i):
            source, target, _ = key_side[i]
            at = pl.ds(TILE, 2 * big)
            return pltpu.make_async_copy(source.at[at], target.at[at], key_sem.at[i])

        def queries(t, _):
            batch, step = lax.div(t, per), lax.rem(t, per)
            talk(comm[:count], t)
            at = pl.ds(pl.multiple_of(TILE + t * TILE, TILE), TILE)
            for i, item in enumerate(query_side):
                tile_load(i, *item, t).wait()

            @pl.when(t + AHEAD < count)
            def _():
                start_tile(t + AHEAD)

            @pl.when(t + AHEAD == count)
            def _():
                for i in range(len(key_side)):
                    key_load(i).start()

            @pl.when(step == 0)
            def _():
                acc[...] = jnp.zeros_like(acc)

            for pair in range(pairs):
                mapped = qf[at, feat_lanes(pair)]
                grads = gr[at, grad_lanes(pair)]
                acc[pair] += dot_tn(grads, mapped)
                grad = dot(grads, sd[batch, pair])
                qs[at, pair_cols(pair)] = feature_back(grad, mapped, qs[at], pair)
            wgrad[...] += dot(n[1 + t], qs[at])

            @pl.when(step == per - 1)
            def _():
                for pair in range(pairs):
                    both = acc[pair]
                    sg[batch, pair] = block_grads(both[:PAIR], norm_rows(both))

            return 0

        lax.fori_loop(0, count, queries, 0)
        for i in range(width // 16):
            at = slice(16 * i, 16 * i + 16)
            store_blocks(query_x, 16 * i, wgrad[at].astype(BF))
        for i in range(len(key_side)):
            key_load(i).wait()

    def key_phase(x, ga, wgrad):
        wait_x = [loads.start(x_hbm, x), loads.start(ga_hbm, ga)]

        def tile_at(t):
            return pl.ds(pl.multiple_of(TILE + t * TILE, TILE), TILE)

        def pack(blocks):
            for i in range(width // 16):
                at = slice(16 * i, 16 * i + 16)
                store_blocks(blocks, 16 * i, wgrad[at].astype(BF))

        def keys(t, _):
            batch = lax.div(t, per)
            talk(comm[count : 2 * count], t)
            at = tile_at(t)
            for pair in range(pairs):
                grad = dot(ones_beside(v[at, pair_cols(pair)]), sg[batch, pair])
                ks[at, pair_cols(pair)] = feature_back(grad, kf[at, feat_lanes(pair)], ks[at], pair)
            wgrad[...] += dot(n[1 + t], ks[at])
            return 0

        def values(t, _):
            batch = lax.div(t, per)
            talk(comm[2 * count : 3 * count], t)
            at = tile_at(t)
            for pair in range(pairs):
                grad = dot_nt(kf[at, feat_lanes(pair)], sg[batch, pair, :PAIR])
                v[at, pair_cols(pair)] = grad.astype(BF)
            wgrad[...] += dot(n[1 + t], v[at])
            return 0

        wgrad[...] = jnp.zeros_like(wgrad)
        lax.fori_loop(0, count, keys, 0)
        for batch in range(2):
            own = slice(batch * LONG, (batch + 1) * LONG)
            for pair in range(pairs):
                lanes, cols = feat_lanes(pair), pair_cols(pair)
                row = batch * pairs + pair
                packed = load_blocks(long_total, row * LONG, LONG, 2 * FEAT).astype(F32)
                grads = block_grads(unpack_pair(packed), long_norm[row : row + 1])
                mapped = kf[own, lanes]
                grad = dot(ones_beside(v[own, cols]), grads)
                v[own, cols] = dot_nt(mapped, grads[:PAIR]).astype(BF)
                ks[own, cols] = feature_back(grad, mapped, ks[own], pair)
        wgrad[...] += dot(n[0], ks[edge])
        pack(key_x)
        wgrad[...] = dot(n[0], v[edge])
        lax.fori_loop(0, count, values, 0)
        pack(value_x)
        for copy in wait_x:
            copy.wait()
        swap_rows(x, cuts)
        vec_held[0] = jnp.zeros(vec_held.shape[1:], F32)
        vec_held[0, 2:6] = vec_in[2:6]
        for i in range(bias_in.shape[1] // width):
            vec_held[0, 6 + i : 7 + i] = bias_in[:, i * width : (i + 1) * width]

        def last(rows_x, rows_ga, at):
            xhat, spread = normalize(rows_x)
            grad = (
                dot_nt(qs[at], wqkv[:, :width])
                + dot_nt(ks[at], wqkv[:, width : 2 * width])
                + dot_nt(v[at], wqkv[:, 2 * width :])
            )
            vec_held[0, 0:1] += jnp.sum(grad * xhat, axis=0, keepdims=True)
            vec_held[0, 1:2] += jnp.sum(grad, axis=0, keepdims=True)
            return rows_ga + norm_back(grad * gain[...], xhat, spread)

        rows_out = RowStore(x, in_grad, store_sem.at[0], TILE)

        def inputs(t, _):
            batch, step = lax.div(t, per), lax.rem(t, per)
            talk(comm[3 * count : 4 * count], t)
            raw_at = pl.ds(pl.multiple_of(LONG + step * TILE, LONG), TILE)
            at = tile_at(t)
            x[batch, raw_at] = last(x[batch, raw_at], ga[at], at)
            rows_out.tile_done(batch, step)
            return 0

        lax.fori_loop(0, count, inputs, 0)
        store_edge(x, last(edge_rows(x), ga[edge], edge))
        vec_steps[0]()
        swap_rows(x, cuts)
        rows_out.finish()
        _all(last_steps)
        totals = [
            pltpu.make_async_copy(source, target, store_sem.at[1 + i])
            for i, (source, target) in enumerate(
                (
                    (out_total, out_out), (query_total, query_out),
                    (key_total, key_out), (value_total, value_out),
                )
            )
        ]
        for total in totals:
            total.start()
        vec_out[...] = vec_held[depth + 1]
        rows_out.wait()
        for total in totals:
            total.wait()

    wide = kf.shape[1]
    pl.run_scoped(
        query_phase,
        pltpu.VMEM((inner_rows, wide), BF),
        pltpu.VMEM((inner_rows, 2 * width), BF),
        pltpu.VMEM((pairs, 2 * PAIR, 2 * FEAT), F32),
        pltpu.VMEM((width, width), F32),
    )
    pl.run_scoped(
        key_phase,
        pltpu.VMEM(x_hbm.shape, F32),
        pltpu.VMEM((inner_rows, width), F32),
        pltpu.VMEM((width, width), F32),
    )
    for item in (ffn_sum, *out_sum, *query_sum, *key_sum, *value_sum, vec_sum):
        item.drain()


def body(
    inputs,
    lengths,
    first_gain,
    first_shift,
    query_weight,
    key_weight,
    value_weight,
    output_weight,
    output_bias,
    projection,
    second_gain,
    second_shift,
    up_weight,
    up_bias,
    down_weight,
    down_bias,
    cotangent,
):
    heads, head_size, feats = projection.shape
    batches, rows, width = inputs.shape
    digits = digits_of(lax.axis_size("seq"))
    ways = 2 * math.prod(digits)
    depth = len(digits)
    pairs = heads // 2
    big = rows - 2 * LONG
    inner = TILE + batches * big
    deep, half = up_weight.shape
    hidden = up_bias.shape[0]
    part = half // CHUNKS
    down_turned = down_weight.T

    lens = lengths.reshape(batches, lengths.shape[2])
    tiles = inner // TILE
    hbm = pl.BlockSpec(memory_space=pl.ANY)
    vmem = pl.BlockSpec(memory_space=pltpu.VMEM)
    smem = pl.BlockSpec(memory_space=pltpu.SMEM)

    def shape(*dims, dtype=BF):
        return jax.ShapeDtypeStruct(dims, dtype)

    def line(vector):
        return vector.reshape(1, -1)

    wide = 2 * FEAT * pairs
    long_block = block_shape(ways, batches * pairs * LONG, 2 * FEAT)
    inner_shapes = [
        ((inner, wide), BF), ((inner, wide), BF), ((inner, width), BF), ((inner, width), BF),
        ((inner, width), BF), ((tiles, width, TILE), BF), ((inner, width), BF),
        ((inner, width), F32), ((inner, width), F32), ((4, pairs, 2 * PAIR, 2 * FEAT), BF),
        ((heads, 2 * LONG, 2 * LONG), BF), ((width, 3 * width), BF), ((width, width), BF),
    ]
    kf, qf, v, ks, qs, n, mix, inv, att, sd, small, wqkv, wo, w = pl.pallas_call(
        functools.partial(attention_forward, digits),
        out_shape=[shape(*dims, dtype=kind) for dims, kind in inner_shapes]
        + [shape(2, *digits, 2 * deep, part)],
        in_specs=[smem, hbm] + [vmem] * 3 + [hbm] * 4 + [vmem] * 3,
        out_specs=[hbm] * 14,
        scratch_shapes=[pltpu.VMEM(inputs.shape, F32)]
        + [pltpu.VMEM(dims, kind) for dims, kind in inner_shapes]
        + [
            pltpu.VMEM((pairs, PAIR, 2 * FEAT), BF),
            pltpu.VMEM((2 * deep, part), BF),
            pltpu.VMEM((batches, pairs, PAIR, 2 * FEAT), F32),
            pltpu.VMEM((batches, pairs, 1, 2 * FEAT), F32),
            pltpu.VMEM((2,) + digits + long_block, BF),
            pltpu.VMEM((2,) + digits + long_block, BF),
            pltpu.SemaphoreType.DMA((16,)),
            pltpu.SemaphoreType.DMA((14,)),
            pltpu.SemaphoreType.DMA,
            pltpu.SemaphoreType.DMA((groups(depth, 2, 2),)),
            pltpu.SemaphoreType.DMA((groups(depth, 2, 2),)),
        ]
        + Whole.scratch(digits, batches * pairs, 2 * FEAT)
        + Scatter.scratch(digits, *long_block),
        compiler_params=pltpu.CompilerParams(
            collective_id=0, has_side_effects=True, vmem_limit_bytes=VMEM_LIMIT
        ),
        name="attention_forward",
    )(
        lens, inputs, line(first_gain), line(first_shift), line(output_bias),
        query_weight, key_weight, value_weight, output_weight, projection, up_weight, down_turned,
    )

    blocks = (2,) + digits + (2 * deep, part)
    output, ga, gr, ffn, ffn_grad, wo_grad, vec_in, bias_in, long_grad, long_norm = pl.pallas_call(
        functools.partial(feed_forward, digits),
        out_shape=[
            shape(*inputs.shape, dtype=F32),
            shape(inner, width, dtype=F32),
            shape(inner, 2 * width),
            shape(*blocks),
            shape(2 * deep, part, dtype=F32),
            shape(width, width, dtype=F32),
            shape(8, width, dtype=F32),
            shape(1, hidden, dtype=F32),
            shape(2, *digits, *long_block),
            shape(batches * pairs, 2 * FEAT, dtype=F32),
        ],
        in_specs=[smem] + [hbm] * 5 + [vmem] * 6 + [hbm],
        out_specs=[hbm] * 4 + [vmem] * 6,
        scratch_shapes=[
            pltpu.VMEM(inputs.shape, F32),
            pltpu.VMEM((inner, width), F32),
            pltpu.VMEM((inner, width), BF),
            pltpu.VMEM((inner, width), F32),
            pltpu.VMEM((inner, width), BF),
            pltpu.VMEM((inner, width), F32),
            pltpu.VMEM((inner, width), F32),
            pltpu.VMEM(blocks, BF),
            pltpu.VMEM(blocks, BF),
            pltpu.VMEM((width, hidden // CHUNKS), BF),
            pltpu.VMEM((width, hidden // CHUNKS), BF),
            pltpu.VMEM((width, hidden // CHUNKS), F32),
            pltpu.VMEM((width, hidden // CHUNKS), F32),
            pltpu.VMEM((TILE, 2 * width), BF),
            pltpu.VMEM((2, big // 2, 2 * width), BF),
            pltpu.VMEM((2 * LONG, wide), BF),
            pltpu.VMEM((2,) + digits + long_block, BF),
            pltpu.VMEM((2,) + digits + long_block, BF),
            pltpu.SemaphoreType.DMA((30,)),
            pltpu.SemaphoreType.DMA((6,)),
            pltpu.SemaphoreType.DMA((groups(depth, 2, 3),)),
            pltpu.SemaphoreType.DMA((groups(depth, 2, 3),)),
        ]
        + Scatter.scratch(digits, 2 * deep, part)
        + Scatter.scratch(digits, *long_block)
        + Whole.scratch(digits, batches * pairs, 2 * FEAT),
        compiler_params=pltpu.CompilerParams(
            collective_id=1, has_side_effects=True, vmem_limit_bytes=VMEM_LIMIT
        ),
        name="feed_forward",
    )(
        lens, cotangent, att, mix, inv, w, wo, line(second_gain), line(second_shift),
        line(up_bias), up_weight, down_turned, qf,
    )

    late_block = block_shape(ways, width, width)
    late_shape = (2,) + digits + late_block
    in_grad, ffn_more, out_w, query, key, value, vectors = pl.pallas_call(
        functools.partial(attention_backward, digits),
        out_shape=[
            shape(*inputs.shape, dtype=F32),
            shape(2 * deep, part, dtype=F32),
            shape(*late_shape),
            shape(*late_shape),
            shape(*late_shape),
            shape(*late_shape),
            shape(16, width, dtype=F32),
        ],
        in_specs=[smem] + [hbm] * 10 + [vmem, hbm] + [vmem] * 8,
        out_specs=[hbm, vmem, hbm, hbm, hbm, hbm, vmem],
        scratch_shapes=[
            pltpu.VMEM((inner, wide), BF),
            pltpu.VMEM((inner, width), BF),
            pltpu.VMEM((inner, width), BF),
            pltpu.VMEM((inner, width), BF),
            pltpu.VMEM((tiles, width, TILE), BF),
            pltpu.VMEM((4, pairs, 2 * PAIR, 2 * FEAT), BF),
            pltpu.VMEM((batches, pairs, 2 * PAIR, 2 * FEAT), BF),
            pltpu.VMEM((pairs, 2 * FEAT, 2 * PAIR), BF),
            pltpu.VMEM(blocks[1:], BF),
        ]
        + [pltpu.VMEM(late_shape, BF)] * 8
        + [
            pltpu.SemaphoreType.DMA((12,)),
            pltpu.SemaphoreType.DMA((4, tiles - 1)),
            pltpu.SemaphoreType.DMA((3,)),
            pltpu.SemaphoreType.DMA((5,)),
            pltpu.SemaphoreType.DMA((groups(depth, 4, 6),)),
            pltpu.SemaphoreType.DMA((groups(depth, 4, 6),)),
        ]
        + Scatter.scratch(digits, 2 * deep, part)
        + Scatter.scratch(digits, *late_block) * 4
        + Whole.scratch(digits, 16, width),
        compiler_params=pltpu.CompilerParams(
            collective_id=2, has_side_effects=True, vmem_limit_bytes=VMEM_LIMIT
        ),
        name="attention_backward",
    )(
        lens, inputs, ga, gr, kf, qf, v, ks, qs, n, sd, small, ffn,
        wo_grad, vec_in, bias_in, long_grad, long_norm, line(first_gain), wqkv, projection,
    )

    def whole(blocks):
        lanes = blocks.shape[-1]
        if lanes != width:
            blocks = blocks.reshape(width // 16, width // lanes, 16, lanes)
            blocks = jnp.swapaxes(blocks, 1, 2)
        return blocks.reshape(width, width).astype(F32)

    ffn_all = jnp.concatenate([ffn_grad, ffn_more], axis=1)
    return (
        output + down_bias,
        in_grad,
        vectors[0],
        vectors[1],
        whole(query),
        whole(key),
        whole(value),
        whole(out_w),
        vectors[2],
        vectors[3],
        vectors[4],
        ffn_all[:deep],
        vectors[6 : 6 + hidden // width].reshape(hidden),
        ffn_all[deep:].T,
        vectors[5],
    )


def solution(mesh):
    rows = P(None, ("seq", "ffn"), None)
    up, down = P("seq", "ffn"), P("ffn", "seq")
    in_specs = (rows, rows) + (P(),) * 10 + (up, P(), down, P(), rows)
    out_specs = (rows, rows) + (P(),) * 9 + (up, P(), down, P())
    return jax.shard_map(body, mesh=mesh, in_specs=in_specs, out_specs=out_specs, check_vma=False)
```

```python
import functools
import math

import jax
import jax.numpy as jnp
from jax import lax
from jax.experimental import pallas as pl
from jax.experimental.pallas import tpu as pltpu
from jax.sharding import PartitionSpec as P

BF, F32 = jnp.bfloat16, jnp.float32
EPS = 1e-5
LONG = 64
TILE = 256
PAIR = 128
AHEAD = 3
CHUNKS = 2
FEAT = 256
VMEM_LIMIT = 63 << 20
LOG16 = math.log(16.0)


def dot(a, b):
    return jnp.dot(a, b, preferred_element_type=F32)


def dot_nt(a, b):
    return lax.dot_general(a, b, (((1,), (1,)), ((), ())), preferred_element_type=F32)


def dot_tn(a, b):
    return lax.dot_general(a, b, (((0,), (0,)), ((), ())), preferred_element_type=F32)


def iota(shape, dim):
    return lax.broadcasted_iota(jnp.int32, shape, dim)


def normalize(rows):
    mean = jnp.mean(rows, axis=-1, keepdims=True)
    centred = rows - mean
    spread = jnp.mean(centred * centred, axis=-1, keepdims=True)
    scale = lax.rsqrt(spread + EPS)
    return centred * scale, scale


def norm_back(grad, xhat, scale):
    return scale * (
        grad
        - jnp.mean(grad, axis=-1, keepdims=True)
        - xhat * jnp.mean(grad * xhat, axis=-1, keepdims=True)
    )


def head_sums(pair):
    first = iota(pair.shape, 1) < PAIR // 2
    zero = jnp.zeros_like(pair)
    return (
        jnp.sum(jnp.where(first, pair, zero), axis=-1, keepdims=True),
        jnp.sum(jnp.where(first, zero, pair), axis=-1, keepdims=True),
    )


def features(scaled, scaled_low, proj, pair):
    cols = slice(pair * PAIR, (pair + 1) * PAIR)
    part = scaled[:, cols]
    first, second = head_sums(part * part)
    product = dot(scaled_low[:, cols], proj[pair])
    return jnp.concatenate(
        [
            jnp.exp(product[:, :FEAT] - (0.5 * first + LOG16)).astype(BF),
            jnp.exp(product[:, FEAT:] - (0.5 * second + LOG16)).astype(BF),
        ],
        axis=1,
    )


def lane_half(shape):
    return iota(shape, 1) < FEAT


def block_sums(both, norm):
    keep = (iota((PAIR, 2 * FEAT), 0) < PAIR // 2) == lane_half((PAIR, 2 * FEAT))
    zero = jnp.zeros((PAIR, 2 * FEAT), F32)
    return jnp.concatenate(
        [
            jnp.where(keep, both, zero).astype(BF),
            jnp.where(keep, jnp.broadcast_to(norm, (PAIR, 2 * FEAT)), zero).astype(BF),
        ],
        axis=0,
    )


def block_grads(both, norm):
    keep = (iota((PAIR, 2 * FEAT), 0) < PAIR // 2) == lane_half((PAIR, 2 * FEAT))
    zero = jnp.zeros((PAIR, 2 * FEAT), F32)
    row = iota((PAIR, 2 * FEAT), 0)
    high = norm.astype(BF).astype(F32)
    wide = jnp.broadcast_to(high, (PAIR, 2 * FEAT))
    rest = jnp.broadcast_to(norm - high, (PAIR, 2 * FEAT))
    return jnp.concatenate(
        [
            jnp.where(keep, both, zero).astype(BF),
            jnp.where(row == 0, wide, jnp.where(row == 1, rest, zero)).astype(BF),
        ],
        axis=0,
    )


def pack_pair(both):
    return jnp.where(lane_half((PAIR // 2, 2 * FEAT)), both[: PAIR // 2], both[PAIR // 2 :])


def norm_rows(both):
    return jnp.where(
        lane_half((1, 2 * FEAT)),
        jnp.sum(both[PAIR : PAIR + PAIR // 2], axis=0, keepdims=True),
        jnp.sum(both[PAIR + PAIR // 2 :], axis=0, keepdims=True),
    )


def unpack_pair(packed):
    return jnp.concatenate([packed, packed], axis=0)


def value_block(values, cols):
    part = values[:, cols]
    first = iota(part.shape, 1) < PAIR // 2
    zero = jnp.zeros_like(part)
    one = jnp.ones_like(part)
    top = jnp.concatenate([jnp.where(first, part, zero), jnp.where(first, one, zero)], axis=1)
    low = jnp.concatenate([jnp.where(first, zero, part), jnp.where(first, zero, one)], axis=1)
    return jnp.concatenate([top, low], axis=0)


def same_small(bounds):
    shape = (2 * LONG, 2 * LONG)

    def label(dim):
        at = iota(shape, dim)
        cut = jnp.where(at < LONG, bounds[0], LONG + bounds[1])
        return jnp.where(at < cut, 1, 0) + jnp.where(at < LONG, 0, 2)

    return label(0) == label(1)


def cuts_of(lens, big):
    cuts, bounds = [], []
    for batch in range(2):
        first, second = lens[batch, 0], lens[batch, 1]
        behind = jnp.where(second == big, first, first + second)
        cuts.append(jnp.where(first == big, 0, behind))
        bounds.append(jnp.where(first == big, second, first))
    return cuts, bounds


def swap_rows(buffer, cuts):
    most = buffer.shape[1]
    width = buffer.shape[2]
    for batch in range(2):
        head = buffer[batch, LONG : 2 * LONG]
        tail = buffer[batch, most - LONG :]
        small_first = iota((LONG, width), 0) < cuts[batch]
        buffer[batch, LONG : 2 * LONG] = jnp.where(small_first, tail, head)
        buffer[batch, most - LONG :] = jnp.where(small_first, head, tail)


class RowStore:
    def __init__(self, buffer, out, semaphore, tile):
        self.buffer, self.out, self.semaphore, self.tile = buffer, out, semaphore, tile

    def start(self, batch, at):
        pltpu.make_async_copy(
            self.buffer.at[batch, at], self.out.at[batch, at], self.semaphore
        ).start()

    def tile_done(self, batch, step):
        first = LONG + step * self.tile
        self.start(batch, pl.ds(pl.multiple_of(first + LONG, LONG), self.tile - LONG))

        @pl.when(step > 0)
        def _():
            self.start(batch, pl.ds(pl.multiple_of(first, LONG), LONG))

    def finish(self):
        rows = self.buffer.shape[1]
        for batch in range(2):
            self.start(batch, pl.ds(0, 2 * LONG))
            self.start(batch, pl.ds(rows - LONG, LONG))

    def wait(self):
        pltpu.make_async_copy(self.buffer, self.out, self.semaphore).wait()


def edge_rows(buffer):
    most = buffer.shape[1]
    return jnp.concatenate(
        [
            buffer[0, :LONG],
            buffer[1, :LONG],
            buffer[0, most - LONG :],
            buffer[1, most - LONG :],
        ],
        axis=0,
    )


def store_edge(buffer, value):
    most = buffer.shape[1]
    buffer[0, :LONG] = value[:LONG]
    buffer[1, :LONG] = value[LONG : 2 * LONG]
    buffer[0, most - LONG :] = value[2 * LONG : 3 * LONG]
    buffer[1, most - LONG :] = value[3 * LONG :]


def digits_of(size):
    out = []
    while size > 1:
        step = 4 if size % 4 == 0 else size
        out.append(step)
        size //= step
    return tuple(out)


class Net:
    def __init__(self, digits, send, recv):
        self.digits = digits
        self.send, self.recv = send, recv
        self.me = lax.axis_index("seq")
        self.core = lax.axis_index("ffn")
        self.slots = {}
        strides = [math.prod(digits[k + 1 :]) for k in range(len(digits))]
        self.own = [lax.rem(lax.div(self.me, s), n) for s, n in zip(strides, digits)]
        self.strides = strides

    def partner(self):
        return (self.me, 1 - self.core)

    def other(self, k, step):
        return lax.rem(self.own[k] + step, self.digits[k])

    def peer(self, k, step):
        return (self.me + (self.other(k, step) - self.own[k]) * self.strides[k], self.core)

    def greet(self):
        semaphore = pltpu.get_barrier_semaphore()
        peers = [self.partner()] + [
            self.peer(k, step) for k, n in enumerate(self.digits) for step in range(1, n)
        ]
        for peer in peers:
            pl.semaphore_signal(
                semaphore, inc=1, device_id=peer, device_id_type=pl.DeviceIdType.MESH
            )

    def meet(self):
        pl.semaphore_wait(
            pltpu.get_barrier_semaphore(), 1 + sum(n - 1 for n in self.digits)
        )

    def copy(self, key, source, target, device):
        slot = self.slots.setdefault(key, len(self.slots))
        return pltpu.make_async_remote_copy(
            src_ref=source,
            dst_ref=target,
            send_sem=self.send.at[slot],
            recv_sem=self.recv.at[slot],
            device_id=device,
            device_id_type=pl.DeviceIdType.MESH,
        )

    def group(self, key, size):
        return self.copy(key, size, size, self.partner())


def groups(depth, gathers, others):
    return gathers * (depth + 1) * (depth + 2) // 2 + others * (depth + 1)


class Gather:
    def __init__(self, net, name, out):
        self.net, self.name, self.out = net, name, out

    def fresh(self, j):
        net = self.net
        if j == 0:
            return [(net.core,) + tuple(net.own)]
        lead = (net.core,) + (slice(None),) * (j - 1)
        return [
            lead + (net.other(j - 1, step),) + tuple(net.own[j:])
            for step in range(1, net.digits[j - 1])
        ]

    def copies(self, j, k):
        net = self.net
        depth = len(net.digits)
        copies = []
        for at in self.fresh(j):
            block = self.out.at[at]
            if k == depth:
                copies.append(net.copy((self.name, j, k), block, block, net.partner()))
                continue
            for step in range(1, net.digits[k]):
                copies.append(net.copy((self.name, j, k), block, block, net.peer(k, step)))
        return copies

    def group(self, j, k):
        digits = self.net.digits
        at = [0] * (1 + len(digits))
        if j:
            at[1:j] = [slice(None)] * (j - 1)
            at[j] = pl.ds(0, digits[j - 1] - 1)
        if k < len(digits):
            at[1 + k] = pl.ds(0, digits[k] - 1)
        return self.net.group((self.name, j, k), self.out.at[tuple(at)])

    def steps(self):
        depth = len(self.net.digits)

        def run(j):
            for i in range(j):
                self.group(i, j - 1).wait_recv()
            for k in range(j, depth + 1):
                for copy in self.copies(j, k):
                    copy.start()

        def last():
            for j in range(depth + 1):
                self.group(j, depth).wait_recv()

        return [functools.partial(run, j) for j in range(depth + 1)] + [last]

    def drain(self):
        depth = len(self.net.digits)
        for j in range(depth + 1):
            for k in range(j, depth + 1):
                self.group(j, k).wait_send()


class Scatter:
    def __init__(self, net, name, blocks, first, slots, parts, finish, apart=None):
        self.net, self.name = net, name
        self.away = (blocks if apart is None else apart).at[1 - net.core]
        self.held = blocks.at[net.core] if apart is None else blocks
        self.first, self.slots, self.parts, self.finish = first, slots, parts, finish

    @staticmethod
    def scratch(digits, rows, cols):
        shapes = [pltpu.VMEM(digits + (rows, cols), BF)]
        for k in reversed(range(len(digits))):
            shapes.append(pltpu.VMEM((digits[k] - 1,) + digits[:k] + (rows, cols), BF))
        for k in reversed(range(1, len(digits))):
            shapes.append(pltpu.VMEM(digits[:k] + (rows, cols), BF))
        return shapes

    @classmethod
    def of(cls, net, name, blocks, refs, finish, apart=None):
        depth = len(net.digits)
        slots, parts = refs[1 : 1 + depth], refs[1 + depth :]
        return cls(net, name, blocks, refs[0], slots, parts, finish, apart)

    def copies(self, k):
        net = self.net
        depth = len(net.digits)
        if k == 0:
            return [net.copy((self.name, 0), self.away, self.first, net.partner())]
        digit = depth - k
        held = self.held if k == 1 else self.parts[k - 2]
        copies = []
        for step in range(1, net.digits[digit]):
            at = (slice(None),) * digit + (net.other(digit, step),)
            copies.append(
                net.copy(
                    (self.name, k),
                    held.at[at],
                    self.slots[k - 1].at[step - 1],
                    net.peer(digit, step),
                )
            )
        return copies

    def group(self, k):
        return self.net.group((self.name, k), self.slots[k - 1] if k else self.first)

    def add(self, k):
        net = self.net
        depth = len(net.digits)
        if k == 0:
            lead = net.digits
            for at in _indices(lead):
                mine = self.held[at].astype(F32)
                self.held[at] = (mine + self.first[at].astype(F32)).astype(BF)
            return
        digit = depth - k
        held = self.held if k == 1 else self.parts[k - 2]
        for at in _indices(net.digits[:digit]):
            total = held[at + (net.own[digit],)].astype(F32)
            for step in range(net.digits[digit] - 1):
                total = total + self.slots[k - 1][(step,) + at].astype(F32)
            if digit:
                self.parts[k - 1][at] = total.astype(BF)
            else:
                self.finish(total)

    def steps(self):
        depth = len(self.net.digits)

        def start(k):
            for copy in self.copies(k):
                copy.start()

        def follow(k):
            self.group(k - 1).wait_recv()
            self.add(k - 1)
            if k <= depth:
                start(k)

        return [functools.partial(start, 0)] + [
            functools.partial(follow, k) for k in range(1, depth + 2)
        ]

    def drain(self):
        for k in range(len(self.net.digits) + 1):
            self.group(k).wait_send()


def _indices(lead):
    if not lead:
        return [()]
    return [(i,) + rest for i in range(lead[0]) for rest in _indices(lead[1:])]


class Whole:
    def __init__(self, net, name, held, slots):
        self.net, self.name, self.held, self.slots = net, name, held, slots

    @staticmethod
    def scratch(digits, rows, cols):
        return [
            pltpu.VMEM((len(digits) + 2, rows, cols), F32),
            pltpu.VMEM((1 + sum(n - 1 for n in digits), rows, cols), F32),
        ]

    def span(self, k):
        digits = self.net.digits
        return (0, 1) if k == 0 else (1 + sum(n - 1 for n in digits[: k - 1]), digits[k - 1] - 1)

    def copies(self, k):
        net = self.net
        source = self.held.at[k]
        first, number = self.span(k)
        peers = [net.partner()] if k == 0 else [net.peer(k - 1, 1 + i) for i in range(number)]
        return [
            net.copy((self.name, k), source, self.slots.at[first + i], peer)
            for i, peer in enumerate(peers)
        ]

    def group(self, k):
        return self.net.group((self.name, k), self.slots.at[pl.ds(*self.span(k))])

    def steps(self):
        depth = len(self.net.digits)

        def start(k):
            for copy in self.copies(k):
                copy.start()

        def follow(k):
            self.group(k - 1).wait_recv()
            total = self.held[k - 1]
            first, number = self.span(k - 1)
            for i in range(number):
                total = total + self.slots[first + i]
            self.held[k] = total
            if k <= depth:
                start(k)

        return [functools.partial(start, 0)] + [
            functools.partial(follow, k) for k in range(1, depth + 2)
        ]

    def drain(self):
        for k in range(len(self.net.digits) + 1):
            self.group(k).wait_send()


def together(*parts):
    most = max(len(part) for part in parts)

    def run(i):
        for part in parts:
            if i < len(part):
                part[i]()

    return [functools.partial(run, i) for i in range(most)]


def block_shape(ways, rows, cols):
    lanes = cols * (rows // 16) // ways
    return 16, lanes


def block_at(digits, index):
    at = []
    for n in reversed(digits):
        at.append(index % n)
        index //= n
    return tuple(reversed(at))


def store_blocks(blocks, row, value):
    lanes = blocks.shape[-1]
    per_row = value.shape[1] // lanes
    ways = (2,) + blocks.shape[1:-2]
    for i in range(value.shape[0] // 16):
        for j in range(per_row):
            at = block_at(ways, (row // 16 + i) * per_row + j)
            blocks[at] = value[16 * i : 16 * i + 16, j * lanes : (j + 1) * lanes]


def load_blocks(blocks, row, rows, cols):
    lanes = blocks.shape[-1]
    per_row = cols // lanes
    ways = (2,) + blocks.shape[1:-2]
    out = []
    for i in range(rows // 16):
        line = [
            blocks[block_at(ways, (row // 16 + i) * per_row + j)] for j in range(per_row)
        ]
        out.append(line[0] if per_row == 1 else jnp.concatenate(line, axis=1))
    return jnp.concatenate(out, axis=0)


class Loads:
    def __init__(self, semaphores):
        self.semaphores = semaphores
        self.count = 0

    def start(self, source, target):
        copy = pltpu.make_async_copy(source, target, self.semaphores.at[self.count])
        self.count += 1
        copy.start()
        return copy


PIECES = ((0, 128), (1088, 64), (128, 192), (320, 256), (576, 256), (832, 256))


def raw_pieces(rows):
    quarter = (rows - 2 * LONG) // 4
    pieces = [(0, 2 * LONG), (rows - LONG, LONG), (2 * LONG, quarter - LONG)]
    return pieces + [(LONG + quarter * i, quarter) for i in range(1, 4)]


def big_start(batch, rows_big, step, tile):
    return TILE + batch * rows_big + step * tile


def pair_projection(projection, pair):
    first, second = projection[2 * pair], projection[2 * pair + 1]
    gap = jnp.zeros_like(first)
    return jnp.concatenate(
        [jnp.concatenate([first, gap], axis=1), jnp.concatenate([gap, second], axis=1)], axis=0
    )


def place(steps, spots, count):
    lists = [[] for _ in range(count)]
    for step, spot in zip(steps, spots, strict=True):
        lists[spot].append(step)
    return lists


def spots(known, number):
    if number == len(known):
        return list(known)
    last = len(known) - 1
    return [known[min(last, -(-i * last // max(1, number - 1)))] for i in range(number)]


def side_by_side(chains):
    most = max(len(chain) for chain in chains)
    return [
        chain[i - most] for i in range(most) for chain in chains if i >= most - len(chain)
    ]


def talk(lists, t):
    for i, steps in enumerate(lists):
        if steps:
            pl.when(t == i)(functools.partial(_all, steps))


def _all(steps):
    for step in steps:
        step()


def all_reduce(scatter, spread):
    first, second = scatter.steps(), spread.steps()
    return first[:-1] + [functools.partial(_both, first[-1], second[0])] + second[1:]


def weight_block(up, down, chunk):
    half = up.shape[1] // CHUNKS
    at = slice(chunk * half, (chunk + 1) * half)
    return jnp.concatenate([up[:, at], down[:, at]], axis=0).astype(BF)


def attention_forward(
    digits, lens, x_hbm, gain, shift, bias, wq_hbm, wk_hbm, wv_hbm, wo_hbm, projection, up, down,
    k_out, q_out, v_out, ks_out, qs_out, n_out, mix_out, inv_out, att_out, sd_out, small_out,
    wqkv_out, wo_out, w_out,
    x, kf, qf, v, ks, qs, n, mix, inv, att, sd, small, wqkv, wo, proj, block, acc, nacc, parts,
    total, load_sem, store_sem, own_sem, send, recv, whole_held, whole_slots, *slots,
):
    rows = x.shape[1]
    big = rows - 2 * LONG
    pairs = proj.shape[0]
    width = wo.shape[0]
    scale = (PAIR // 2) ** -0.25
    depth = len(digits)
    net = Net(digits, send, recv)
    loads = Loads(load_sem)
    pieces = raw_pieces(rows)
    pending = {}

    def load_rows(some):
        for piece in some:
            for batch in range(2):
                span = pl.ds(*piece)
                pending[batch, piece] = loads.start(x_hbm.at[batch, span], x.at[batch, span])

    load_rows(pieces[:2])
    weights = [
        loads.start(source, att.at[pl.ds(i * width, width)])
        for i, source in enumerate((wq_hbm, wk_hbm, wv_hbm, wo_hbm))
    ]
    net.greet()
    block[...] = weight_block(up, down, 0)
    own_block = pltpu.make_async_copy(block, w_out.at[(net.core,) + tuple(net.own)], own_sem)
    own_block.start()
    for pair in range(pairs):
        proj[pair] = pair_projection(projection, pair).astype(BF)
    own_block.wait()
    net.meet()
    gather = Gather(net, "w", w_out)
    gather_steps = gather.steps()
    gather_steps[0]()

    def finish(value):
        total[(net.core,) + tuple(net.own)] = value.astype(BF)

    scatter = Scatter.of(net, "s", parts, slots, finish)
    spread = Gather(net, "t", total)
    whole = Whole(net, "n", whole_held, whole_slots)
    sum_steps = together(all_reduce(scatter, spread), whole.steps())
    cuts, bounds = cuts_of(lens, big)
    for i, copy in enumerate(weights):
        copy.wait()
        rounded = att[i * width : (i + 1) * width].astype(BF)
        if i < 3:
            wqkv[:, i * width : (i + 1) * width] = rounded
        else:
            wo[...] = rounded

    def front(rows_x, tile):
        xhat, _ = normalize(rows_x)
        low = (xhat * gain[...] + shift[...]).astype(BF)
        n[tile] = low.T
        raw = dot(low, wqkv[...])
        q = raw[:, :width] * scale
        k = raw[:, width : 2 * width] * scale
        return q, k, raw[:, 2 * width :].astype(BF)

    def attend(numer_denom, at, pair):
        cols = slice(pair * PAIR, (pair + 1) * PAIR)
        inverse = 1.0 / numer_denom[:, PAIR:]
        inv[at, cols] = inverse
        mix[at, cols] = (numer_denom[:, :PAIR] * inverse).astype(BF)

    load_rows(pieces[2:])
    for piece in pieces[:2]:
        for batch in range(2):
            pending[batch, piece].wait()
    swap_rows(x, cuts)
    edge = slice(0, TILE)
    q, k, values = front(edge_rows(x), 0)
    v[edge] = values
    k_low = k.astype(BF)
    ks[edge] = k_low
    for pair in range(pairs):
        cols = slice(pair * PAIR, (pair + 1) * PAIR)
        feats = slice(pair * 2 * FEAT, (pair + 1) * 2 * FEAT)
        mapped = features(k, k_low, proj, pair)
        kf[edge, feats] = mapped
        for batch in range(2):
            own = slice(batch * LONG, (batch + 1) * LONG)
            both = dot_tn(values[own, cols], mapped[own])
            row = batch * pairs + pair
            store_blocks(parts, row * LONG, pack_pair(both).astype(BF))
            whole_held[0, row : row + 1] = jnp.sum(mapped[own].astype(F32), axis=0, keepdims=True)
    sum_steps[0]()
    q_low = q.astype(BF)
    qs[edge] = q_low
    same = same_small(bounds)
    shorts = slice(2 * LONG, TILE)
    for pair in range(pairs):
        cols = slice(pair * PAIR, (pair + 1) * PAIR)
        feats = slice(pair * 2 * FEAT, (pair + 1) * 2 * FEAT)
        mapped = features(q, q_low, proj, pair)
        qf[edge, feats] = mapped
        scores = []
        for head in range(2):
            lanes = slice((2 * pair + head) * FEAT, (2 * pair + head + 1) * FEAT)
            score = dot_nt(
                mapped[shorts, head * FEAT : (head + 1) * FEAT], kf[shorts, lanes]
            )
            score = jnp.where(same, score, 0.0).astype(BF)
            small[2 * pair + head] = score
            scores.append(score)
        attend(
            dot(jnp.concatenate(scores, axis=1), value_block(values[shorts], cols)), shorts, pair
        )

    def store(source, target, at, slot):
        pltpu.make_async_copy(source.at[at], target.at[at], store_sem.at[slot]).start()

    first_pass = ((kf, k_out), (qf, q_out), (v, v_out), (ks, ks_out), (qs, qs_out), (n, n_out))
    second_pass = ((mix, mix_out), (inv, inv_out), (att, att_out))
    once = ((small, small_out), (wqkv, wqkv_out), (wo, wo_out))

    def store_first(at, tile):
        for slot, (source, target) in enumerate(first_pass):
            store(source, target, tile if source is n else at, slot)

    def store_second(at):
        for slot, (source, target) in enumerate(second_pass):
            store(source, target, at, len(first_pass) + slot)

    def whole_copy(i):
        slot = len(first_pass) + len(second_pass) + i
        return pltpu.make_async_copy(*once[i], store_sem.at[slot])

    store_first(pl.ds(0, TILE), 0)
    for i in range(3):
        whole_copy(i).start()
    for piece in pieces[2:]:
        for batch in range(2):
            pending[batch, piece].wait()
    acc[...] = jnp.zeros_like(acc)
    nacc[...] = jnp.zeros_like(nacc)
    per = big // TILE
    count = 2 * per
    comm = place(
        sum_steps[1:] + gather_steps[1:],
        spots((1, 3, 5, 7, count + 2, count + 6), len(sum_steps) - 1)
        + spots((3, count, count + 4), len(gather_steps) - 1),
        2 * count,
    )

    def pass_one(t, _):
        batch, step = lax.div(t, per), lax.rem(t, per)
        talk(comm[:count], t)
        raw_at = pl.ds(pl.multiple_of(LONG + step * TILE, LONG), TILE)
        at = pl.ds(pl.multiple_of(TILE + t * TILE, TILE), TILE)
        q, k, values = front(x[batch, raw_at], 1 + t)
        v[at] = values
        k_low = k.astype(BF)
        q_low = q.astype(BF)
        ks[at] = k_low
        qs[at] = q_low
        for pair in range(pairs):
            cols = slice(pair * PAIR, (pair + 1) * PAIR)
            feats = slice(pair * 2 * FEAT, (pair + 1) * 2 * FEAT)
            mapped = features(k, k_low, proj, pair)
            kf[at, feats] = mapped
            acc[batch, pair] += dot_tn(values[:, cols], mapped)
            nacc[batch, pair] += jnp.sum(mapped.astype(F32), axis=0, keepdims=True)
            qf[at, feats] = features(q, q_low, proj, pair)
        store_first(at, 1 + t)
        return 0

    lax.fori_loop(0, count, pass_one, 0)
    for batch in range(2):
        for pair in range(pairs):
            sd[batch, pair] = block_sums(acc[batch, pair], nacc[batch, pair])

    sd_copies = [
        pltpu.make_async_copy(sd.at[pl.ds(i, 2)], sd_out.at[pl.ds(i, 2)], store_sem.at[12 + i // 2])
        for i in (0, 2)
    ]
    sd_copies[0].start()

    def pass_two(t, _):
        batch, step = lax.div(t, per), lax.rem(t, per)
        talk(comm[count:], t)
        raw_at = pl.ds(pl.multiple_of(LONG + step * TILE, LONG), TILE)
        at = pl.ds(pl.multiple_of(TILE + t * TILE, TILE), TILE)
        for pair in range(pairs):
            feats = slice(pair * 2 * FEAT, (pair + 1) * 2 * FEAT)
            attend(dot_nt(qf[at, feats], sd[batch, pair]), at, pair)
        att[at] = x[batch, raw_at] + dot(mix[at], wo[...]) + bias[...]
        store_second(at)
        return 0

    lax.fori_loop(0, count, pass_two, 0)
    for batch in range(2):
        own = slice(batch * LONG, (batch + 1) * LONG)
        for pair in range(pairs):
            feats = slice(pair * 2 * FEAT, (pair + 1) * 2 * FEAT)
            row = batch * pairs + pair
            packed = load_blocks(total, row * LONG, LONG, 2 * FEAT).astype(F32)
            sd[2 + batch, pair] = block_sums(
                unpack_pair(packed), whole_held[depth + 1, row : row + 1]
            )
            attend(dot_nt(qf[own, feats], sd[2 + batch, pair]), own, pair)
    att[edge] = edge_rows(x) + dot(mix[edge], wo[...]) + bias[...]
    store_second(pl.ds(0, TILE))
    sd_copies[1].start()
    for slot, (source, target) in enumerate(first_pass + second_pass):
        pltpu.make_async_copy(source, target, store_sem.at[slot]).wait()
    for i in range(len(once)):
        whole_copy(i).wait()
    for copy in sd_copies:
        copy.wait()
    gather.drain()
    scatter.drain()
    spread.drain()
    whole.drain()


def _both(first, second):
    first()
    second()


def feed_forward(
    digits, lens, cot_hbm, att_hbm, mix_hbm, inv_hbm, w_hbm, wo, gain, shift, down_bias, up_bias,
    up_own, down_own, q_hbm,
    out_hbm, ga_out, g_out, x_out, ffn_out, wo_grad, vec_grad, bias_grad, long_out, norm_out,
    cot, att, mix, inv, second, branch, grad_second, w_first, w_second, up, down, dup, ddown,
    gr_edge, gr, qf, parts, long_total, load_sem, store_sem, send, recv, *refs,
):
    rows = cot.shape[1]
    big = rows - 2 * LONG
    width = wo.shape[0]
    pairs = width // PAIR
    tile = big // 2
    per = big // tile
    count = 2 * per
    depth = len(digits)
    cuts, _ = cuts_of(lens, big)
    net = Net(digits, send, recv)
    net.greet()
    loads = Loads(load_sem)
    deep = w_first.shape[-2] // 2
    half = w_first.shape[-1]
    wait_w = loads.start(w_hbm, w_first)
    pieces = raw_pieces(rows)
    inner = [(0, TILE)] + [(TILE + tile * i, tile) for i in range(count)]

    def load_cot(some):
        return [
            loads.start(cot_hbm.at[batch, pl.ds(*piece)], cot.at[batch, pl.ds(*piece)])
            for piece in some
            for batch in range(2)
        ]

    def load_inner(source, target, some):
        return [loads.start(source.at[pl.ds(*p)], target.at[pl.ds(*p)]) for p in some]

    first_waits = load_inner(att_hbm, att, inner[:1]) + load_cot(pieces[:2])
    w_second[(net.core,) + tuple(net.own)] = weight_block(up_own, down_own, 1)
    net.meet()
    gather = Gather(net, "w", w_second)
    gather_steps = gather.steps()
    gather_steps[0]()

    def finish(value):
        ffn_out[...] = value

    scatter = Scatter.of(net, "f", w_first, refs[: 2 * depth], finish)
    scatter_steps = scatter.steps()

    def finish_long(value):
        long_total[(net.core,) + tuple(net.own)] = value.astype(BF)

    long_scatter = Scatter.of(net, "s", parts, refs[2 * depth : 4 * depth], finish_long)
    long_spread = Gather(net, "t", long_total)
    norm_held, norm_slots = refs[4 * depth :]
    norm_sum = Whole(net, "n", norm_held, norm_slots)
    long_steps = together(all_reduce(long_scatter, long_spread), norm_sum.steps())
    members = _indices(digits)
    group = max(1, 16 // deep)

    def unpack(w):
        for core in range(2):
            cols = slice(core * half, (core + 1) * half)
            for first in range(0, len(members), group):
                parts = [w[(core,) + members[first + i]] for i in range(group)]
                at = slice(first * deep, (first + group) * deep)
                if group == 1:
                    up[at, cols] = parts[0][:deep]
                    down[at, cols] = parts[0][deep:]
                else:
                    up[at, cols] = jnp.concatenate([part[:deep] for part in parts], axis=0)
                    down[at, cols] = jnp.concatenate([part[deep:] for part in parts], axis=0)

    def pack(w):
        for core in range(2):
            cols = slice(core * half, (core + 1) * half)
            for i, member in enumerate(members):
                at = slice(i * deep, (i + 1) * deep)
                w[(core,) + member] = jnp.concatenate(
                    [dup[at, cols], ddown[at, cols]], axis=0
                ).astype(BF)

    def bias_lanes(chunk):
        return [
            slice((CHUNKS * core + chunk) * half, (CHUNKS * core + chunk + 1) * half)
            for core in range(2)
        ]

    def add_row(at, value):
        vec_grad[at : at + 1] += jnp.sum(value, axis=0, keepdims=True)

    def hidden_part(chunk, second_low, grad_low):
        bias = jnp.concatenate([up_bias[:, lanes] for lanes in bias_lanes(chunk)], axis=1)
        hidden = dot(second_low, up[...]) + bias
        gauss = jnp.exp(-0.5 * hidden * hidden) * (1.0 / math.sqrt(2.0 * math.pi))
        cdf = 0.5 + 0.5 * lax.erf(hidden * math.sqrt(0.5))
        active = (hidden * cdf).astype(BF)
        slope = cdf + hidden * gauss
        grad_hidden = (dot(grad_low, down[...]) * slope).astype(BF)
        dup[...] += dot(second_low.T, grad_hidden)
        ddown[...] += dot(grad_low.T, active)
        bias_sum = jnp.sum(grad_hidden.astype(F32), axis=0, keepdims=True)
        for core, lanes in enumerate(bias_lanes(chunk)):
            bias_grad[:, lanes] += bias_sum[:, core * half : (core + 1) * half]
        return dot_nt(active, down[...]), dot_nt(grad_hidden, up[...])

    def first_block(at, grad_out):
        xhat, _ = normalize(att[at])
        low = (xhat * gain[...] + shift[...]).astype(BF)
        second[at] = low
        branch[at], grad_second[at] = hidden_part(0, low, grad_out.astype(BF))

    def second_block(at, grad_out, put, between=lambda: None):
        more, grad_more = hidden_part(1, second[at], grad_out.astype(BF))
        between()
        att_rows = att[at]
        xhat, scale = normalize(att_rows)
        output = att_rows + (branch[at] + more) + down_bias[...]
        grad = grad_second[at] + grad_more
        grad_att = grad_out + norm_back(grad * gain[...], xhat, scale)
        add_row(2, grad_att)
        add_row(3, grad * xhat)
        add_row(4, grad)
        add_row(5, grad_out)
        grad_att_low = grad_att.astype(BF)
        mixed = mix[at]
        wo_grad[...] += dot_tn(mixed, grad_att_low)
        grad_mixed = dot_nt(grad_att_low, wo[...]).astype(BF).astype(F32)
        for pair in range(pairs):
            cols = slice(pair * PAIR, (pair + 1) * PAIR)
            part = grad_mixed[:, cols]
            inverse = inv[at, cols]
            first, last = head_sums(part * mixed[:, cols].astype(F32))
            lane = iota(part.shape, 1)
            grad_denom = -jnp.where(lane < PAIR // 2, first, last) * inverse
            high = grad_denom.astype(BF).astype(F32)
            both = jnp.where(lane % (PAIR // 2) < PAIR // 4, high, grad_denom - high)
            put(2 * pair, (part * inverse).astype(BF))
            put(2 * pair + 1, (both * (4.0 / PAIR)).astype(BF))
        att[at] = grad_att
        return output

    def lanes_of(i):
        return slice(i * PAIR, (i + 1) * PAIR)

    def store_g(t):
        slot = lax.rem(t, 2)
        at = pl.ds(pl.multiple_of(TILE + t * tile, TILE), tile)
        return pltpu.make_async_copy(gr.at[slot], g_out.at[at], store_sem.at[slot])

    def store_att(at):
        pltpu.make_async_copy(att.at[at], ga_out.at[at], store_sem.at[2]).start()

    def rows_at(t):
        batch, step = lax.div(t, per), lax.rem(t, per)
        raw_at = pl.ds(pl.multiple_of(LONG + step * tile, LONG), tile)
        return batch, raw_at, pl.ds(pl.multiple_of(TILE + t * tile, TILE), tile)

    for ref in (dup, ddown, wo_grad, vec_grad, bias_grad):
        ref[...] = jnp.zeros_like(ref)
    wait_w.wait()
    for copy in first_waits:
        copy.wait()
    next_waits = load_inner(att_hbm, att, inner[1:]) + load_cot(pieces[2:])
    unpack(w_first)
    edge = pl.ds(0, TILE)
    swap_rows(cot, cuts)
    first_block(edge, edge_rows(cot))
    for copy in next_waits:
        copy.wait()
    last_waits = [loads.start(q_hbm.at[pl.ds(0, 2 * LONG)], qf)]
    for some in (inner[:1], inner[1:]):
        last_waits += load_inner(mix_hbm, mix, some) + load_inner(inv_hbm, inv, some)
    gather_at = place(gather_steps[1:], spots((1, 3, count), len(gather_steps) - 1), count + 1)

    def first_pass(t, _):
        talk(gather_at[:count], t)
        batch, raw_at, at = rows_at(t)
        first_block(at, cot[batch, raw_at])
        return 0

    lax.fori_loop(0, count, first_pass, 0)
    _all(gather_at[count])
    pack(w_first)
    scatter_steps[0]()
    unpack(w_second)
    dup[...] = jnp.zeros_like(dup)
    ddown[...] = jnp.zeros_like(ddown)
    for copy in last_waits:
        copy.wait()

    def put_edge(i, value):
        gr_edge[:, lanes_of(i)] = value

    store_edge(cot, second_block(edge, edge_rows(cot), put_edge))
    store_att(edge)
    edge_copy = pltpu.make_async_copy(gr_edge, g_out.at[edge], store_sem.at[3])
    edge_copy.start()
    for batch in range(2):
        own = slice(batch * LONG, (batch + 1) * LONG)
        for pair in range(pairs):
            grads = gr_edge[own, 2 * pair * PAIR : (2 * pair + 2) * PAIR]
            both = dot_tn(grads, qf[own, 2 * pair * FEAT : (2 * pair + 2) * FEAT])
            row = batch * pairs + pair
            store_blocks(parts, row * LONG, pack_pair(both[:PAIR]).astype(BF))
            norm_held[0, row : row + 1] = norm_rows(both)
    long_steps[0]()
    scatter_at = place(
        long_steps[1:] + scatter_steps[1:],
        spots((0, 3, 5, 7, 2 * count, 2 * count), len(long_steps) - 1)
        + spots((0, 6, 2 * count), len(scatter_steps) - 1),
        2 * count + 1,
    )

    out_store = RowStore(cot, out_hbm, store_sem.at[4], tile)
    finals = scatter_at[2 * count]
    split = sum(step in long_steps for step in finals)
    last_steps = side_by_side([finals[:split], finals[split:]])

    def second_pass(t, _):
        talk(scatter_at[: 2 * count : 2], t)
        batch, raw_at, at = rows_at(t)

        @pl.when(t >= 2)
        def _():
            store_g(t - 2).wait()

        def put(i, value):
            gr[lax.rem(t, 2), :, lanes_of(i)] = value

        cot[batch, raw_at] = second_block(
            at, cot[batch, raw_at], put, functools.partial(talk, scatter_at[1 : 2 * count : 2], t)
        )
        out_store.tile_done(batch, lax.rem(t, per))
        store_att(at)
        store_g(t).start()
        return 0

    lax.fori_loop(0, count, second_pass, 0)
    swap_rows(cot, cuts)
    out_store.finish()
    gather.drain()
    pack(w_second)
    x_copy = pltpu.make_async_copy(w_second, x_out, store_sem.at[5])
    x_copy.start()
    _all(last_steps)
    long_out[...] = long_total[...]
    norm_out[...] = norm_held[depth + 1]
    store_g(count - 2).wait()
    store_g(count - 1).wait()
    pltpu.make_async_copy(att, ga_out, store_sem.at[2]).wait()
    edge_copy.wait()
    out_store.wait()
    x_copy.wait()
    for item in (scatter, long_scatter, long_spread, norm_sum):
        item.drain()


def attention_backward(
    digits, lens, x_hbm, ga_hbm, g_hbm, k_hbm, q_hbm, v_hbm, ks_hbm, qs_hbm, n_hbm,
    sd_hbm, small, ffn_hbm, wo_grad, vec_in, bias_in, long_total, long_norm, gain, wqkv,
    projection,
    in_grad, ffn_out, out_out, query_out, key_out, value_out, vec_out,
    kf, v, ks, qs, n, sd, sg, back, ffn, out_x, out_total, query_x, query_total, key_x, key_total,
    value_x, value_total, load_sem, tile_sem, key_sem, store_sem, send, recv, *refs,
):
    rows = x_hbm.shape[1]
    big = rows - 2 * LONG
    pairs = back.shape[0]
    width = wqkv.shape[0]
    inner_rows = kf.shape[0]
    scale = (PAIR // 2) ** -0.25
    depth = len(digits)
    net = Net(digits, send, recv)
    each = 2 * depth
    refs = list(refs)

    def take(number):
        taken, refs[:] = refs[:number], refs[number:]
        return taken

    loads = Loads(load_sem)
    per = big // TILE
    count = 2 * per
    shorts = slice(2 * LONG, TILE)
    edge = slice(0, TILE)
    cuts, bounds = cuts_of(lens, big)
    same = same_small(bounds)

    def finish_ffn(value):
        ffn_out[...] = value

    ffn_sum = Scatter.of(net, "f", ffn, take(each), finish_ffn, apart=ffn_hbm)

    def reduction(name, blocks, total):
        def finish(value):
            total[(net.core,) + tuple(net.own)] = value.astype(BF)

        return Scatter.of(net, name, blocks, take(each), finish), Gather(net, name + "t", total)

    out_sum = reduction("o", out_x, out_total)
    query_sum = reduction("q", query_x, query_total)
    key_sum = reduction("k", key_x, key_total)
    value_sum = reduction("l", value_x, value_total)
    vec_held, vec_slots = take(2)
    vec_sum = Whole(net, "v", vec_held, vec_slots)
    ffn_steps = ffn_sum.steps()
    out_steps = all_reduce(*out_sum)
    query_steps = all_reduce(*query_sum)
    key_steps = all_reduce(*key_sum)
    value_steps = all_reduce(*value_sum)
    vec_steps = vec_sum.steps()
    last_spot = 4 * count
    number = len(out_steps)
    chains = (
        (out_steps[1:], spots((1, 5, 8, 16, 21, 26), number - 1)),
        (ffn_steps[1:], spots((2, 16, 26), len(ffn_steps) - 1)),
        (query_steps, spots((8, 11, 20, 24, 30, 32, 32), number)),
        (value_steps, spots((16, 18, 24, 30, 32, 32, 32), number)),
        (key_steps, spots((24, 26, 32, 32, 32, 32, 32), number)),
    )
    comm = [[] for _ in range(last_spot)]
    ends = []
    for steps, at in chains:
        ends.append([step for step, spot in zip(steps, at, strict=True) if spot == last_spot])
        for step, spot in zip(steps, at, strict=True):
            if spot < last_spot:
                comm[spot].append(step)
    last_steps = side_by_side([end for end in ends if end] + [vec_steps[1:]])

    def feat_lanes(pair):
        return slice(pair * 2 * FEAT, (pair + 1) * 2 * FEAT)

    def pair_cols(pair):
        return slice(pair * PAIR, (pair + 1) * PAIR)

    def grad_lanes(pair):
        return slice(2 * pair * PAIR, (2 * pair + 2) * PAIR)

    def feature_back(grad, mapped, scaled, pair):
        term = (grad * mapped.astype(F32)).astype(BF)
        both = dot(term, back[pair])
        return (
            (both[:, :PAIR] - scaled[:, pair_cols(pair)].astype(F32) * both[:, PAIR:]) * scale
        ).astype(BF)

    def ones_beside(values):
        return jnp.concatenate([values, jnp.ones_like(values)], axis=1)

    def first_tile(tiled):
        waits = []
        for source, target, by_rows in tiled:
            at = pl.ds(0, TILE) if by_rows else pl.ds(0, 1)
            waits.append(loads.start(source.at[at], target.at[at]))
        return waits

    def tile_load(i, source, target, by_rows, t):
        if by_rows:
            at = pl.ds(pl.multiple_of(TILE + t * TILE, TILE), TILE)
        else:
            at = pl.ds(1 + t, 1)
        return pltpu.make_async_copy(source.at[at], target.at[at], tile_sem.at[i, t])

    def query_phase(qf, gr, acc, wgrad):
        query_side = [(g_hbm, gr, True), (q_hbm, qf, True), (qs_hbm, qs, True), (n_hbm, n, False)]
        key_side = [(k_hbm, kf, True), (v_hbm, v, True), (ks_hbm, ks, True)]
        net.greet()
        wait_edge = first_tile(query_side + key_side)
        wait_edge.append(loads.start(sd_hbm.at[pl.ds(2, 2)], sd.at[pl.ds(2, 2)]))
        wait_ffn = loads.start(ffn_hbm.at[net.core], ffn)
        wait_sd = loads.start(sd_hbm.at[pl.ds(0, 2)], sd.at[pl.ds(0, 2)])

        def start_tile(t):
            for i, item in enumerate(query_side):
                tile_load(i, *item, t).start()

        for i in range(width // 16):
            at = slice(16 * i, 16 * i + 16)
            store_blocks(out_x, 16 * i, wo_grad[at].astype(BF))
        net.meet()
        out_steps[0]()
        ffn_steps[0]()
        for pair in range(pairs):
            turned = pair_projection(projection, pair).T
            own = (iota(turned.shape, 0) < FEAT) == (iota(turned.shape, 1) < PAIR // 2)
            back[pair] = jnp.concatenate([turned, jnp.where(own, 1.0, 0.0)], axis=1).astype(BF)
        for copy in wait_edge:
            copy.wait()
        for t in range(AHEAD):
            start_tile(t)
        for pair in range(pairs):
            lanes, cols = feat_lanes(pair), pair_cols(pair)
            mapped_q, mapped_k = qf[edge, lanes], kf[shorts, lanes]
            grads, values = gr[edge, grad_lanes(pair)], v[shorts, cols]
            grad_q = [
                dot(grads[batch * LONG : (batch + 1) * LONG], sd[2 + batch, pair])
                for batch in range(2)
            ]
            weight = dot_nt(grads[shorts], value_block(values, slice(0, PAIR)))
            more_q, more_k, more_v = [], [], []
            for head in range(2):
                own = slice(head * FEAT, (head + 1) * FEAT)
                part = jnp.where(same, weight[:, head * PAIR : (head + 1) * PAIR], 0.0).astype(BF)
                more_q.append(dot(part, mapped_k[:, own]))
                more_k.append(dot_tn(part, mapped_q[shorts, own]))
                more_v.append(dot_tn(small[2 * pair + head], grads[shorts, :PAIR]))
            grad_q.append(jnp.concatenate(more_q, axis=1))
            grad_k = jnp.concatenate(more_k, axis=1)
            grad_v = jnp.where(iota((2 * LONG, PAIR), 1) < PAIR // 2, more_v[0], more_v[1])
            qs[edge, cols] = feature_back(
                jnp.concatenate(grad_q, axis=0), mapped_q, qs[edge], pair
            )
            ks[shorts, cols] = feature_back(grad_k, mapped_k, ks[shorts], pair)
            v[shorts, cols] = grad_v.astype(BF)
        wgrad[...] = dot(n[0], qs[edge])
        wait_ffn.wait()
        wait_sd.wait()

        def key_load(i):
            source, target, _ = key_side[i]
            at = pl.ds(TILE, 2 * big)
            return pltpu.make_async_copy(source.at[at], target.at[at], key_sem.at[i])

        def queries(t, _):
            batch, step = lax.div(t, per), lax.rem(t, per)
            talk(comm[:count], t)
            at = pl.ds(pl.multiple_of(TILE + t * TILE, TILE), TILE)
            for i, item in enumerate(query_side):
                tile_load(i, *item, t).wait()

            @pl.when(t + AHEAD < count)
            def _():
                start_tile(t + AHEAD)

            @pl.when(t + AHEAD == count)
            def _():
                for i in range(len(key_side)):
                    key_load(i).start()

            @pl.when(step == 0)
            def _():
                acc[...] = jnp.zeros_like(acc)

            for pair in range(pairs):
                mapped = qf[at, feat_lanes(pair)]
                grads = gr[at, grad_lanes(pair)]
                acc[pair] += dot_tn(grads, mapped)
                grad = dot(grads, sd[batch, pair])
                qs[at, pair_cols(pair)] = feature_back(grad, mapped, qs[at], pair)
            wgrad[...] += dot(n[1 + t], qs[at])

            @pl.when(step == per - 1)
            def _():
                for pair in range(pairs):
                    both = acc[pair]
                    sg[batch, pair] = block_grads(both[:PAIR], norm_rows(both))

            return 0

        lax.fori_loop(0, count, queries, 0)
        for i in range(width // 16):
            at = slice(16 * i, 16 * i + 16)
            store_blocks(query_x, 16 * i, wgrad[at].astype(BF))
        for i in range(len(key_side)):
            key_load(i).wait()

    def key_phase(x, ga, wgrad, gv):
        wait_x = [loads.start(x_hbm, x), loads.start(ga_hbm, ga)]

        def tile_at(t):
            return pl.ds(pl.multiple_of(TILE + t * TILE, TILE), TILE)

        def pack(blocks):
            for i in range(width // 16):
                at = slice(16 * i, 16 * i + 16)
                store_blocks(blocks, 16 * i, wgrad[at].astype(BF))

        def keys(t, _):
            batch = lax.div(t, per)
            talk(comm[2 * count : 3 * count], t)
            at = tile_at(t)
            for pair in range(pairs):
                grad = dot(ones_beside(v[at, pair_cols(pair)]), sg[batch, pair])
                ks[at, pair_cols(pair)] = feature_back(grad, kf[at, feat_lanes(pair)], ks[at], pair)
            wgrad[...] += dot(n[1 + t], ks[at])
            return 0

        def values(t, _):
            batch = lax.div(t, per)
            talk(comm[count : 2 * count], t)
            at = tile_at(t)
            for pair in range(pairs):
                grad = dot_nt(kf[at, feat_lanes(pair)], sg[batch, pair, :PAIR])
                gv[at, pair_cols(pair)] = grad.astype(BF)
            wgrad[...] += dot(n[1 + t], gv[at])
            return 0

        for batch in range(2):
            own = slice(batch * LONG, (batch + 1) * LONG)
            for pair in range(pairs):
                lanes, cols = feat_lanes(pair), pair_cols(pair)
                row = batch * pairs + pair
                packed = load_blocks(long_total, row * LONG, LONG, 2 * FEAT).astype(F32)
                grads = block_grads(unpack_pair(packed), long_norm[row : row + 1])
                mapped = kf[own, lanes]
                grad = dot(ones_beside(v[own, cols]), grads)
                gv[own, cols] = dot_nt(mapped, grads[:PAIR]).astype(BF)
                ks[own, cols] = feature_back(grad, mapped, ks[own], pair)
        gv[shorts] = v[shorts]
        wgrad[...] = dot(n[0], gv[edge])
        lax.fori_loop(0, count, values, 0)
        pack(value_x)
        wgrad[...] = dot(n[0], ks[edge])
        lax.fori_loop(0, count, keys, 0)
        pack(key_x)
        for copy in wait_x:
            copy.wait()
        swap_rows(x, cuts)
        vec_held[0] = jnp.zeros(vec_held.shape[1:], F32)
        vec_held[0, 2:6] = vec_in[2:6]
        for i in range(bias_in.shape[1] // width):
            vec_held[0, 6 + i : 7 + i] = bias_in[:, i * width : (i + 1) * width]

        def last(rows_x, rows_ga, at):
            xhat, spread = normalize(rows_x)
            grad = (
                dot_nt(qs[at], wqkv[:, :width])
                + dot_nt(ks[at], wqkv[:, width : 2 * width])
                + dot_nt(gv[at], wqkv[:, 2 * width :])
            )
            vec_held[0, 0:1] += jnp.sum(grad * xhat, axis=0, keepdims=True)
            vec_held[0, 1:2] += jnp.sum(grad, axis=0, keepdims=True)
            return rows_ga + norm_back(grad * gain[...], xhat, spread)

        rows_out = RowStore(x, in_grad, store_sem.at[0], TILE)

        def inputs(t, _):
            batch, step = lax.div(t, per), lax.rem(t, per)
            talk(comm[3 * count : 4 * count], t)
            raw_at = pl.ds(pl.multiple_of(LONG + step * TILE, LONG), TILE)
            at = tile_at(t)
            x[batch, raw_at] = last(x[batch, raw_at], ga[at], at)
            rows_out.tile_done(batch, step)
            return 0

        lax.fori_loop(0, count, inputs, 0)
        store_edge(x, last(edge_rows(x), ga[edge], edge))
        vec_steps[0]()
        swap_rows(x, cuts)
        rows_out.finish()
        _all(last_steps)
        totals = [
            pltpu.make_async_copy(source, target, store_sem.at[1 + i])
            for i, (source, target) in enumerate(
                (
                    (out_total, out_out), (query_total, query_out),
                    (key_total, key_out), (value_total, value_out),
                )
            )
        ]
        for total in totals:
            total.start()
        vec_out[...] = vec_held[depth + 1]
        rows_out.wait()
        for total in totals:
            total.wait()

    wide = kf.shape[1]
    pl.run_scoped(
        query_phase,
        pltpu.VMEM((inner_rows, wide), BF),
        pltpu.VMEM((inner_rows, 2 * width), BF),
        pltpu.VMEM((pairs, 2 * PAIR, 2 * FEAT), F32),
        pltpu.VMEM((width, width), F32),
    )
    pl.run_scoped(
        key_phase,
        pltpu.VMEM(x_hbm.shape, F32),
        pltpu.VMEM((inner_rows, width), F32),
        pltpu.VMEM((width, width), F32),
        pltpu.VMEM((inner_rows, width), BF),
    )
    for item in (ffn_sum, *out_sum, *query_sum, *key_sum, *value_sum, vec_sum):
        item.drain()


def finish(
    out_raw, in_raw, vectors, ffn_first, ffn_second, *refs
):
    totals, refs = refs[:4], refs[4:]
    out, in_grad, grads, refs = refs[0], refs[1], refs[2:6], refs[6:]
    up_grad, down_grad, up_bias, lines, refs = refs[0], refs[1], refs[2], refs[3:9], refs[9:]
    held, wide, rows, load_sem, store_sem, row_sem = refs
    pieces = []
    size = out_raw.shape[1] // 3
    for i, (source, target) in enumerate(((out_raw, out), (in_raw, in_grad))):
        for batch in range(2):
            for part in range(3):
                at = (batch, pl.ds(part * size, size))
                slot = len(pieces)
                inner = rows.at[(i,) + at]
                pieces.append(
                    (
                        pltpu.make_async_copy(source.at[at], inner, row_sem.at[0, slot]),
                        pltpu.make_async_copy(inner, target.at[at], row_sem.at[1, slot]),
                    )
                )
    for load, _ in pieces:
        load.start()
    loads = []
    for i, total in enumerate(totals):
        loads.append(pltpu.make_async_copy(total, held.at[i], load_sem.at[i]))
        loads[i].start()
    copies = []
    for load, keep in pieces:
        load.wait()
        keep.start()
        copies.append(keep)
    deep, part = up_grad.shape[0], ffn_first.shape[1]
    for i, ffn in enumerate((ffn_first, ffn_second)):
        lanes = slice(i * part, (i + 1) * part)
        up_grad[:, lanes] = ffn[:deep]
        down_grad[:, lanes] = ffn[deep:]
    for i, row in enumerate(lines):
        row[...] = vectors[i : i + 1]
    width = vectors.shape[1]
    for i in range(up_bias.shape[1] // width):
        up_bias[:, i * width : (i + 1) * width] = vectors[6 + i : 7 + i]
    for i, copy in enumerate(loads):
        copy.wait()
        wide[i] = load_blocks(held.at[i], 0, width, width).astype(F32)
        copies.append(pltpu.make_async_copy(wide.at[i], grads[i], store_sem.at[i]))
        copies[-1].start()
    for copy in copies:
        copy.wait()


def body(
    inputs,
    lengths,
    first_gain,
    first_shift,
    query_weight,
    key_weight,
    value_weight,
    output_weight,
    output_bias,
    projection,
    second_gain,
    second_shift,
    up_weight,
    up_bias,
    down_weight,
    down_bias,
    cotangent,
):
    heads, head_size, feats = projection.shape
    batches, rows, width = inputs.shape
    digits = digits_of(lax.axis_size("seq"))
    ways = 2 * math.prod(digits)
    depth = len(digits)
    pairs = heads // 2
    big = rows - 2 * LONG
    inner = TILE + batches * big
    deep, half = up_weight.shape
    hidden = up_bias.shape[0]
    part = half // CHUNKS
    down_turned = down_weight.T

    lens = lengths.reshape(batches, lengths.shape[2])
    tiles = inner // TILE
    hbm = pl.BlockSpec(memory_space=pl.ANY)
    vmem = pl.BlockSpec(memory_space=pltpu.VMEM)
    smem = pl.BlockSpec(memory_space=pltpu.SMEM)

    def shape(*dims, dtype=BF):
        return jax.ShapeDtypeStruct(dims, dtype)

    def line(vector):
        return vector.reshape(1, -1)

    wide = 2 * FEAT * pairs
    long_block = block_shape(ways, batches * pairs * LONG, 2 * FEAT)
    inner_shapes = [
        ((inner, wide), BF), ((inner, wide), BF), ((inner, width), BF), ((inner, width), BF),
        ((inner, width), BF), ((tiles, width, TILE), BF), ((inner, width), BF),
        ((inner, width), F32), ((inner, width), F32), ((4, pairs, 2 * PAIR, 2 * FEAT), BF),
        ((heads, 2 * LONG, 2 * LONG), BF), ((width, 3 * width), BF), ((width, width), BF),
    ]
    kf, qf, v, ks, qs, n, mix, inv, att, sd, small, wqkv, wo, w = pl.pallas_call(
        functools.partial(attention_forward, digits),
        out_shape=[shape(*dims, dtype=kind) for dims, kind in inner_shapes]
        + [shape(2, *digits, 2 * deep, part)],
        in_specs=[smem, hbm] + [vmem] * 3 + [hbm] * 4 + [vmem] * 3,
        out_specs=[hbm] * 14,
        scratch_shapes=[pltpu.VMEM(inputs.shape, F32)]
        + [pltpu.VMEM(dims, kind) for dims, kind in inner_shapes]
        + [
            pltpu.VMEM((pairs, PAIR, 2 * FEAT), BF),
            pltpu.VMEM((2 * deep, part), BF),
            pltpu.VMEM((batches, pairs, PAIR, 2 * FEAT), F32),
            pltpu.VMEM((batches, pairs, 1, 2 * FEAT), F32),
            pltpu.VMEM((2,) + digits + long_block, BF),
            pltpu.VMEM((2,) + digits + long_block, BF),
            pltpu.SemaphoreType.DMA((16,)),
            pltpu.SemaphoreType.DMA((14,)),
            pltpu.SemaphoreType.DMA,
            pltpu.SemaphoreType.DMA((groups(depth, 2, 2),)),
            pltpu.SemaphoreType.DMA((groups(depth, 2, 2),)),
        ]
        + Whole.scratch(digits, batches * pairs, 2 * FEAT)
        + Scatter.scratch(digits, *long_block),
        compiler_params=pltpu.CompilerParams(
            collective_id=0, has_side_effects=True, vmem_limit_bytes=VMEM_LIMIT
        ),
        name="attention_forward",
    )(
        lens, inputs, line(first_gain), line(first_shift), line(output_bias),
        query_weight, key_weight, value_weight, output_weight, projection, up_weight, down_turned,
    )

    blocks = (2,) + digits + (2 * deep, part)
    output, ga, gr, ffn, ffn_grad, wo_grad, vec_in, bias_in, long_grad, long_norm = pl.pallas_call(
        functools.partial(feed_forward, digits),
        out_shape=[
            shape(*inputs.shape, dtype=F32),
            shape(inner, width, dtype=F32),
            shape(inner, 2 * width),
            shape(*blocks),
            shape(2 * deep, part, dtype=F32),
            shape(width, width, dtype=F32),
            shape(8, width, dtype=F32),
            shape(1, hidden, dtype=F32),
            shape(2, *digits, *long_block),
            shape(batches * pairs, 2 * FEAT, dtype=F32),
        ],
        in_specs=[smem] + [hbm] * 5 + [vmem] * 7 + [hbm],
        out_specs=[hbm] * 4 + [vmem] * 6,
        scratch_shapes=[
            pltpu.VMEM(inputs.shape, F32),
            pltpu.VMEM((inner, width), F32),
            pltpu.VMEM((inner, width), BF),
            pltpu.VMEM((inner, width), F32),
            pltpu.VMEM((inner, width), BF),
            pltpu.VMEM((inner, width), F32),
            pltpu.VMEM((inner, width), F32),
            pltpu.VMEM(blocks, BF),
            pltpu.VMEM(blocks, BF),
            pltpu.VMEM((width, hidden // CHUNKS), BF),
            pltpu.VMEM((width, hidden // CHUNKS), BF),
            pltpu.VMEM((width, hidden // CHUNKS), F32),
            pltpu.VMEM((width, hidden // CHUNKS), F32),
            pltpu.VMEM((TILE, 2 * width), BF),
            pltpu.VMEM((2, big // 2, 2 * width), BF),
            pltpu.VMEM((2 * LONG, wide), BF),
            pltpu.VMEM((2,) + digits + long_block, BF),
            pltpu.VMEM((2,) + digits + long_block, BF),
            pltpu.SemaphoreType.DMA((30,)),
            pltpu.SemaphoreType.DMA((6,)),
            pltpu.SemaphoreType.DMA((groups(depth, 2, 3),)),
            pltpu.SemaphoreType.DMA((groups(depth, 2, 3),)),
        ]
        + Scatter.scratch(digits, 2 * deep, part)
        + Scatter.scratch(digits, *long_block)
        + Whole.scratch(digits, batches * pairs, 2 * FEAT),
        compiler_params=pltpu.CompilerParams(
            collective_id=1, has_side_effects=True, vmem_limit_bytes=VMEM_LIMIT
        ),
        name="feed_forward",
    )(
        lens, cotangent, att, mix, inv, w, wo, line(second_gain), line(second_shift),
        line(down_bias), line(up_bias), up_weight, down_turned, qf,
    )

    late_block = block_shape(ways, width, width)
    late_shape = (2,) + digits + late_block
    in_grad, ffn_more, out_w, query, key, value, vectors = pl.pallas_call(
        functools.partial(attention_backward, digits),
        out_shape=[
            shape(*inputs.shape, dtype=F32),
            shape(2 * deep, part, dtype=F32),
            shape(*late_shape),
            shape(*late_shape),
            shape(*late_shape),
            shape(*late_shape),
            shape(16, width, dtype=F32),
        ],
        in_specs=[smem] + [hbm] * 10 + [vmem, hbm] + [vmem] * 8,
        out_specs=[hbm, vmem, hbm, hbm, hbm, hbm, vmem],
        scratch_shapes=[
            pltpu.VMEM((inner, wide), BF),
            pltpu.VMEM((inner, width), BF),
            pltpu.VMEM((inner, width), BF),
            pltpu.VMEM((inner, width), BF),
            pltpu.VMEM((tiles, width, TILE), BF),
            pltpu.VMEM((4, pairs, 2 * PAIR, 2 * FEAT), BF),
            pltpu.VMEM((batches, pairs, 2 * PAIR, 2 * FEAT), BF),
            pltpu.VMEM((pairs, 2 * FEAT, 2 * PAIR), BF),
            pltpu.VMEM(blocks[1:], BF),
        ]
        + [pltpu.VMEM(late_shape, BF)] * 8
        + [
            pltpu.SemaphoreType.DMA((12,)),
            pltpu.SemaphoreType.DMA((4, tiles - 1)),
            pltpu.SemaphoreType.DMA((3,)),
            pltpu.SemaphoreType.DMA((5,)),
            pltpu.SemaphoreType.DMA((groups(depth, 4, 6),)),
            pltpu.SemaphoreType.DMA((groups(depth, 4, 6),)),
        ]
        + Scatter.scratch(digits, 2 * deep, part)
        + Scatter.scratch(digits, *late_block) * 4
        + Whole.scratch(digits, 16, width),
        compiler_params=pltpu.CompilerParams(
            collective_id=2, has_side_effects=True, vmem_limit_bytes=VMEM_LIMIT
        ),
        name="attention_backward",
    )(
        lens, inputs, ga, gr, kf, qf, v, ks, qs, n, sd, small, ffn,
        wo_grad, vec_in, bias_in, long_grad, long_norm, line(first_gain), wqkv, projection,
    )

    full = shape(width, width, dtype=F32)
    output, in_grad, query, key, value, out_w, up_grad, down_grad, up_line, *lines = pl.pallas_call(
        finish,
        out_shape=[shape(*inputs.shape, dtype=F32)] * 2
        + [full] * 4
        + [shape(deep, half, dtype=F32)] * 2
        + [shape(1, hidden, dtype=F32)]
        + [shape(1, width, dtype=F32)] * 6,
        in_specs=[hbm] * 2 + [vmem] * 3 + [hbm] * 4,
        out_specs=[hbm] * 6 + [vmem] * 9,
        scratch_shapes=[
            pltpu.VMEM((4,) + late_shape, BF),
            pltpu.VMEM((4, width, width), F32),
            pltpu.VMEM((2,) + inputs.shape, F32),
            pltpu.SemaphoreType.DMA((4,)),
            pltpu.SemaphoreType.DMA((4,)),
            pltpu.SemaphoreType.DMA((2, 12)),
        ],
        compiler_params=pltpu.CompilerParams(vmem_limit_bytes=VMEM_LIMIT),
        name="finish",
    )(output, in_grad, vectors, ffn_grad, ffn_more, query, key, value, out_w)
    lines = [row.reshape(width) for row in lines]
    return (
        output, in_grad, lines[0], lines[1], query, key, value, out_w, lines[2], lines[3],
        lines[4], up_grad, up_line.reshape(hidden), down_grad.T, lines[5],
    )


def solution(mesh):
    rows = P(None, ("seq", "ffn"), None)
    up, down = P("seq", "ffn"), P("ffn", "seq")
    in_specs = (rows, rows) + (P(),) * 10 + (up, P(), down, P(), rows)
    out_specs = (rows, rows) + (P(),) * 9 + (up, P(), down, P())
    return jax.shard_map(body, mesh=mesh, in_specs=in_specs, out_specs=out_specs, check_vma=False)
```

```python
import functools
import math

import jax
import jax.numpy as jnp
from jax import lax
from jax.experimental import pallas as pl
from jax.experimental.pallas import tpu as pltpu
from jax.sharding import PartitionSpec as P

BF, F32 = jnp.bfloat16, jnp.float32
EPS = 1e-5
LONG = 64
TILE = 256
PAIR = 128
AHEAD = 3
CHUNKS = 2
FEAT = 256
VMEM_LIMIT = 63 << 20
LOG16 = math.log(16.0)


def dot(a, b):
    return jnp.dot(a, b, preferred_element_type=F32)


def dot_nt(a, b):
    return lax.dot_general(a, b, (((1,), (1,)), ((), ())), preferred_element_type=F32)


def dot_tn(a, b):
    return lax.dot_general(a, b, (((0,), (0,)), ((), ())), preferred_element_type=F32)


def iota(shape, dim):
    return lax.broadcasted_iota(jnp.int32, shape, dim)


def normalize(rows):
    mean = jnp.mean(rows, axis=-1, keepdims=True)
    centred = rows - mean
    spread = jnp.mean(centred * centred, axis=-1, keepdims=True)
    scale = lax.rsqrt(spread + EPS)
    return centred * scale, scale


def norm_back(grad, xhat, scale):
    return scale * (
        grad
        - jnp.mean(grad, axis=-1, keepdims=True)
        - xhat * jnp.mean(grad * xhat, axis=-1, keepdims=True)
    )


def head_sums(pair):
    first = iota(pair.shape, 1) < PAIR // 2
    zero = jnp.zeros_like(pair)
    return (
        jnp.sum(jnp.where(first, pair, zero), axis=-1, keepdims=True),
        jnp.sum(jnp.where(first, zero, pair), axis=-1, keepdims=True),
    )


def features(scaled, scaled_low, proj, pair):
    cols = slice(pair * PAIR, (pair + 1) * PAIR)
    part = scaled[:, cols]
    first, second = head_sums(part * part)
    product = dot(scaled_low[:, cols], proj[pair])
    return jnp.concatenate(
        [
            jnp.exp(product[:, :FEAT] - (0.5 * first + LOG16)).astype(BF),
            jnp.exp(product[:, FEAT:] - (0.5 * second + LOG16)).astype(BF),
        ],
        axis=1,
    )


def lane_half(shape):
    return iota(shape, 1) < FEAT


def block_sums(both, norm):
    keep = (iota((PAIR, 2 * FEAT), 0) < PAIR // 2) == lane_half((PAIR, 2 * FEAT))
    zero = jnp.zeros((PAIR, 2 * FEAT), F32)
    return jnp.concatenate(
        [
            jnp.where(keep, both, zero).astype(BF),
            jnp.where(keep, jnp.broadcast_to(norm, (PAIR, 2 * FEAT)), zero).astype(BF),
        ],
        axis=0,
    )


def block_grads(both, norm):
    keep = (iota((PAIR, 2 * FEAT), 0) < PAIR // 2) == lane_half((PAIR, 2 * FEAT))
    zero = jnp.zeros((PAIR, 2 * FEAT), F32)
    row = iota((PAIR, 2 * FEAT), 0)
    high = norm.astype(BF).astype(F32)
    wide = jnp.broadcast_to(high, (PAIR, 2 * FEAT))
    rest = jnp.broadcast_to(norm - high, (PAIR, 2 * FEAT))
    return jnp.concatenate(
        [
            jnp.where(keep, both, zero).astype(BF),
            jnp.where(row == 0, wide, jnp.where(row == 1, rest, zero)).astype(BF),
        ],
        axis=0,
    )


def pack_pair(both):
    return jnp.where(lane_half((PAIR // 2, 2 * FEAT)), both[: PAIR // 2], both[PAIR // 2 :])


def norm_rows(both):
    return jnp.where(
        lane_half((1, 2 * FEAT)),
        jnp.sum(both[PAIR : PAIR + PAIR // 2], axis=0, keepdims=True),
        jnp.sum(both[PAIR + PAIR // 2 :], axis=0, keepdims=True),
    )


def unpack_pair(packed):
    return jnp.concatenate([packed, packed], axis=0)


def value_block(values, cols):
    part = values[:, cols]
    first = iota(part.shape, 1) < PAIR // 2
    zero = jnp.zeros_like(part)
    one = jnp.ones_like(part)
    top = jnp.concatenate([jnp.where(first, part, zero), jnp.where(first, one, zero)], axis=1)
    low = jnp.concatenate([jnp.where(first, zero, part), jnp.where(first, zero, one)], axis=1)
    return jnp.concatenate([top, low], axis=0)


def same_small(bounds):
    shape = (2 * LONG, 2 * LONG)

    def label(dim):
        at = iota(shape, dim)
        cut = jnp.where(at < LONG, bounds[0], LONG + bounds[1])
        return jnp.where(at < cut, 1, 0) + jnp.where(at < LONG, 0, 2)

    return label(0) == label(1)


def cuts_of(lens, big):
    cuts, bounds = [], []
    for batch in range(2):
        first, second = lens[batch, 0], lens[batch, 1]
        behind = jnp.where(second == big, first, first + second)
        cuts.append(jnp.where(first == big, 0, behind))
        bounds.append(jnp.where(first == big, second, first))
    return cuts, bounds


def swap_rows(buffer, cuts):
    most = buffer.shape[1]
    width = buffer.shape[2]
    for batch in range(2):
        head = buffer[batch, LONG : 2 * LONG]
        tail = buffer[batch, most - LONG :]
        small_first = iota((LONG, width), 0) < cuts[batch]
        buffer[batch, LONG : 2 * LONG] = jnp.where(small_first, tail, head)
        buffer[batch, most - LONG :] = jnp.where(small_first, head, tail)


class RowStore:
    def __init__(self, buffer, out, semaphore, tile):
        self.buffer, self.out, self.semaphore, self.tile = buffer, out, semaphore, tile

    def start(self, batch, at):
        pltpu.make_async_copy(
            self.buffer.at[batch, at], self.out.at[batch, at], self.semaphore
        ).start()

    def tile_done(self, batch, step):
        first = LONG + step * self.tile
        self.start(batch, pl.ds(pl.multiple_of(first + LONG, LONG), self.tile - LONG))

        @pl.when(step > 0)
        def _():
            self.start(batch, pl.ds(pl.multiple_of(first, LONG), LONG))

    def finish(self):
        rows = self.buffer.shape[1]
        for batch in range(2):
            self.start(batch, pl.ds(0, 2 * LONG))
            self.start(batch, pl.ds(rows - LONG, LONG))

    def wait(self):
        pltpu.make_async_copy(self.buffer, self.out, self.semaphore).wait()


def edge_rows(buffer):
    most = buffer.shape[1]
    return jnp.concatenate(
        [
            buffer[0, :LONG],
            buffer[1, :LONG],
            buffer[0, most - LONG :],
            buffer[1, most - LONG :],
        ],
        axis=0,
    )


def store_edge(buffer, value):
    most = buffer.shape[1]
    buffer[0, :LONG] = value[:LONG]
    buffer[1, :LONG] = value[LONG : 2 * LONG]
    buffer[0, most - LONG :] = value[2 * LONG : 3 * LONG]
    buffer[1, most - LONG :] = value[3 * LONG :]


def digits_of(size):
    out = []
    while size > 1:
        step = 4 if size % 4 == 0 else size
        out.append(step)
        size //= step
    return tuple(out)


class Net:
    def __init__(self, digits, send, recv):
        self.digits = digits
        self.send, self.recv = send, recv
        self.me = lax.axis_index("seq")
        self.core = lax.axis_index("ffn")
        self.slots = {}
        strides = [math.prod(digits[k + 1 :]) for k in range(len(digits))]
        self.own = [lax.rem(lax.div(self.me, s), n) for s, n in zip(strides, digits)]
        self.strides = strides

    def partner(self):
        return (self.me, 1 - self.core)

    def other(self, k, step):
        return lax.rem(self.own[k] + step, self.digits[k])

    def peer(self, k, step):
        return (self.me + (self.other(k, step) - self.own[k]) * self.strides[k], self.core)

    def greet(self):
        semaphore = pltpu.get_barrier_semaphore()
        peers = [self.partner()] + [
            self.peer(k, step) for k, n in enumerate(self.digits) for step in range(1, n)
        ]
        for peer in peers:
            pl.semaphore_signal(
                semaphore, inc=1, device_id=peer, device_id_type=pl.DeviceIdType.MESH
            )

    def meet(self):
        pl.semaphore_wait(
            pltpu.get_barrier_semaphore(), 1 + sum(n - 1 for n in self.digits)
        )

    def copy(self, key, source, target, device):
        slot = self.slots.setdefault(key, len(self.slots))
        return pltpu.make_async_remote_copy(
            src_ref=source,
            dst_ref=target,
            send_sem=self.send.at[slot],
            recv_sem=self.recv.at[slot],
            device_id=device,
            device_id_type=pl.DeviceIdType.MESH,
        )

    def group(self, key, size):
        return self.copy(key, size, size, self.partner())


def groups(depth, gathers, others):
    return gathers * (depth + 1) * (depth + 2) // 2 + others * (depth + 1)


class Gather:
    def __init__(self, net, name, out):
        self.net, self.name, self.out = net, name, out

    def fresh(self, j):
        net = self.net
        if j == 0:
            return [(net.core,) + tuple(net.own)]
        lead = (net.core,) + (slice(None),) * (j - 1)
        return [
            lead + (net.other(j - 1, step),) + tuple(net.own[j:])
            for step in range(1, net.digits[j - 1])
        ]

    def copies(self, j, k):
        net = self.net
        depth = len(net.digits)
        copies = []
        for at in self.fresh(j):
            block = self.out.at[at]
            if k == depth:
                copies.append(net.copy((self.name, j, k), block, block, net.partner()))
                continue
            for step in range(1, net.digits[k]):
                copies.append(net.copy((self.name, j, k), block, block, net.peer(k, step)))
        return copies

    def group(self, j, k):
        digits = self.net.digits
        at = [0] * (1 + len(digits))
        if j:
            at[1:j] = [slice(None)] * (j - 1)
            at[j] = pl.ds(0, digits[j - 1] - 1)
        if k < len(digits):
            at[1 + k] = pl.ds(0, digits[k] - 1)
        return self.net.group((self.name, j, k), self.out.at[tuple(at)])

    def steps(self):
        depth = len(self.net.digits)

        def run(j):
            for i in range(j):
                self.group(i, j - 1).wait_recv()
            for k in range(j, depth + 1):
                for copy in self.copies(j, k):
                    copy.start()

        def last():
            for j in range(depth + 1):
                self.group(j, depth).wait_recv()

        return [functools.partial(run, j) for j in range(depth + 1)] + [last]

    def drain(self):
        depth = len(self.net.digits)
        for j in range(depth + 1):
            for k in range(j, depth + 1):
                self.group(j, k).wait_send()


class Scatter:
    def __init__(self, net, name, blocks, first, slots, parts, finish, apart=None):
        self.net, self.name = net, name
        self.away = (blocks if apart is None else apart).at[1 - net.core]
        self.held = blocks.at[net.core] if apart is None else blocks
        self.first, self.slots, self.parts, self.finish = first, slots, parts, finish

    @staticmethod
    def scratch(digits, rows, cols):
        shapes = [pltpu.VMEM(digits + (rows, cols), BF)]
        for k in reversed(range(len(digits))):
            shapes.append(pltpu.VMEM((digits[k] - 1,) + digits[:k] + (rows, cols), BF))
        for k in reversed(range(1, len(digits))):
            shapes.append(pltpu.VMEM(digits[:k] + (rows, cols), BF))
        return shapes

    @classmethod
    def of(cls, net, name, blocks, refs, finish, apart=None):
        depth = len(net.digits)
        slots, parts = refs[1 : 1 + depth], refs[1 + depth :]
        return cls(net, name, blocks, refs[0], slots, parts, finish, apart)

    def copies(self, k):
        net = self.net
        depth = len(net.digits)
        if k == 0:
            return [net.copy((self.name, 0), self.away, self.first, net.partner())]
        digit = depth - k
        held = self.held if k == 1 else self.parts[k - 2]
        copies = []
        for step in range(1, net.digits[digit]):
            at = (slice(None),) * digit + (net.other(digit, step),)
            copies.append(
                net.copy(
                    (self.name, k),
                    held.at[at],
                    self.slots[k - 1].at[step - 1],
                    net.peer(digit, step),
                )
            )
        return copies

    def group(self, k):
        return self.net.group((self.name, k), self.slots[k - 1] if k else self.first)

    def add(self, k):
        net = self.net
        depth = len(net.digits)
        if k == 0:
            lead = net.digits
            for at in _indices(lead):
                mine = self.held[at].astype(F32)
                self.held[at] = (mine + self.first[at].astype(F32)).astype(BF)
            return
        digit = depth - k
        held = self.held if k == 1 else self.parts[k - 2]
        for at in _indices(net.digits[:digit]):
            total = held[at + (net.own[digit],)].astype(F32)
            for step in range(net.digits[digit] - 1):
                total = total + self.slots[k - 1][(step,) + at].astype(F32)
            if digit:
                self.parts[k - 1][at] = total.astype(BF)
            else:
                self.finish(total)

    def steps(self):
        depth = len(self.net.digits)

        def start(k):
            for copy in self.copies(k):
                copy.start()

        def follow(k):
            self.group(k - 1).wait_recv()
            self.add(k - 1)
            if k <= depth:
                start(k)

        return [functools.partial(start, 0)] + [
            functools.partial(follow, k) for k in range(1, depth + 2)
        ]

    def drain(self):
        for k in range(len(self.net.digits) + 1):
            self.group(k).wait_send()


def _indices(lead):
    if not lead:
        return [()]
    return [(i,) + rest for i in range(lead[0]) for rest in _indices(lead[1:])]


class Whole:
    def __init__(self, net, name, held, slots):
        self.net, self.name, self.held, self.slots = net, name, held, slots

    @staticmethod
    def scratch(digits, rows, cols):
        return [
            pltpu.VMEM((len(digits) + 2, rows, cols), F32),
            pltpu.VMEM((1 + sum(n - 1 for n in digits), rows, cols), F32),
        ]

    def span(self, k):
        digits = self.net.digits
        return (0, 1) if k == 0 else (1 + sum(n - 1 for n in digits[: k - 1]), digits[k - 1] - 1)

    def copies(self, k):
        net = self.net
        source = self.held.at[k]
        first, number = self.span(k)
        peers = [net.partner()] if k == 0 else [net.peer(k - 1, 1 + i) for i in range(number)]
        return [
            net.copy((self.name, k), source, self.slots.at[first + i], peer)
            for i, peer in enumerate(peers)
        ]

    def group(self, k):
        return self.net.group((self.name, k), self.slots.at[pl.ds(*self.span(k))])

    def steps(self):
        depth = len(self.net.digits)

        def start(k):
            for copy in self.copies(k):
                copy.start()

        def follow(k):
            self.group(k - 1).wait_recv()
            total = self.held[k - 1]
            first, number = self.span(k - 1)
            for i in range(number):
                total = total + self.slots[first + i]
            self.held[k] = total
            if k <= depth:
                start(k)

        return [functools.partial(start, 0)] + [
            functools.partial(follow, k) for k in range(1, depth + 2)
        ]

    def drain(self):
        for k in range(len(self.net.digits) + 1):
            self.group(k).wait_send()


def together(*parts):
    most = max(len(part) for part in parts)

    def run(i):
        for part in parts:
            if i < len(part):
                part[i]()

    return [functools.partial(run, i) for i in range(most)]


def block_shape(ways, rows, cols):
    lanes = cols * (rows // 16) // ways
    return 16, lanes


def block_at(digits, index):
    at = []
    for n in reversed(digits):
        at.append(index % n)
        index //= n
    return tuple(reversed(at))


def store_blocks(blocks, row, value):
    lanes = blocks.shape[-1]
    per_row = value.shape[1] // lanes
    ways = (2,) + blocks.shape[1:-2]
    for i in range(value.shape[0] // 16):
        for j in range(per_row):
            at = block_at(ways, (row // 16 + i) * per_row + j)
            blocks[at] = value[16 * i : 16 * i + 16, j * lanes : (j + 1) * lanes]


def load_blocks(blocks, row, rows, cols):
    lanes = blocks.shape[-1]
    per_row = cols // lanes
    ways = (2,) + blocks.shape[1:-2]
    out = []
    for i in range(rows // 16):
        line = [
            blocks[block_at(ways, (row // 16 + i) * per_row + j)] for j in range(per_row)
        ]
        out.append(line[0] if per_row == 1 else jnp.concatenate(line, axis=1))
    return jnp.concatenate(out, axis=0)


class Loads:
    def __init__(self, semaphores):
        self.semaphores = semaphores
        self.count = 0

    def start(self, source, target):
        copy = pltpu.make_async_copy(source, target, self.semaphores.at[self.count])
        self.count += 1
        copy.start()
        return copy


PIECES = ((0, 128), (1088, 64), (128, 192), (320, 256), (576, 256), (832, 256))


def raw_pieces(rows):
    quarter = (rows - 2 * LONG) // 4
    pieces = [(0, 2 * LONG), (rows - LONG, LONG), (2 * LONG, quarter - LONG)]
    return pieces + [(LONG + quarter * i, quarter) for i in range(1, 4)]


def big_start(batch, rows_big, step, tile):
    return TILE + batch * rows_big + step * tile


def pair_projection(projection, pair):
    first, second = projection[2 * pair], projection[2 * pair + 1]
    gap = jnp.zeros_like(first)
    return jnp.concatenate(
        [jnp.concatenate([first, gap], axis=1), jnp.concatenate([gap, second], axis=1)], axis=0
    )


def place(steps, spots, count):
    lists = [[] for _ in range(count)]
    for step, spot in zip(steps, spots, strict=True):
        lists[spot].append(step)
    return lists


def spots(known, number):
    if number == len(known):
        return list(known)
    last = len(known) - 1
    return [known[min(last, -(-i * last // max(1, number - 1)))] for i in range(number)]


def side_by_side(chains):
    most = max(len(chain) for chain in chains)
    return [
        chain[i - most] for i in range(most) for chain in chains if i >= most - len(chain)
    ]


def talk(lists, t):
    for i, steps in enumerate(lists):
        if steps:
            pl.when(t == i)(functools.partial(_all, steps))


def _all(steps):
    for step in steps:
        step()


def all_reduce(scatter, spread):
    first, second = scatter.steps(), spread.steps()
    return first[:-1] + [functools.partial(_both, first[-1], second[0])] + second[1:]


def weight_block(up, down, chunk):
    half = up.shape[1] // CHUNKS
    at = slice(chunk * half, (chunk + 1) * half)
    return jnp.concatenate([up[:, at], down[:, at]], axis=0).astype(BF)


def attention_forward(
    digits, lens, x_hbm, gain, shift, bias, wq_hbm, wk_hbm, wv_hbm, wo_hbm, projection, up, down,
    k_out, q_out, v_out, ks_out, qs_out, n_out, mix_out, inv_out, att_out, sd_out, small_out,
    wqkv_out, wo_out, w_out,
    x, kf, qf, v, ks, qs, n, mix, inv, att, sd, small, wqkv, wo, proj, block, acc, nacc, parts,
    total, load_sem, store_sem, own_sem, send, recv, whole_held, whole_slots, *slots,
):
    rows = x.shape[1]
    big = rows - 2 * LONG
    pairs = proj.shape[0]
    width = wo.shape[0]
    scale = (PAIR // 2) ** -0.25
    depth = len(digits)
    net = Net(digits, send, recv)
    loads = Loads(load_sem)
    pieces = raw_pieces(rows)
    pending = {}

    def load_rows(some):
        for piece in some:
            for batch in range(2):
                span = pl.ds(*piece)
                pending[batch, piece] = loads.start(x_hbm.at[batch, span], x.at[batch, span])

    load_rows(pieces[:2])
    weights = [
        loads.start(source, att.at[pl.ds(i * width, width)])
        for i, source in enumerate((wq_hbm, wk_hbm, wv_hbm, wo_hbm))
    ]
    net.greet()
    block[...] = weight_block(up, down, 0)
    own_block = pltpu.make_async_copy(block, w_out.at[(net.core,) + tuple(net.own)], own_sem)
    own_block.start()
    for pair in range(pairs):
        proj[pair] = pair_projection(projection, pair).astype(BF)
    own_block.wait()
    net.meet()
    gather = Gather(net, "w", w_out)
    gather_steps = gather.steps()
    gather_steps[0]()

    def finish(value):
        total[(net.core,) + tuple(net.own)] = value.astype(BF)

    scatter = Scatter.of(net, "s", parts, slots, finish)
    spread = Gather(net, "t", total)
    whole = Whole(net, "n", whole_held, whole_slots)
    sum_steps = together(all_reduce(scatter, spread), whole.steps())
    cuts, bounds = cuts_of(lens, big)
    for i, copy in enumerate(weights):
        copy.wait()
        rounded = att[i * width : (i + 1) * width].astype(BF)
        if i < 3:
            wqkv[:, i * width : (i + 1) * width] = rounded
        else:
            wo[...] = rounded

    def front(rows_x, tile):
        xhat, _ = normalize(rows_x)
        low = (xhat * gain[...] + shift[...]).astype(BF)
        n[tile] = low.T
        raw = dot(low, wqkv[...])
        q = raw[:, :width] * scale
        k = raw[:, width : 2 * width] * scale
        return q, k, raw[:, 2 * width :].astype(BF)

    def attend(numer_denom, at, pair):
        cols = slice(pair * PAIR, (pair + 1) * PAIR)
        inverse = 1.0 / numer_denom[:, PAIR:]
        inv[at, cols] = inverse
        mix[at, cols] = (numer_denom[:, :PAIR] * inverse).astype(BF)

    load_rows(pieces[2:])
    for piece in pieces[:2]:
        for batch in range(2):
            pending[batch, piece].wait()
    swap_rows(x, cuts)
    edge = slice(0, TILE)
    q, k, values = front(edge_rows(x), 0)
    v[edge] = values
    k_low = k.astype(BF)
    ks[edge] = k_low
    for pair in range(pairs):
        cols = slice(pair * PAIR, (pair + 1) * PAIR)
        feats = slice(pair * 2 * FEAT, (pair + 1) * 2 * FEAT)
        mapped = features(k, k_low, proj, pair)
        kf[edge, feats] = mapped
        for batch in range(2):
            own = slice(batch * LONG, (batch + 1) * LONG)
            both = dot_tn(values[own, cols], mapped[own])
            row = batch * pairs + pair
            store_blocks(parts, row * LONG, pack_pair(both).astype(BF))
            whole_held[0, row : row + 1] = jnp.sum(mapped[own].astype(F32), axis=0, keepdims=True)
    sum_steps[0]()
    q_low = q.astype(BF)
    qs[edge] = q_low
    same = same_small(bounds)
    shorts = slice(2 * LONG, TILE)
    for pair in range(pairs):
        cols = slice(pair * PAIR, (pair + 1) * PAIR)
        feats = slice(pair * 2 * FEAT, (pair + 1) * 2 * FEAT)
        mapped = features(q, q_low, proj, pair)
        qf[edge, feats] = mapped
        scores = []
        for head in range(2):
            lanes = slice((2 * pair + head) * FEAT, (2 * pair + head + 1) * FEAT)
            score = dot_nt(
                mapped[shorts, head * FEAT : (head + 1) * FEAT], kf[shorts, lanes]
            )
            score = jnp.where(same, score, 0.0).astype(BF)
            small[2 * pair + head] = score
            scores.append(score)
        attend(
            dot(jnp.concatenate(scores, axis=1), value_block(values[shorts], cols)), shorts, pair
        )

    def store(source, target, at, slot):
        pltpu.make_async_copy(source.at[at], target.at[at], store_sem.at[slot]).start()

    first_pass = ((kf, k_out), (qf, q_out), (v, v_out), (ks, ks_out), (qs, qs_out), (n, n_out))
    second_pass = ((mix, mix_out), (inv, inv_out), (att, att_out))
    once = ((small, small_out), (wqkv, wqkv_out), (wo, wo_out))

    def store_first(at, tile):
        for slot, (source, target) in enumerate(first_pass):
            store(source, target, tile if source is n else at, slot)

    def store_second(at):
        for slot, (source, target) in enumerate(second_pass):
            store(source, target, at, len(first_pass) + slot)

    def whole_copy(i):
        slot = len(first_pass) + len(second_pass) + i
        return pltpu.make_async_copy(*once[i], store_sem.at[slot])

    store_first(pl.ds(0, TILE), 0)
    for i in range(3):
        whole_copy(i).start()
    for piece in pieces[2:]:
        for batch in range(2):
            pending[batch, piece].wait()
    acc[...] = jnp.zeros_like(acc)
    nacc[...] = jnp.zeros_like(nacc)
    per = big // TILE
    count = 2 * per
    comm = place(
        sum_steps[1:] + gather_steps[1:],
        spots((1, 3, 5, 7, count + 2, count + 6), len(sum_steps) - 1)
        + spots((3, count, count + 4), len(gather_steps) - 1),
        2 * count,
    )

    def pass_one(t, _):
        batch, step = lax.div(t, per), lax.rem(t, per)
        talk(comm[:count], t)
        raw_at = pl.ds(pl.multiple_of(LONG + step * TILE, LONG), TILE)
        at = pl.ds(pl.multiple_of(TILE + t * TILE, TILE), TILE)
        q, k, values = front(x[batch, raw_at], 1 + t)
        v[at] = values
        k_low = k.astype(BF)
        q_low = q.astype(BF)
        ks[at] = k_low
        qs[at] = q_low
        for pair in range(pairs):
            cols = slice(pair * PAIR, (pair + 1) * PAIR)
            feats = slice(pair * 2 * FEAT, (pair + 1) * 2 * FEAT)
            mapped = features(k, k_low, proj, pair)
            kf[at, feats] = mapped
            acc[batch, pair] += dot_tn(values[:, cols], mapped)
            nacc[batch, pair] += jnp.sum(mapped.astype(F32), axis=0, keepdims=True)
            qf[at, feats] = features(q, q_low, proj, pair)
        store_first(at, 1 + t)
        return 0

    lax.fori_loop(0, count, pass_one, 0)
    for batch in range(2):
        for pair in range(pairs):
            sd[batch, pair] = block_sums(acc[batch, pair], nacc[batch, pair])

    sd_copies = [
        pltpu.make_async_copy(sd.at[pl.ds(i, 2)], sd_out.at[pl.ds(i, 2)], store_sem.at[12 + i // 2])
        for i in (0, 2)
    ]
    sd_copies[0].start()

    def pass_two(t, _):
        batch, step = lax.div(t, per), lax.rem(t, per)
        talk(comm[count:], t)
        raw_at = pl.ds(pl.multiple_of(LONG + step * TILE, LONG), TILE)
        at = pl.ds(pl.multiple_of(TILE + t * TILE, TILE), TILE)
        for pair in range(pairs):
            feats = slice(pair * 2 * FEAT, (pair + 1) * 2 * FEAT)
            attend(dot_nt(qf[at, feats], sd[batch, pair]), at, pair)
        att[at] = x[batch, raw_at] + dot(mix[at], wo[...]) + bias[...]
        store_second(at)
        return 0

    lax.fori_loop(0, count, pass_two, 0)
    for batch in range(2):
        own = slice(batch * LONG, (batch + 1) * LONG)
        for pair in range(pairs):
            feats = slice(pair * 2 * FEAT, (pair + 1) * 2 * FEAT)
            row = batch * pairs + pair
            packed = load_blocks(total, row * LONG, LONG, 2 * FEAT).astype(F32)
            sd[2 + batch, pair] = block_sums(
                unpack_pair(packed), whole_held[depth + 1, row : row + 1]
            )
            attend(dot_nt(qf[own, feats], sd[2 + batch, pair]), own, pair)
    att[edge] = edge_rows(x) + dot(mix[edge], wo[...]) + bias[...]
    store_second(pl.ds(0, TILE))
    sd_copies[1].start()
    for slot, (source, target) in enumerate(first_pass + second_pass):
        pltpu.make_async_copy(source, target, store_sem.at[slot]).wait()
    for i in range(len(once)):
        whole_copy(i).wait()
    for copy in sd_copies:
        copy.wait()
    gather.drain()
    scatter.drain()
    spread.drain()
    whole.drain()


def _both(first, second):
    first()
    second()


def feed_forward(
    digits, lens, cot_hbm, att_hbm, mix_hbm, inv_hbm, w_hbm, wo, gain, shift, down_bias, up_bias,
    up_own, down_own, q_hbm,
    out_hbm, ga_out, g_out, x_out, ffn_out, wo_grad, vec_grad, bias_grad, long_out, norm_out,
    cot, att, mix, inv, second, branch, grad_second, w_first, w_second, up, down, dup, ddown,
    gr_edge, gr, qf, parts, long_total, load_sem, store_sem, send, recv, *refs,
):
    rows = cot.shape[1]
    big = rows - 2 * LONG
    width = wo.shape[0]
    pairs = width // PAIR
    tile = big // 2
    per = big // tile
    count = 2 * per
    depth = len(digits)
    cuts, _ = cuts_of(lens, big)
    net = Net(digits, send, recv)
    net.greet()
    loads = Loads(load_sem)
    deep = w_first.shape[-2] // 2
    half = w_first.shape[-1]
    wait_w = loads.start(w_hbm, w_first)
    pieces = raw_pieces(rows)
    inner = [(0, TILE)] + [(TILE + tile * i, tile) for i in range(count)]

    def load_cot(some):
        return [
            loads.start(cot_hbm.at[batch, pl.ds(*piece)], cot.at[batch, pl.ds(*piece)])
            for piece in some
            for batch in range(2)
        ]

    def load_inner(source, target, some):
        return [loads.start(source.at[pl.ds(*p)], target.at[pl.ds(*p)]) for p in some]

    first_waits = load_inner(att_hbm, att, inner[:1]) + load_cot(pieces[:2])
    w_second[(net.core,) + tuple(net.own)] = weight_block(up_own, down_own, 1)
    net.meet()
    gather = Gather(net, "w", w_second)
    gather_steps = gather.steps()
    gather_steps[0]()

    def finish(value):
        ffn_out[...] = value

    scatter = Scatter.of(net, "f", w_first, refs[: 2 * depth], finish)
    scatter_steps = scatter.steps()

    def finish_long(value):
        long_total[(net.core,) + tuple(net.own)] = value.astype(BF)

    long_scatter = Scatter.of(net, "s", parts, refs[2 * depth : 4 * depth], finish_long)
    long_spread = Gather(net, "t", long_total)
    norm_held, norm_slots = refs[4 * depth :]
    norm_sum = Whole(net, "n", norm_held, norm_slots)
    long_steps = together(all_reduce(long_scatter, long_spread), norm_sum.steps())
    members = _indices(digits)
    group = max(1, 16 // deep)

    def unpack(w):
        for core in range(2):
            cols = slice(core * half, (core + 1) * half)
            for first in range(0, len(members), group):
                parts = [w[(core,) + members[first + i]] for i in range(group)]
                at = slice(first * deep, (first + group) * deep)
                if group == 1:
                    up[at, cols] = parts[0][:deep]
                    down[at, cols] = parts[0][deep:]
                else:
                    up[at, cols] = jnp.concatenate([part[:deep] for part in parts], axis=0)
                    down[at, cols] = jnp.concatenate([part[deep:] for part in parts], axis=0)

    def pack(w):
        for core in range(2):
            cols = slice(core * half, (core + 1) * half)
            for i, member in enumerate(members):
                at = slice(i * deep, (i + 1) * deep)
                w[(core,) + member] = jnp.concatenate(
                    [dup[at, cols], ddown[at, cols]], axis=0
                ).astype(BF)

    def bias_lanes(chunk):
        return [
            slice((CHUNKS * core + chunk) * half, (CHUNKS * core + chunk + 1) * half)
            for core in range(2)
        ]

    def add_row(at, value):
        vec_grad[at : at + 1] += jnp.sum(value, axis=0, keepdims=True)

    def hidden_part(chunk, second_low, grad_low):
        bias = jnp.concatenate([up_bias[:, lanes] for lanes in bias_lanes(chunk)], axis=1)
        hidden = dot(second_low, up[...]) + bias
        gauss = jnp.exp(-0.5 * hidden * hidden) * (1.0 / math.sqrt(2.0 * math.pi))
        cdf = 0.5 + 0.5 * lax.erf(hidden * math.sqrt(0.5))
        active = (hidden * cdf).astype(BF)
        slope = cdf + hidden * gauss
        grad_hidden = (dot(grad_low, down[...]) * slope).astype(BF)
        dup[...] += dot(second_low.T, grad_hidden)
        ddown[...] += dot(grad_low.T, active)
        bias_sum = jnp.sum(grad_hidden.astype(F32), axis=0, keepdims=True)
        for core, lanes in enumerate(bias_lanes(chunk)):
            bias_grad[:, lanes] += bias_sum[:, core * half : (core + 1) * half]
        return dot_nt(active, down[...]), dot_nt(grad_hidden, up[...])

    def first_block(at, grad_out):
        xhat, _ = normalize(att[at])
        low = (xhat * gain[...] + shift[...]).astype(BF)
        second[at] = low
        branch[at], grad_second[at] = hidden_part(0, low, grad_out.astype(BF))

    def second_block(at, grad_out, put, between=lambda: None):
        more, grad_more = hidden_part(1, second[at], grad_out.astype(BF))
        between()
        att_rows = att[at]
        xhat, scale = normalize(att_rows)
        output = att_rows + (branch[at] + more) + down_bias[...]
        grad = grad_second[at] + grad_more
        grad_att = grad_out + norm_back(grad * gain[...], xhat, scale)
        add_row(2, grad_att)
        add_row(3, grad * xhat)
        add_row(4, grad)
        add_row(5, grad_out)
        grad_att_low = grad_att.astype(BF)
        mixed = mix[at]
        wo_grad[...] += dot_tn(mixed, grad_att_low)
        grad_mixed = dot_nt(grad_att_low, wo[...]).astype(BF).astype(F32)
        for pair in range(pairs):
            cols = slice(pair * PAIR, (pair + 1) * PAIR)
            part = grad_mixed[:, cols]
            inverse = inv[at, cols]
            first, last = head_sums(part * mixed[:, cols].astype(F32))
            lane = iota(part.shape, 1)
            grad_denom = -jnp.where(lane < PAIR // 2, first, last) * inverse
            high = grad_denom.astype(BF).astype(F32)
            both = jnp.where(lane % (PAIR // 2) < PAIR // 4, high, grad_denom - high)
            put(2 * pair, (part * inverse).astype(BF))
            put(2 * pair + 1, (both * (4.0 / PAIR)).astype(BF))
        att[at] = grad_att
        return output

    def lanes_of(i):
        return slice(i * PAIR, (i + 1) * PAIR)

    def store_g(t):
        slot = lax.rem(t, 2)
        at = pl.ds(pl.multiple_of(TILE + t * tile, TILE), tile)
        return pltpu.make_async_copy(gr.at[slot], g_out.at[at], store_sem.at[slot])

    def store_att(at):
        pltpu.make_async_copy(att.at[at], ga_out.at[at], store_sem.at[2]).start()

    def rows_at(t):
        batch, step = lax.div(t, per), lax.rem(t, per)
        raw_at = pl.ds(pl.multiple_of(LONG + step * tile, LONG), tile)
        return batch, raw_at, pl.ds(pl.multiple_of(TILE + t * tile, TILE), tile)

    for ref in (dup, ddown, wo_grad, vec_grad, bias_grad):
        ref[...] = jnp.zeros_like(ref)
    wait_w.wait()
    for copy in first_waits:
        copy.wait()
    next_waits = load_inner(att_hbm, att, inner[1:]) + load_cot(pieces[2:])
    unpack(w_first)
    edge = pl.ds(0, TILE)
    swap_rows(cot, cuts)
    first_block(edge, edge_rows(cot))
    for copy in next_waits:
        copy.wait()
    last_waits = [loads.start(q_hbm.at[pl.ds(0, 2 * LONG)], qf)]
    for some in (inner[:1], inner[1:]):
        last_waits += load_inner(mix_hbm, mix, some) + load_inner(inv_hbm, inv, some)
    gather_at = place(
        gather_steps[1:-1], spots((1, count), len(gather_steps) - 2), count + 1
    )

    def first_pass(t, _):
        talk(gather_at[:count], t)
        batch, raw_at, at = rows_at(t)
        first_block(at, cot[batch, raw_at])
        return 0

    lax.fori_loop(0, count, first_pass, 0)
    _all(gather_at[count])
    pack(w_first)
    scatter_steps[0]()
    gather_steps[-1]()
    unpack(w_second)
    dup[...] = jnp.zeros_like(dup)
    ddown[...] = jnp.zeros_like(ddown)
    for copy in last_waits:
        copy.wait()

    def put_edge(i, value):
        gr_edge[:, lanes_of(i)] = value

    store_edge(cot, second_block(edge, edge_rows(cot), put_edge))
    store_att(edge)
    edge_copy = pltpu.make_async_copy(gr_edge, g_out.at[edge], store_sem.at[3])
    edge_copy.start()
    for batch in range(2):
        own = slice(batch * LONG, (batch + 1) * LONG)
        for pair in range(pairs):
            grads = gr_edge[own, 2 * pair * PAIR : (2 * pair + 2) * PAIR]
            both = dot_tn(grads, qf[own, 2 * pair * FEAT : (2 * pair + 2) * FEAT])
            row = batch * pairs + pair
            store_blocks(parts, row * LONG, pack_pair(both[:PAIR]).astype(BF))
            norm_held[0, row : row + 1] = norm_rows(both)
    long_steps[0]()
    scatter_at = place(
        long_steps[1:] + scatter_steps[1:],
        spots((0, 3, 5, 7, 2 * count, 2 * count), len(long_steps) - 1)
        + spots((0, 6, 2 * count), len(scatter_steps) - 1),
        2 * count + 1,
    )

    out_store = RowStore(cot, out_hbm, store_sem.at[4], tile)
    finals = scatter_at[2 * count]
    split = sum(step in long_steps for step in finals)
    last_steps = side_by_side([finals[:split], finals[split:]])

    def second_pass(t, _):
        talk(scatter_at[: 2 * count : 2], t)
        batch, raw_at, at = rows_at(t)

        @pl.when(t >= 2)
        def _():
            store_g(t - 2).wait()

        def put(i, value):
            gr[lax.rem(t, 2), :, lanes_of(i)] = value

        cot[batch, raw_at] = second_block(
            at, cot[batch, raw_at], put, functools.partial(talk, scatter_at[1 : 2 * count : 2], t)
        )
        out_store.tile_done(batch, lax.rem(t, per))
        store_att(at)
        store_g(t).start()
        return 0

    lax.fori_loop(0, count, second_pass, 0)
    swap_rows(cot, cuts)
    out_store.finish()
    gather.drain()
    pack(w_second)
    x_copy = pltpu.make_async_copy(w_second, x_out, store_sem.at[5])
    x_copy.start()
    _all(last_steps)
    long_out[...] = long_total[...]
    norm_out[...] = norm_held[depth + 1]
    store_g(count - 2).wait()
    store_g(count - 1).wait()
    pltpu.make_async_copy(att, ga_out, store_sem.at[2]).wait()
    edge_copy.wait()
    out_store.wait()
    x_copy.wait()
    for item in (scatter, long_scatter, long_spread, norm_sum):
        item.drain()


def attention_backward(
    digits, lens, x_hbm, ga_hbm, g_hbm, k_hbm, q_hbm, v_hbm, ks_hbm, qs_hbm, n_hbm,
    sd_hbm, small, ffn_hbm, wo_grad, vec_in, bias_in, long_total, long_norm, gain, wqkv,
    projection,
    in_grad, ffn_out, out_out, query_out, key_out, value_out, vec_out,
    kf, v, ks, qs, n, sd, sg, back, ffn, out_x, out_total, query_x, query_total, key_x, key_total,
    value_x, value_total, load_sem, tile_sem, key_sem, store_sem, send, recv, *refs,
):
    rows = x_hbm.shape[1]
    big = rows - 2 * LONG
    pairs = back.shape[0]
    width = wqkv.shape[0]
    inner_rows = kf.shape[0]
    scale = (PAIR // 2) ** -0.25
    depth = len(digits)
    net = Net(digits, send, recv)
    each = 2 * depth
    refs = list(refs)

    def take(number):
        taken, refs[:] = refs[:number], refs[number:]
        return taken

    loads = Loads(load_sem)
    per = big // TILE
    count = 2 * per
    shorts = slice(2 * LONG, TILE)
    edge = slice(0, TILE)
    cuts, bounds = cuts_of(lens, big)
    same = same_small(bounds)

    def finish_ffn(value):
        ffn_out[...] = value

    ffn_sum = Scatter.of(net, "f", ffn, take(each), finish_ffn, apart=ffn_hbm)

    def reduction(name, blocks, total):
        def finish(value):
            total[(net.core,) + tuple(net.own)] = value.astype(BF)

        return Scatter.of(net, name, blocks, take(each), finish), Gather(net, name + "t", total)

    out_sum = reduction("o", out_x, out_total)
    query_sum = reduction("q", query_x, query_total)
    key_sum = reduction("k", key_x, key_total)
    value_sum = reduction("l", value_x, value_total)
    vec_held, vec_slots = take(2)
    vec_sum = Whole(net, "v", vec_held, vec_slots)
    ffn_steps = ffn_sum.steps()
    out_steps = all_reduce(*out_sum)
    query_steps = all_reduce(*query_sum)
    key_steps = all_reduce(*key_sum)
    value_steps = all_reduce(*value_sum)
    vec_steps = vec_sum.steps()
    last_spot = 4 * count
    number = len(out_steps)
    chains = (
        (out_steps[1:], spots((1, 5, 8, 16, 21, 26), number - 1)),
        (ffn_steps[1:], spots((2, 16, 26), len(ffn_steps) - 1)),
        (query_steps, spots((8, 11, 20, 24, 30, 32, 32), number)),
        (value_steps, spots((16, 18, 24, 30, 32, 32, 32), number)),
        (key_steps, spots((24, 26, 32, 32, 32, 32, 32), number)),
    )
    comm = [[] for _ in range(last_spot)]
    ends = []
    for steps, at in chains:
        ends.append([step for step, spot in zip(steps, at, strict=True) if spot == last_spot])
        for step, spot in zip(steps, at, strict=True):
            if spot < last_spot:
                comm[spot].append(step)
    last_steps = side_by_side([end for end in ends if end] + [vec_steps[1:]])

    def feat_lanes(pair):
        return slice(pair * 2 * FEAT, (pair + 1) * 2 * FEAT)

    def pair_cols(pair):
        return slice(pair * PAIR, (pair + 1) * PAIR)

    def grad_lanes(pair):
        return slice(2 * pair * PAIR, (2 * pair + 2) * PAIR)

    def feature_back(grad, mapped, scaled, pair):
        term = (grad * mapped.astype(F32)).astype(BF)
        both = dot(term, back[pair])
        return (
            (both[:, :PAIR] - scaled[:, pair_cols(pair)].astype(F32) * both[:, PAIR:]) * scale
        ).astype(BF)

    def ones_beside(values):
        return jnp.concatenate([values, jnp.ones_like(values)], axis=1)

    def first_tile(tiled):
        waits = []
        for source, target, by_rows in tiled:
            at = pl.ds(0, TILE) if by_rows else pl.ds(0, 1)
            waits.append(loads.start(source.at[at], target.at[at]))
        return waits

    def tile_load(i, source, target, by_rows, t):
        if by_rows:
            at = pl.ds(pl.multiple_of(TILE + t * TILE, TILE), TILE)
        else:
            at = pl.ds(1 + t, 1)
        return pltpu.make_async_copy(source.at[at], target.at[at], tile_sem.at[i, t])

    def query_phase(qf, gr, acc, wgrad):
        query_side = [(g_hbm, gr, True), (q_hbm, qf, True), (qs_hbm, qs, True), (n_hbm, n, False)]
        key_side = [(k_hbm, kf, True), (v_hbm, v, True), (ks_hbm, ks, True)]
        net.greet()
        wait_edge = first_tile(query_side + key_side)
        wait_edge.append(loads.start(sd_hbm.at[pl.ds(2, 2)], sd.at[pl.ds(2, 2)]))
        wait_ffn = loads.start(ffn_hbm.at[net.core], ffn)
        wait_sd = loads.start(sd_hbm.at[pl.ds(0, 2)], sd.at[pl.ds(0, 2)])

        def start_tile(t):
            for i, item in enumerate(query_side):
                tile_load(i, *item, t).start()

        for i in range(width // 16):
            at = slice(16 * i, 16 * i + 16)
            store_blocks(out_x, 16 * i, wo_grad[at].astype(BF))
        net.meet()
        out_steps[0]()
        ffn_steps[0]()
        for pair in range(pairs):
            turned = pair_projection(projection, pair).T
            own = (iota(turned.shape, 0) < FEAT) == (iota(turned.shape, 1) < PAIR // 2)
            back[pair] = jnp.concatenate([turned, jnp.where(own, 1.0, 0.0)], axis=1).astype(BF)
        for copy in wait_edge:
            copy.wait()
        for t in range(AHEAD):
            start_tile(t)
        for pair in range(pairs):
            lanes, cols = feat_lanes(pair), pair_cols(pair)
            mapped_q, mapped_k = qf[edge, lanes], kf[shorts, lanes]
            grads, values = gr[edge, grad_lanes(pair)], v[shorts, cols]
            grad_q = [
                dot(grads[batch * LONG : (batch + 1) * LONG], sd[2 + batch, pair])
                for batch in range(2)
            ]
            weight = dot_nt(grads[shorts], value_block(values, slice(0, PAIR)))
            more_q, more_k, more_v = [], [], []
            for head in range(2):
                own = slice(head * FEAT, (head + 1) * FEAT)
                part = jnp.where(same, weight[:, head * PAIR : (head + 1) * PAIR], 0.0).astype(BF)
                more_q.append(dot(part, mapped_k[:, own]))
                more_k.append(dot_tn(part, mapped_q[shorts, own]))
                more_v.append(dot_tn(small[2 * pair + head], grads[shorts, :PAIR]))
            grad_q.append(jnp.concatenate(more_q, axis=1))
            grad_k = jnp.concatenate(more_k, axis=1)
            grad_v = jnp.where(iota((2 * LONG, PAIR), 1) < PAIR // 2, more_v[0], more_v[1])
            qs[edge, cols] = feature_back(
                jnp.concatenate(grad_q, axis=0), mapped_q, qs[edge], pair
            )
            ks[shorts, cols] = feature_back(grad_k, mapped_k, ks[shorts], pair)
            v[shorts, cols] = grad_v.astype(BF)
        wgrad[...] = dot(n[0], qs[edge])
        wait_ffn.wait()
        wait_sd.wait()

        def key_load(i):
            source, target, _ = key_side[i]
            at = pl.ds(TILE, 2 * big)
            return pltpu.make_async_copy(source.at[at], target.at[at], key_sem.at[i])

        def queries(t, _):
            batch, step = lax.div(t, per), lax.rem(t, per)
            talk(comm[:count], t)
            at = pl.ds(pl.multiple_of(TILE + t * TILE, TILE), TILE)
            for i, item in enumerate(query_side):
                tile_load(i, *item, t).wait()

            @pl.when(t + AHEAD < count)
            def _():
                start_tile(t + AHEAD)

            @pl.when(t + AHEAD == count)
            def _():
                for i in range(len(key_side)):
                    key_load(i).start()

            @pl.when(step == 0)
            def _():
                acc[...] = jnp.zeros_like(acc)

            for pair in range(pairs):
                mapped = qf[at, feat_lanes(pair)]
                grads = gr[at, grad_lanes(pair)]
                acc[pair] += dot_tn(grads, mapped)
                grad = dot(grads, sd[batch, pair])
                qs[at, pair_cols(pair)] = feature_back(grad, mapped, qs[at], pair)
            wgrad[...] += dot(n[1 + t], qs[at])

            @pl.when(step == per - 1)
            def _():
                for pair in range(pairs):
                    both = acc[pair]
                    sg[batch, pair] = block_grads(both[:PAIR], norm_rows(both))

            return 0

        lax.fori_loop(0, count, queries, 0)
        for i in range(width // 16):
            at = slice(16 * i, 16 * i + 16)
            store_blocks(query_x, 16 * i, wgrad[at].astype(BF))
        for i in range(len(key_side)):
            key_load(i).wait()

    def key_phase(x, ga, wgrad, gv):
        wait_x = [loads.start(x_hbm, x), loads.start(ga_hbm, ga)]

        def tile_at(t):
            return pl.ds(pl.multiple_of(TILE + t * TILE, TILE), TILE)

        def pack(blocks):
            for i in range(width // 16):
                at = slice(16 * i, 16 * i + 16)
                store_blocks(blocks, 16 * i, wgrad[at].astype(BF))

        def keys(t, _):
            batch = lax.div(t, per)
            talk(comm[2 * count : 3 * count], t)
            at = tile_at(t)
            for pair in range(pairs):
                grad = dot(ones_beside(v[at, pair_cols(pair)]), sg[batch, pair])
                ks[at, pair_cols(pair)] = feature_back(grad, kf[at, feat_lanes(pair)], ks[at], pair)
            wgrad[...] += dot(n[1 + t], ks[at])
            return 0

        def values(t, _):
            batch = lax.div(t, per)
            talk(comm[count : 2 * count], t)
            at = tile_at(t)
            for pair in range(pairs):
                grad = dot_nt(kf[at, feat_lanes(pair)], sg[batch, pair, :PAIR])
                gv[at, pair_cols(pair)] = grad.astype(BF)
            wgrad[...] += dot(n[1 + t], gv[at])
            return 0

        for batch in range(2):
            own = slice(batch * LONG, (batch + 1) * LONG)
            for pair in range(pairs):
                lanes, cols = feat_lanes(pair), pair_cols(pair)
                row = batch * pairs + pair
                packed = load_blocks(long_total, row * LONG, LONG, 2 * FEAT).astype(F32)
                grads = block_grads(unpack_pair(packed), long_norm[row : row + 1])
                mapped = kf[own, lanes]
                grad = dot(ones_beside(v[own, cols]), grads)
                gv[own, cols] = dot_nt(mapped, grads[:PAIR]).astype(BF)
                ks[own, cols] = feature_back(grad, mapped, ks[own], pair)
        gv[shorts] = v[shorts]
        wgrad[...] = dot(n[0], gv[edge])
        lax.fori_loop(0, count, values, 0)
        pack(value_x)
        wgrad[...] = dot(n[0], ks[edge])
        lax.fori_loop(0, count, keys, 0)
        pack(key_x)
        for copy in wait_x:
            copy.wait()
        swap_rows(x, cuts)
        vec_held[0] = jnp.zeros(vec_held.shape[1:], F32)
        vec_held[0, 2:6] = vec_in[2:6]
        for i in range(bias_in.shape[1] // width):
            vec_held[0, 6 + i : 7 + i] = bias_in[:, i * width : (i + 1) * width]

        def last(rows_x, rows_ga, at):
            xhat, spread = normalize(rows_x)
            grad = (
                dot_nt(qs[at], wqkv[:, :width])
                + dot_nt(ks[at], wqkv[:, width : 2 * width])
                + dot_nt(gv[at], wqkv[:, 2 * width :])
            )
            vec_held[0, 0:1] += jnp.sum(grad * xhat, axis=0, keepdims=True)
            vec_held[0, 1:2] += jnp.sum(grad, axis=0, keepdims=True)
            return rows_ga + norm_back(grad * gain[...], xhat, spread)

        rows_out = RowStore(x, in_grad, store_sem.at[0], TILE)

        def inputs(t, _):
            batch, step = lax.div(t, per), lax.rem(t, per)
            talk(comm[3 * count : 4 * count], t)
            raw_at = pl.ds(pl.multiple_of(LONG + step * TILE, LONG), TILE)
            at = tile_at(t)
            x[batch, raw_at] = last(x[batch, raw_at], ga[at], at)
            rows_out.tile_done(batch, step)
            return 0

        lax.fori_loop(0, count, inputs, 0)
        store_edge(x, last(edge_rows(x), ga[edge], edge))
        vec_steps[0]()
        swap_rows(x, cuts)
        rows_out.finish()
        _all(last_steps)
        totals = [
            pltpu.make_async_copy(source, target, store_sem.at[1 + i])
            for i, (source, target) in enumerate(
                (
                    (out_total, out_out), (query_total, query_out),
                    (key_total, key_out), (value_total, value_out),
                )
            )
        ]
        for total in totals:
            total.start()
        vec_out[...] = vec_held[depth + 1]
        rows_out.wait()
        for total in totals:
            total.wait()

    wide = kf.shape[1]
    pl.run_scoped(
        query_phase,
        pltpu.VMEM((inner_rows, wide), BF),
        pltpu.VMEM((inner_rows, 2 * width), BF),
        pltpu.VMEM((pairs, 2 * PAIR, 2 * FEAT), F32),
        pltpu.VMEM((width, width), F32),
    )
    pl.run_scoped(
        key_phase,
        pltpu.VMEM(x_hbm.shape, F32),
        pltpu.VMEM((inner_rows, width), F32),
        pltpu.VMEM((width, width), F32),
        pltpu.VMEM((inner_rows, width), BF),
    )
    for item in (ffn_sum, *out_sum, *query_sum, *key_sum, *value_sum, vec_sum):
        item.drain()


def finish(
    out_raw, in_raw, vectors, ffn_first, ffn_second, *refs
):
    totals, refs = refs[:4], refs[4:]
    out, in_grad, grads, refs = refs[0], refs[1], refs[2:6], refs[6:]
    up_grad, down_grad, up_bias, lines, refs = refs[0], refs[1], refs[2], refs[3:9], refs[9:]
    held, wide, rows, load_sem, store_sem, row_sem = refs
    pieces = []
    size = out_raw.shape[1] // 6
    for i, (source, target) in enumerate(((out_raw, out), (in_raw, in_grad))):
        for batch in range(2):
            for part in range(6):
                at = (batch, pl.ds(part * size, size))
                slot = len(pieces)
                inner = rows.at[(i,) + at]
                pieces.append(
                    (
                        pltpu.make_async_copy(source.at[at], inner, row_sem.at[0, slot]),
                        pltpu.make_async_copy(inner, target.at[at], row_sem.at[1, slot]),
                    )
                )
    loads = []
    for i, total in enumerate(totals):
        loads.append(pltpu.make_async_copy(total, held.at[i], load_sem.at[i]))
        loads[i].start()
    for load, _ in pieces:
        load.start()
    copies = []
    deep, part = up_grad.shape[0], ffn_first.shape[1]
    for i, ffn in enumerate((ffn_first, ffn_second)):
        lanes = slice(i * part, (i + 1) * part)
        up_grad[:, lanes] = ffn[:deep]
        down_grad[:, lanes] = ffn[deep:]
    for i, row in enumerate(lines):
        row[...] = vectors[i : i + 1]
    width = vectors.shape[1]
    for i in range(up_bias.shape[1] // width):
        up_bias[:, i * width : (i + 1) * width] = vectors[6 + i : 7 + i]
    for i, copy in enumerate(loads):
        copy.wait()
        wide[i] = load_blocks(held.at[i], 0, width, width).astype(F32)
        copies.append(pltpu.make_async_copy(wide.at[i], grads[i], store_sem.at[i]))
        copies[-1].start()
    for load, keep in pieces:
        load.wait()
        keep.start()
        copies.append(keep)
    for copy in copies:
        copy.wait()


def body(
    inputs,
    lengths,
    first_gain,
    first_shift,
    query_weight,
    key_weight,
    value_weight,
    output_weight,
    output_bias,
    projection,
    second_gain,
    second_shift,
    up_weight,
    up_bias,
    down_weight,
    down_bias,
    cotangent,
):
    heads, head_size, feats = projection.shape
    batches, rows, width = inputs.shape
    digits = digits_of(lax.axis_size("seq"))
    ways = 2 * math.prod(digits)
    depth = len(digits)
    pairs = heads // 2
    big = rows - 2 * LONG
    inner = TILE + batches * big
    deep, half = up_weight.shape
    hidden = up_bias.shape[0]
    part = half // CHUNKS
    down_turned = down_weight.T

    lens = lengths.reshape(batches, lengths.shape[2])
    tiles = inner // TILE
    hbm = pl.BlockSpec(memory_space=pl.ANY)
    vmem = pl.BlockSpec(memory_space=pltpu.VMEM)
    smem = pl.BlockSpec(memory_space=pltpu.SMEM)

    def shape(*dims, dtype=BF):
        return jax.ShapeDtypeStruct(dims, dtype)

    def line(vector):
        return vector.reshape(1, -1)

    wide = 2 * FEAT * pairs
    long_block = block_shape(ways, batches * pairs * LONG, 2 * FEAT)
    inner_shapes = [
        ((inner, wide), BF), ((inner, wide), BF), ((inner, width), BF), ((inner, width), BF),
        ((inner, width), BF), ((tiles, width, TILE), BF), ((inner, width), BF),
        ((inner, width), F32), ((inner, width), F32), ((4, pairs, 2 * PAIR, 2 * FEAT), BF),
        ((heads, 2 * LONG, 2 * LONG), BF), ((width, 3 * width), BF), ((width, width), BF),
    ]
    kf, qf, v, ks, qs, n, mix, inv, att, sd, small, wqkv, wo, w = pl.pallas_call(
        functools.partial(attention_forward, digits),
        out_shape=[shape(*dims, dtype=kind) for dims, kind in inner_shapes]
        + [shape(2, *digits, 2 * deep, part)],
        in_specs=[smem, hbm] + [vmem] * 3 + [hbm] * 4 + [vmem] * 3,
        out_specs=[hbm] * 14,
        scratch_shapes=[pltpu.VMEM(inputs.shape, F32)]
        + [pltpu.VMEM(dims, kind) for dims, kind in inner_shapes]
        + [
            pltpu.VMEM((pairs, PAIR, 2 * FEAT), BF),
            pltpu.VMEM((2 * deep, part), BF),
            pltpu.VMEM((batches, pairs, PAIR, 2 * FEAT), F32),
            pltpu.VMEM((batches, pairs, 1, 2 * FEAT), F32),
            pltpu.VMEM((2,) + digits + long_block, BF),
            pltpu.VMEM((2,) + digits + long_block, BF),
            pltpu.SemaphoreType.DMA((16,)),
            pltpu.SemaphoreType.DMA((14,)),
            pltpu.SemaphoreType.DMA,
            pltpu.SemaphoreType.DMA((groups(depth, 2, 2),)),
            pltpu.SemaphoreType.DMA((groups(depth, 2, 2),)),
        ]
        + Whole.scratch(digits, batches * pairs, 2 * FEAT)
        + Scatter.scratch(digits, *long_block),
        compiler_params=pltpu.CompilerParams(
            collective_id=0, has_side_effects=True, vmem_limit_bytes=VMEM_LIMIT
        ),
        name="attention_forward",
    )(
        lens, inputs, line(first_gain), line(first_shift), line(output_bias),
        query_weight, key_weight, value_weight, output_weight, projection, up_weight, down_turned,
    )

    blocks = (2,) + digits + (2 * deep, part)
    output, ga, gr, ffn, ffn_grad, wo_grad, vec_in, bias_in, long_grad, long_norm = pl.pallas_call(
        functools.partial(feed_forward, digits),
        out_shape=[
            shape(*inputs.shape, dtype=F32),
            shape(inner, width, dtype=F32),
            shape(inner, 2 * width),
            shape(*blocks),
            shape(2 * deep, part, dtype=F32),
            shape(width, width, dtype=F32),
            shape(8, width, dtype=F32),
            shape(1, hidden, dtype=F32),
            shape(2, *digits, *long_block),
            shape(batches * pairs, 2 * FEAT, dtype=F32),
        ],
        in_specs=[smem] + [hbm] * 5 + [vmem] * 7 + [hbm],
        out_specs=[hbm] * 4 + [vmem] * 6,
        scratch_shapes=[
            pltpu.VMEM(inputs.shape, F32),
            pltpu.VMEM((inner, width), F32),
            pltpu.VMEM((inner, width), BF),
            pltpu.VMEM((inner, width), F32),
            pltpu.VMEM((inner, width), BF),
            pltpu.VMEM((inner, width), F32),
            pltpu.VMEM((inner, width), F32),
            pltpu.VMEM(blocks, BF),
            pltpu.VMEM(blocks, BF),
            pltpu.VMEM((width, hidden // CHUNKS), BF),
            pltpu.VMEM((width, hidden // CHUNKS), BF),
            pltpu.VMEM((width, hidden // CHUNKS), F32),
            pltpu.VMEM((width, hidden // CHUNKS), F32),
            pltpu.VMEM((TILE, 2 * width), BF),
            pltpu.VMEM((2, big // 2, 2 * width), BF),
            pltpu.VMEM((2 * LONG, wide), BF),
            pltpu.VMEM((2,) + digits + long_block, BF),
            pltpu.VMEM((2,) + digits + long_block, BF),
            pltpu.SemaphoreType.DMA((30,)),
            pltpu.SemaphoreType.DMA((6,)),
            pltpu.SemaphoreType.DMA((groups(depth, 2, 3),)),
            pltpu.SemaphoreType.DMA((groups(depth, 2, 3),)),
        ]
        + Scatter.scratch(digits, 2 * deep, part)
        + Scatter.scratch(digits, *long_block)
        + Whole.scratch(digits, batches * pairs, 2 * FEAT),
        compiler_params=pltpu.CompilerParams(
            collective_id=1, has_side_effects=True, vmem_limit_bytes=VMEM_LIMIT
        ),
        name="feed_forward",
    )(
        lens, cotangent, att, mix, inv, w, wo, line(second_gain), line(second_shift),
        line(down_bias), line(up_bias), up_weight, down_turned, qf,
    )

    late_block = block_shape(ways, width, width)
    late_shape = (2,) + digits + late_block
    in_grad, ffn_more, out_w, query, key, value, vectors = pl.pallas_call(
        functools.partial(attention_backward, digits),
        out_shape=[
            shape(*inputs.shape, dtype=F32),
            shape(2 * deep, part, dtype=F32),
            shape(*late_shape),
            shape(*late_shape),
            shape(*late_shape),
            shape(*late_shape),
            shape(16, width, dtype=F32),
        ],
        in_specs=[smem] + [hbm] * 10 + [vmem, hbm] + [vmem] * 8,
        out_specs=[hbm, vmem, hbm, hbm, hbm, hbm, vmem],
        scratch_shapes=[
            pltpu.VMEM((inner, wide), BF),
            pltpu.VMEM((inner, width), BF),
            pltpu.VMEM((inner, width), BF),
            pltpu.VMEM((inner, width), BF),
            pltpu.VMEM((tiles, width, TILE), BF),
            pltpu.VMEM((4, pairs, 2 * PAIR, 2 * FEAT), BF),
            pltpu.VMEM((batches, pairs, 2 * PAIR, 2 * FEAT), BF),
            pltpu.VMEM((pairs, 2 * FEAT, 2 * PAIR), BF),
            pltpu.VMEM(blocks[1:], BF),
        ]
        + [pltpu.VMEM(late_shape, BF)] * 8
        + [
            pltpu.SemaphoreType.DMA((12,)),
            pltpu.SemaphoreType.DMA((4, tiles - 1)),
            pltpu.SemaphoreType.DMA((3,)),
            pltpu.SemaphoreType.DMA((5,)),
            pltpu.SemaphoreType.DMA((groups(depth, 4, 6),)),
            pltpu.SemaphoreType.DMA((groups(depth, 4, 6),)),
        ]
        + Scatter.scratch(digits, 2 * deep, part)
        + Scatter.scratch(digits, *late_block) * 4
        + Whole.scratch(digits, 16, width),
        compiler_params=pltpu.CompilerParams(
            collective_id=2, has_side_effects=True, vmem_limit_bytes=VMEM_LIMIT
        ),
        name="attention_backward",
    )(
        lens, inputs, ga, gr, kf, qf, v, ks, qs, n, sd, small, ffn,
        wo_grad, vec_in, bias_in, long_grad, long_norm, line(first_gain), wqkv, projection,
    )

    full = shape(width, width, dtype=F32)
    output, in_grad, query, key, value, out_w, up_grad, down_grad, up_line, *lines = pl.pallas_call(
        finish,
        out_shape=[shape(*inputs.shape, dtype=F32)] * 2
        + [full] * 4
        + [shape(deep, half, dtype=F32)] * 2
        + [shape(1, hidden, dtype=F32)]
        + [shape(1, width, dtype=F32)] * 6,
        in_specs=[hbm] * 2 + [vmem] * 3 + [hbm] * 4,
        out_specs=[hbm] * 6 + [vmem] * 9,
        scratch_shapes=[
            pltpu.VMEM((4,) + late_shape, BF),
            pltpu.VMEM((4, width, width), F32),
            pltpu.VMEM((2,) + inputs.shape, F32),
            pltpu.SemaphoreType.DMA((4,)),
            pltpu.SemaphoreType.DMA((4,)),
            pltpu.SemaphoreType.DMA((2, 24)),
        ],
        compiler_params=pltpu.CompilerParams(vmem_limit_bytes=VMEM_LIMIT),
        name="finish",
    )(output, in_grad, vectors, ffn_grad, ffn_more, query, key, value, out_w)
    lines = [row.reshape(width) for row in lines]
    return (
        output, in_grad, lines[0], lines[1], query, key, value, out_w, lines[2], lines[3],
        lines[4], up_grad, up_line.reshape(hidden), down_grad.T, lines[5],
    )


def solution(mesh):
    rows = P(None, ("seq", "ffn"), None)
    up, down = P("seq", "ffn"), P("ffn", "seq")
    in_specs = (rows, rows) + (P(),) * 10 + (up, P(), down, P(), rows)
    out_specs = (rows, rows) + (P(),) * 9 + (up, P(), down, P())
    return jax.shard_map(body, mesh=mesh, in_specs=in_specs, out_specs=out_specs, check_vma=False)
```
